32 devices in a mesh: gx: 4 (over y, x), gy: 8 (over z, core).
Axes of the slice: x: 2, y: 2, z: 4, core: 2. Of those that a mesh axis runs over, the one named last changes fastest.
Arguments:
- xi_coarse: float32 [512, 1024], P('gx', 'gy'), may hold values from -6 to 6
- xi_middle: float32 [1024, 2048], P('gx', 'gy'), may hold values from -6 to 6
- xi_fine: float32 [2048, 4096], P('gx', 'gy'), may hold values from -6 to 6
- coef_middle: bfloat16 [4, 9, 512, 1024], P(None, None, 'gx', 'gy'), may hold values from -1.1953125 to 1.1953125
- coef_fine: bfloat16 [4, 9, 1024, 2048], P(None, None, 'gx', 'gy'), may hold values from -1.1953125 to 1.1953125
- kern_u: bfloat16 [4, 16, 1024, 512], P('gx', 'gy'), may hold values from -0.25 to 0.25
- kern_v: bfloat16 [4, 16, 1024, 512], P('gx', 'gy'), may hold values from -0.25 to 0.25
- vis_data: bfloat16 [4, 16, 1024, 1024], P('gx', 'gy'), may hold values from -6 to 6
- facet_tiles: int32 [4, 16, 2], P('gx', 'gy'), may hold values from 0 to 7, as said below
- facet_weight: float32 [4, 16, 2], P('gx', 'gy'), may hold values from 0.5 to 1.5
- facet_count: int32 [4, 16], P('gx', 'gy'), may hold values from 256 to 1024, as said below
Outputs:
- grad_coarse: float32 [512, 1024], P('gx', 'gy')
- grad_middle: float32 [1024, 2048], P('gx', 'gy')
- grad_fine: float32 [2048, 4096], P('gx', 'gy')
- potential: float32 [], replicated
The draws below stay inside these ranges and needn't reach their ends.
Inputs may be any that keep to these rules, and one draw needn't show every extreme that they name: `facet_tiles`: every tile column of a row is named by some facet of that row. `facet_count`: bins 0 to the count minus one of a facet are used.
All inputs are finite; a program needn't handle non-finite values.
Results may differ from the reference program's by a relative error of at most 0.0085.
Values may be sent and summed in bfloat16 or wider, within the bound.
No kernel may reach another device: no remote copies, remote signals or barrier semaphores. Data moves between devices by JAX's collectives and lax.ppermute only.
A program may use at most 320 MiB of HBM per device.

```python
import jax
import jax.numpy as jnp
from jax import lax

TS = 512
BINS = 1024
FAC_DEV = 2
LIST = 2
TROW = 8
FROWS = 4
FCOLS = 16
NC0R = 512
NC0C = 1024
NC1R = 1024
NC1C = 2048
NC2R = 2048
NC2C = 4096


def draw_facet_tiles(key, part):
    keys = jax.random.split(key, FROWS + 1)
    leading = jax.vmap(lambda one_key: jax.random.permutation(one_key, TROW))(keys[:FROWS]).astype(jnp.int32)
    others = jax.random.randint(keys[FROWS], (FROWS, FCOLS, LIST), 0, TROW).astype(jnp.int32)
    spread = jnp.repeat(leading, FAC_DEV, axis=1)
    first_kind = (jnp.arange(FCOLS, dtype=jnp.int32) % FAC_DEV == 0)[None, :]
    first_slot = jnp.where(first_kind, spread, others[:, :, 0])
    return others.at[:, :, 0].set(first_slot)


def draw_facet_count(key, part):
    counts = jax.random.randint(key, (FROWS, FCOLS), BINS // 4, BINS + 1).astype(jnp.int32)
    counts = counts.at[0, 0].set(BINS)
    return counts.at[0, 1].set(BINS // 4)


def block_scale(rng, extent, shards, smallest, high):
    level = 1.0
    for dim, blocks in shards:
        steps = jax.random.uniform(jax.random.fold_in(jax.random.fold_in(rng, 6), dim), (blocks,), jnp.float32, smallest / len(shards), high / len(shards))
        level = level * jnp.repeat(jnp.exp(steps), extent[dim] // blocks).reshape((-1,) + (1,) * (len(extent) - 1 - dim))
    return level


def bell_draw(own_key, extent, scale, limit, cuts=(), held_as=jnp.bfloat16):
    level = block_scale(own_key, extent, cuts, -0.22, 0.18) if cuts else 1.0
    drawn = jax.random.normal(own_key, extent, jnp.float32) * scale * level
    return jnp.minimum(jnp.maximum(drawn, -limit), limit).astype(held_as)


def setup_inputs(seed: int = 0) -> dict:
    key_list = jax.random.split(jax.random.key(seed), 12)
    xi_coarse = bell_draw(key_list[0], (NC0R, NC0C), 1.0, 6.0, ((0, 4), (1, 8)), jnp.float32)
    xi_middle = bell_draw(key_list[1], (NC1R, NC1C), 1.0, 6.0, ((0, 4), (1, 8)), jnp.float32)
    xi_fine = bell_draw(key_list[2], (NC2R, NC2C), 1.0, 6.0, ((0, 4), (1, 8)), jnp.float32)
    coef_middle = bell_draw(key_list[3], (4, 9, NC0R, NC0C), 0.2, 1.1953125, ((2, 4), (3, 8)))
    coef_fine = bell_draw(key_list[4], (4, 9, NC1R, NC1C), 0.2, 1.1953125, ((2, 4), (3, 8)))
    kern_u = bell_draw(key_list[5], (FROWS, FCOLS, BINS, TS), TS ** -0.5, 0.25, ((0, 4), (1, 8)))
    kern_v = bell_draw(key_list[6], (FROWS, FCOLS, BINS, TS), TS ** -0.5, 0.25, ((0, 4), (1, 8)))
    vis_data = bell_draw(key_list[7], (FROWS, FCOLS, BINS, BINS), 1.0, 6.0, ((0, 4), (1, 8)))
    facet_tiles = draw_facet_tiles(jax.random.fold_in(key_list[11], 71), 0)
    facet_weight = jnp.clip(0.5 + 1.0 * jax.random.uniform(key_list[9], (FROWS, FCOLS, LIST), jnp.float32) ** block_scale(key_list[9], (FROWS, FCOLS, LIST), ((0, 4), (1, 8)), -0.2, 0.2), 0.5, 1.5)
    facet_count = draw_facet_count(jax.random.fold_in(key_list[11], 71), 0)
    return dict(xi_coarse=xi_coarse, xi_middle=xi_middle, xi_fine=xi_fine, coef_middle=coef_middle, coef_fine=coef_fine, kern_u=kern_u, kern_v=kern_v, vis_data=vis_data, facet_tiles=facet_tiles, facet_weight=facet_weight, facet_count=facet_count)


inv_noise = 0.125


def alternate(quads, rows, cols):
    return quads.reshape(2, 2, rows, cols).transpose(2, 0, 3, 1).reshape(2 * rows, 2 * cols)


def refine(padded, weights):
    rows, cols = weights.shape[2], weights.shape[3]
    quads = []
    for child in range(4):
        total = jnp.zeros((rows, cols), jnp.float32)
        for near in range(9):
            shift_r, shift_c = near // 3 - 1, near % 3 - 1
            window = padded[1 + shift_r:1 + shift_r + rows, 1 + shift_c:1 + shift_c + cols]
            total = total + weights[child, near].astype(jnp.float32) * window
        quads.append(total)
    return alternate(jnp.stack(quads), rows, cols)


def parent_terms(grad, weights):
    rows, cols = weights.shape[2], weights.shape[3]
    quads = grad.reshape(rows, 2, cols, 2).transpose(1, 3, 0, 2).reshape(4, rows, cols)
    parts = []
    for near in range(9):
        total = jnp.zeros((rows, cols), jnp.float32)
        for child in range(4):
            total = total + weights[child, near].astype(jnp.float32) * quads[child]
        parts.append(total)
    return jnp.stack(parts)


def collect_back(padded, rows, cols):
    total = jnp.zeros((rows, cols), jnp.float32)
    for near in range(9):
        shift_r, shift_c = near // 3 - 1, near % 3 - 1
        total = total + padded[near, 1 - shift_r:1 - shift_r + rows, 1 - shift_c:1 - shift_c + cols]
    return total


def back(grad, weights):
    rows, cols = weights.shape[2], weights.shape[3]
    stack = parent_terms(grad, weights)
    return collect_back(jnp.pad(stack, ((0, 0), (1, 1), (1, 1))), rows, cols)


def one_facet(items):
    fsum, ku, kv, data, count = items
    amp = jnp.dot(ku, fsum.astype(jnp.bfloat16), preferred_element_type=jnp.float32).astype(jnp.bfloat16)
    vis = jnp.dot(amp, kv.T, preferred_element_type=jnp.float32)
    live = (jnp.arange(BINS, dtype=jnp.int32) < count).astype(jnp.float32)
    resid = live[:, None] * (vis - data.astype(jnp.float32))
    lik = 0.5 * inv_noise * jnp.sum(resid * resid)
    dvis = (inv_noise * resid).astype(jnp.bfloat16)
    damp = jnp.dot(dvis, kv, preferred_element_type=jnp.float32).astype(jnp.bfloat16)
    dsum = jnp.dot(ku.T, damp, preferred_element_type=jnp.float32)
    return lik, dsum


def reference(xi_coarse, xi_middle, xi_fine, coef_middle, coef_fine, kern_u, kern_v, vis_data, facet_tiles, facet_weight, facet_count):
    level_middle = refine(jnp.pad(xi_coarse, 1), coef_middle) + xi_middle
    level_fine = refine(jnp.pad(level_middle, 1), coef_fine) + xi_fine
    sky = level_fine.astype(jnp.bfloat16)
    tiles = sky.reshape(FROWS, TS, TROW, TS).transpose(0, 2, 1, 3).astype(jnp.float32)
    onehot = (facet_tiles[:, :, :, None] == jnp.arange(TROW, dtype=jnp.int32)).astype(jnp.float32)
    mixing = jnp.sum(facet_weight[:, :, :, None] * onehot, axis=2)
    sums = jnp.einsum("rqt,rtxy->rqxy", mixing, tiles, precision=lax.Precision.HIGHEST)
    liks, dsums = lax.map(one_facet, (sums.reshape(-1, TS, TS), kern_u.reshape(-1, BINS, TS), kern_v.reshape(-1, BINS, TS), vis_data.reshape(-1, BINS, BINS), facet_count.reshape(-1)))
    dsums = dsums.reshape(FROWS, FCOLS, TS, TS)
    dtiles = jnp.einsum("rqt,rqxy->rtxy", mixing, dsums, precision=lax.Precision.HIGHEST)
    dsky = dtiles.transpose(0, 2, 1, 3).reshape(FROWS * TS, TROW * TS)
    grad_fine = dsky + xi_fine
    dmiddle = back(dsky, coef_fine)
    grad_middle = dmiddle + xi_middle
    grad_coarse = back(dmiddle, coef_middle) + xi_coarse
    prior = 0.5 * (jnp.sum(xi_coarse * xi_coarse) + jnp.sum(xi_middle * xi_middle) + jnp.sum(xi_fine * xi_fine))
    potential = (prior + jnp.sum(liks)) / (FROWS * TS * TROW * TS)
    return grad_coarse, grad_middle, grad_fine, potential
```

```python
import functools

import jax
import jax.numpy as jnp
from jax import lax
from jax.experimental import pallas as pl
from jax.experimental.pallas import tpu as pltpu
from jax.sharding import PartitionSpec as P

inv_noise = 0.125
vmem = 56 * 1024 * 1024
f32 = jnp.float32
bf16 = jnp.bfloat16


def extended(x, sides, width):
    for axis, dim in sides:
        size, length = (lax.axis_size(axis), x.shape[dim])
        up = [(i, (i + 1) % size) for i in range(size - 1)]
        down = [(j, i) for i, j in up]
        last = lax.slice_in_dim(x, length - width, length, axis=dim)
        leading = lax.slice_in_dim(x, 0, width, axis=dim)
        before = lax.ppermute(last, axis, up)
        after = lax.ppermute(leading, axis, down)
        x = jnp.concatenate([before, x, after], axis=dim)
    return x


def widen(field):
    return extended(field, (("gx", 0), ("gy", 1)), 1)


def halves(x):
    high = x.astype(bf16)
    return high, (x - high.astype(f32)).astype(bf16)


def interleaver(cols, transposed):
    shape = (2 * cols, 2 * cols)
    split = lax.broadcasted_iota(jnp.int32, shape, 1 if transposed else 0)
    whole = lax.broadcasted_iota(jnp.int32, shape, 0 if transposed else 1)
    place = jnp.where(split >= cols, 2 * (split - cols) + 1, 2 * split)
    return (place == whole).astype(f32).astype(bf16)


def refine_kernel(blk, pad_ref, coef_ref, xi_ref, out_ref, sq_ref, win, perm, lhs, mix):
    rows, cols = win.shape[1:]
    step = pl.program_id(0)

    @pl.when(step == 0)
    def _():
        for near in range(9):
            r, c = near // 3, near % 3
            win[near] = pad_ref[r : r + rows, c : c + cols]
        perm[...] = interleaver(cols, False)
        sq_ref[...] = jnp.zeros_like(sq_ref)

    base = step * blk

    def part(i, carry):
        r0 = pl.multiple_of(i * 16, 16)
        total = [jnp.zeros((16, cols), f32) for _ in range(4)]
        for near in range(9):
            w = win[near, pl.ds(pl.multiple_of(base + r0, 16), 16), :]
            for child in range(4):
                total[child] += coef_ref[child, near, pl.ds(r0, 16), :].astype(f32) * w
        for child in range(4):
            a, b = child // 2, child % 2
            high, low = halves(total[child])
            lhs[pl.ds(2 * a * blk + r0, 16), b * cols : (b + 1) * cols] = high
            lhs[pl.ds((2 * a + 1) * blk + r0, 16), b * cols : (b + 1) * cols] = low
        return carry

    lax.fori_loop(0, blk // 16, part, 0)
    field = jnp.dot(lhs[...], perm[...], preferred_element_type=f32)
    xi = xi_ref[...]
    for tile in range(2 * cols // 128):
        lanes = slice(tile * 128, (tile + 1) * 128)
        for a in range(2):
            mix[tile, pl.ds(a, blk, stride=2), :] = (
                field[2 * a * blk : (2 * a + 1) * blk, lanes]
                + field[(2 * a + 1) * blk : (2 * a + 2) * blk, lanes]
            )
        out_ref[:, lanes] = (mix[tile] + xi[:, lanes]).astype(out_ref.dtype)
    sq_ref[...] += jnp.sum((xi * xi).reshape(2 * blk // 8, 8, 2 * cols), axis=0)


def refine(padded, coef, xi, dtype):
    rows, cols = coef.shape[2:]
    blk = 64
    return pl.pallas_call(
        functools.partial(refine_kernel, blk),
        grid=(rows // blk,),
        in_specs=[
            pl.BlockSpec((rows + 2, cols + 2), lambda i: (0, 0)),
            pl.BlockSpec((4, 9, blk, cols), lambda i: (0, 0, i, 0)),
            pl.BlockSpec((2 * blk, 2 * cols), lambda i: (i, 0)),
        ],
        out_specs=[
            pl.BlockSpec((2 * blk, 2 * cols), lambda i: (i, 0)),
            pl.BlockSpec((8, 2 * cols), lambda i: (0, 0)),
        ],
        out_shape=[
            jax.ShapeDtypeStruct((2 * rows, 2 * cols), dtype),
            jax.ShapeDtypeStruct((8, 2 * cols), f32),
        ],
        scratch_shapes=[
            pltpu.VMEM((9, rows, cols), f32),
            pltpu.VMEM((2 * cols, 2 * cols), bf16),
            pltpu.VMEM((4 * blk, 2 * cols), bf16),
            pltpu.VMEM((2 * cols // 128, 2 * blk, 128), f32),
        ],
        compiler_params=pltpu.CompilerParams(vmem_limit_bytes=vmem),
        name="refine",
    )(padded, coef, xi)


def back_kernel(blk, g_ref, coef_ref, xi_ref, grad_ref, main_ref, cols_ref, terms, perm, mix, rowed):
    rows, cols = terms.shape[1:]
    step = pl.program_id(0)

    @pl.when(step == 0)
    def _():
        perm[...] = interleaver(cols, True)

    base = step * blk
    g = g_ref[...]
    grad_ref[...] = g.astype(f32) + xi_ref[...]
    if g.dtype == bf16:
        split = jnp.dot(g, perm[...], preferred_element_type=f32)
    else:
        high, low = halves(g)
        both = jnp.dot(jnp.concatenate([high, low]), perm[...], preferred_element_type=f32)
        split = both[: 2 * blk] + both[2 * blk :]
    for tile in range(2 * cols // 128):
        mix[tile] = split[:, tile * 128 : (tile + 1) * 128]

    def part(i, carry):
        r0 = pl.multiple_of(i * 16, 16)
        quads = []
        for a in range(2):
            for b in range(2):
                tiles = range(b * cols // 128, (b + 1) * cols // 128)
                lines = [mix[t, pl.ds(2 * r0 + a, 16, stride=2), :] for t in tiles]
                quads.append(jnp.concatenate(lines, axis=1))
        for near in range(9):
            total = jnp.zeros((16, cols), f32)
            for child in range(4):
                total += coef_ref[child, near, pl.ds(r0, 16), :].astype(f32) * quads[child]
            terms[near, pl.ds(pl.multiple_of(base + r0, 16), 16), :] = total
        return carry

    lax.fori_loop(0, blk // 16, part, 0)

    @pl.when(step == pl.num_programs(0) - 1)
    def _():
        rowed[...] = jnp.zeros_like(rowed)
        for near in range(9):
            r, c = near // 3, near % 3
            rowed[c, 7 + r : 7 + r + rows, :] += terms[near]
        lane = lax.broadcasted_iota(jnp.int32, (rows + 16, cols), 1)
        from_left = pltpu.roll(rowed[2], 1, 1)
        from_right = pltpu.roll(rowed[0], cols - 1, 1)
        main_ref[...] = (
            rowed[1]
            + jnp.where(lane == 0, 0.0, from_left)
            + jnp.where(lane == cols - 1, 0.0, from_right)
        )
        cols_ref[0] = rowed[0, :, :128]
        cols_ref[1] = rowed[2, :, cols - 128 :]


def back(g, coef, xi):
    rows, cols = coef.shape[2:]
    blk = 64
    grad, main, side = pl.pallas_call(
        functools.partial(back_kernel, blk),
        grid=(rows // blk,),
        in_specs=[
            pl.BlockSpec((2 * blk, 2 * cols), lambda i: (i, 0)),
            pl.BlockSpec((4, 9, blk, cols), lambda i: (0, 0, i, 0)),
            pl.BlockSpec((2 * blk, 2 * cols), lambda i: (i, 0)),
        ],
        out_specs=[
            pl.BlockSpec((2 * blk, 2 * cols), lambda i: (i, 0)),
            pl.BlockSpec((rows + 16, cols), lambda i: (0, 0)),
            pl.BlockSpec((2, rows + 16, 128), lambda i: (0, 0, 0)),
        ],
        out_shape=[
            jax.ShapeDtypeStruct((2 * rows, 2 * cols), f32),
            jax.ShapeDtypeStruct((rows + 16, cols), f32),
            jax.ShapeDtypeStruct((2, rows + 16, 128), f32),
        ],
        scratch_shapes=[
            pltpu.VMEM((9, rows, cols), f32),
            pltpu.VMEM((2 * cols, 2 * cols), bf16),
            pltpu.VMEM((2 * cols // 128, 2 * blk, 128), f32),
            pltpu.VMEM((3, rows + 16, cols), f32),
        ],
        compiler_params=pltpu.CompilerParams(vmem_limit_bytes=vmem),
        name="back",
    )(g, coef, xi)
    size = lax.axis_size("gy")
    right = [(i, i + 1) for i in range(size - 1)]
    left = [(j, i) for i, j in right]
    from_left = lax.ppermute(side[1, 7 : 9 + rows, 127], "gy", right)
    from_right = lax.ppermute(side[0, 7 : 9 + rows, 0], "gy", left)
    main = main[7 : 9 + rows]
    ends = jnp.pad(from_left[:, None], ((0, 0), (0, cols - 1))) + jnp.pad(
        from_right[:, None], ((0, 0), (cols - 1, 0))
    )
    size = lax.axis_size("gx")
    down = [(i, i + 1) for i in range(size - 1)]
    up = [(j, i) for i, j in down]
    from_above = lax.ppermute(main[-1:] + ends[-1:], "gx", down)
    from_below = lax.ppermute(main[:1] + ends[:1], "gx", up)
    result = (
        main[1:-1]
        + ends[1:-1]
        + jnp.pad(from_above, ((0, rows - 1), (0, 0)))
        + jnp.pad(from_below, ((rows - 1, 0), (0, 0)))
    )
    return grad, result


def facet_kernel(
    blk, lists, weights, counts, one_ref, two_ref, ku_ref, kv_ref, data_ref, out_ref, lik_ref, sums, dsum
):
    facet, step = pl.program_id(0), pl.program_id(1)
    facets, steps = pl.num_programs(0), pl.num_programs(1)

    @pl.when((facet == 0) & (step == 0))
    def _():
        lik_ref[...] = jnp.zeros_like(lik_ref)

    @pl.when(step == 0)
    def _():
        sums[...] = (
            weights[facet, 0] * one_ref[0].astype(f32) + weights[facet, 1] * two_ref[0].astype(f32)
        ).astype(bf16)
        dsum[facet] = jnp.zeros(dsum.shape[1:], f32)

    count = counts[facet] - step * blk

    @pl.when(count > 0)
    def _():
        ku, kv = ku_ref[0, 0], kv_ref[0, 0]
        amp = jnp.dot(ku, sums[...], preferred_element_type=f32).astype(bf16)
        vis = lax.dot_general(amp, kv, (((1,), (1,)), ((), ())), preferred_element_type=f32)
        live = lax.broadcasted_iota(jnp.int32, vis.shape, 0) < count
        resid = jnp.where(live, vis - data_ref[0, 0].astype(f32), 0.0)
        lik_ref[...] += jnp.sum((resid * resid).reshape(blk // 8, 8, vis.shape[1]), axis=0)
        dvis = (inv_noise * resid).astype(bf16)
        damp = jnp.dot(dvis, kv, preferred_element_type=f32).astype(bf16)
        dsum[facet] += lax.dot_general(
            ku, damp, (((0,), (0,)), ((), ())), preferred_element_type=f32
        )

    @pl.when((facet == facets - 1) & (step == steps - 1))
    def _():
        for t in range(out_ref.shape[0]):
            total = None
            for f in range(dsum.shape[0]):
                scale = jnp.float32(0.0)
                for s in range(lists.shape[1]):
                    scale += jnp.where(lists[f, s] == t, weights[f, s], 0.0)
                term = scale * dsum[f]
                total = term if total is None else total + term
            out_ref[t] = total.astype(bf16)


def facets(tiles, ku, kv, data, lists, weights, counts):
    number, bins, side = ku.shape[1:]
    blk = 256
    return pl.pallas_call(
        functools.partial(facet_kernel, blk),
        grid_spec=pltpu.PrefetchScalarGridSpec(
            num_scalar_prefetch=3,
            grid=(number, bins // blk),
            in_specs=[
                pl.BlockSpec((1, side, side), lambda f, i, ls, ws, cs: (ls[f, 0], 0, 0)),
                pl.BlockSpec((1, side, side), lambda f, i, ls, ws, cs: (ls[f, 1], 0, 0)),
                pl.BlockSpec((1, 1, blk, side), lambda f, i, ls, ws, cs: (0, f, i, 0)),
                pl.BlockSpec((1, 1, bins, side), lambda f, i, ls, ws, cs: (0, f, 0, 0)),
                pl.BlockSpec((1, 1, blk, bins), lambda f, i, ls, ws, cs: (0, f, i, 0)),
            ],
            out_specs=[
                pl.BlockSpec(tiles.shape, lambda f, i, ls, ws, cs: (0, 0, 0)),
                pl.BlockSpec((8, bins), lambda f, i, ls, ws, cs: (0, 0)),
            ],
            scratch_shapes=[
                pltpu.VMEM((side, side), bf16),
                pltpu.VMEM((number, side, side), f32),
            ],
        ),
        out_shape=[
            jax.ShapeDtypeStruct(tiles.shape, bf16),
            jax.ShapeDtypeStruct((8, bins), f32),
        ],
        compiler_params=pltpu.CompilerParams(vmem_limit_bytes=vmem),
        name="facets",
    )(lists, weights, counts, tiles, tiles, ku, kv, data)


def body(
    xi_coarse,
    xi_middle,
    xi_fine,
    coef_middle,
    coef_fine,
    kern_u,
    kern_v,
    vis_data,
    facet_tiles,
    facet_weight,
    facet_count,
):
    side = xi_fine.shape[0]
    level_middle, sq_middle = refine(widen(xi_coarse), coef_middle, xi_middle, f32)
    sky, sq_fine = refine(widen(level_middle), coef_fine, xi_fine, bf16)
    tiles = lax.all_gather(sky, "gy", axis=0)
    dtiles, lik = facets(
        tiles, kern_u, kern_v, vis_data, facet_tiles[0], facet_weight[0], facet_count[0]
    )
    potential = 0.5 * (jnp.sum(xi_coarse * xi_coarse) + jnp.sum(sq_middle) + jnp.sum(sq_fine))
    potential = (potential + 0.5 * inv_noise * jnp.sum(lik))[None]
    for axis in ("gy", "gx"):
        size = lax.axis_size(axis)
        hop = 1
        while hop < size:
            potential += lax.ppermute(potential, axis, [(i, i ^ hop) for i in range(size)])
            hop *= 2
    dsky = lax.psum_scatter(dtiles, "gy", scatter_dimension=0, tiled=False)
    grad_fine, dmiddle = back(dsky, coef_fine, xi_fine)
    grad_middle, dcoarse = back(dmiddle, coef_middle, xi_middle)
    grad_coarse = dcoarse + xi_coarse
    cells = lax.axis_size("gx") * lax.axis_size("gy") * side * side
    return (grad_coarse, grad_middle, grad_fine, potential[0] / cells)


def solution(mesh):
    placed = (
        P("gx", "gy"),
        P("gx", "gy"),
        P("gx", "gy"),
        P(None, None, "gx", "gy"),
        P(None, None, "gx", "gy"),
        P("gx", "gy", None, None),
        P("gx", "gy", None, None),
        P("gx", "gy", None, None),
        P("gx", "gy", None),
        P("gx", "gy", None),
        P("gx", "gy"),
    )
    return jax.shard_map(
        body,
        mesh=mesh,
        in_specs=placed,
        out_specs=(P("gx", "gy"), P("gx", "gy"), P("gx", "gy"), P()),
        check_vma=False,
    )
```

```python
import functools

import jax
import jax.numpy as jnp
from jax import lax
from jax.experimental import pallas as pl
from jax.experimental.pallas import tpu as pltpu
from jax.sharding import PartitionSpec as P

inv_noise = 0.125
vmem = 56 * 1024 * 1024
f32 = jnp.float32
bf16 = jnp.bfloat16


def extended(x, sides, width):
    for axis, dim in sides:
        size, length = (lax.axis_size(axis), x.shape[dim])
        up = [(i, (i + 1) % size) for i in range(size - 1)]
        down = [(j, i) for i, j in up]
        last = lax.slice_in_dim(x, length - width, length, axis=dim)
        leading = lax.slice_in_dim(x, 0, width, axis=dim)
        before = lax.ppermute(last, axis, up)
        after = lax.ppermute(leading, axis, down)
        x = jnp.concatenate([before, x, after], axis=dim)
    return x


def widen(field):
    return extended(field, (("gx", 0), ("gy", 1)), 1)


def halves(x):
    high = x.astype(bf16)
    return high, (x - high.astype(f32)).astype(bf16)


def interleaver(cols, transposed):
    shape = (2 * cols, 2 * cols)
    split = lax.broadcasted_iota(jnp.int32, shape, 1 if transposed else 0)
    whole = lax.broadcasted_iota(jnp.int32, shape, 0 if transposed else 1)
    place = jnp.where(split >= cols, 2 * (split - cols) + 1, 2 * split)
    return (place == whole).astype(f32).astype(bf16)


def refine_kernel(blk, pad_ref, coef_ref, xi_ref, out_ref, sq_ref, win, perm, lhs, mix):
    rows, cols = win.shape[1:]
    step = pl.program_id(0)

    @pl.when(step == 0)
    def _():
        for near in range(9):
            r, c = near // 3, near % 3
            win[near] = pad_ref[r : r + rows, c : c + cols]
        perm[...] = interleaver(cols, False)
        sq_ref[...] = jnp.zeros_like(sq_ref)

    base = step * blk

    def part(i, carry):
        r0 = pl.multiple_of(i * 16, 16)
        total = [jnp.zeros((16, cols), f32) for _ in range(4)]
        for near in range(9):
            w = win[near, pl.ds(pl.multiple_of(base + r0, 16), 16), :]
            for child in range(4):
                total[child] += coef_ref[child, near, pl.ds(r0, 16), :].astype(f32) * w
        for child in range(4):
            a, b = child // 2, child % 2
            high, low = halves(total[child])
            lhs[pl.ds(2 * a * blk + r0, 16), b * cols : (b + 1) * cols] = high
            lhs[pl.ds((2 * a + 1) * blk + r0, 16), b * cols : (b + 1) * cols] = low
        return carry

    lax.fori_loop(0, blk // 16, part, 0)
    field = jnp.dot(lhs[...], perm[...], preferred_element_type=f32)
    xi = xi_ref[...]
    for tile in range(2 * cols // 128):
        lanes = slice(tile * 128, (tile + 1) * 128)
        for a in range(2):
            mix[tile, pl.ds(a, blk, stride=2), :] = (
                field[2 * a * blk : (2 * a + 1) * blk, lanes]
                + field[(2 * a + 1) * blk : (2 * a + 2) * blk, lanes]
            )
        out_ref[:, lanes] = (mix[tile] + xi[:, lanes]).astype(out_ref.dtype)
    sq_ref[...] += jnp.sum((xi * xi).reshape(2 * blk // 8, 8, 2 * cols), axis=0)


def refine(padded, coef, xi, dtype):
    rows, cols = coef.shape[2:]
    blk = 64
    return pl.pallas_call(
        functools.partial(refine_kernel, blk),
        grid=(rows // blk,),
        in_specs=[
            pl.BlockSpec((rows + 2, cols + 2), lambda i: (0, 0)),
            pl.BlockSpec((4, 9, blk, cols), lambda i: (0, 0, i, 0)),
            pl.BlockSpec((2 * blk, 2 * cols), lambda i: (i, 0)),
        ],
        out_specs=[
            pl.BlockSpec((2 * blk, 2 * cols), lambda i: (i, 0)),
            pl.BlockSpec((8, 2 * cols), lambda i: (0, 0)),
        ],
        out_shape=[
            jax.ShapeDtypeStruct((2 * rows, 2 * cols), dtype),
            jax.ShapeDtypeStruct((8, 2 * cols), f32),
        ],
        scratch_shapes=[
            pltpu.VMEM((9, rows, cols), f32),
            pltpu.VMEM((2 * cols, 2 * cols), bf16),
            pltpu.VMEM((4 * blk, 2 * cols), bf16),
            pltpu.VMEM((2 * cols // 128, 2 * blk, 128), f32),
        ],
        compiler_params=pltpu.CompilerParams(vmem_limit_bytes=vmem),
        name="refine",
    )(padded, coef, xi)


def back_kernel(blk, number, *refs):
    parts = refs[:number]
    coef_ref, xi_ref, grad_ref, main_ref, cols_ref, terms, perm, mix, rowed = refs[number:]
    rows, cols = terms.shape[1:]
    step = pl.program_id(0)

    @pl.when(step == 0)
    def _():
        perm[...] = interleaver(cols, True)

    base = step * blk
    g = parts[0][...].astype(f32)
    for part in parts[1:]:
        g += part[...].astype(f32)
    grad_ref[...] = g + xi_ref[...]
    high, low = halves(g)
    both = jnp.dot(jnp.concatenate([high, low]), perm[...], preferred_element_type=f32)
    split = both[: 2 * blk] + both[2 * blk :]
    for tile in range(2 * cols // 128):
        mix[tile] = split[:, tile * 128 : (tile + 1) * 128]

    def part(i, carry):
        r0 = pl.multiple_of(i * 16, 16)
        quads = []
        for a in range(2):
            for b in range(2):
                tiles = range(b * cols // 128, (b + 1) * cols // 128)
                lines = [mix[t, pl.ds(2 * r0 + a, 16, stride=2), :] for t in tiles]
                quads.append(jnp.concatenate(lines, axis=1))
        for near in range(9):
            total = jnp.zeros((16, cols), f32)
            for child in range(4):
                total += coef_ref[child, near, pl.ds(r0, 16), :].astype(f32) * quads[child]
            terms[near, pl.ds(pl.multiple_of(base + r0, 16), 16), :] = total
        return carry

    lax.fori_loop(0, blk // 16, part, 0)

    @pl.when(step == pl.num_programs(0) - 1)
    def _():
        rowed[...] = jnp.zeros_like(rowed)
        for near in range(9):
            r, c = near // 3, near % 3
            rowed[c, 7 + r : 7 + r + rows, :] += terms[near]
        lane = lax.broadcasted_iota(jnp.int32, (rows + 16, cols), 1)
        from_left = pltpu.roll(rowed[2], 1, 1)
        from_right = pltpu.roll(rowed[0], cols - 1, 1)
        main_ref[...] = (
            rowed[1]
            + jnp.where(lane == 0, 0.0, from_left)
            + jnp.where(lane == cols - 1, 0.0, from_right)
        )
        cols_ref[0] = rowed[0, :, :128]
        cols_ref[1] = rowed[2, :, cols - 128 :]


def back(parts, coef, xi):
    rows, cols = coef.shape[2:]
    blk = 64
    grad, main, side = pl.pallas_call(
        functools.partial(back_kernel, blk, len(parts)),
        grid=(rows // blk,),
        in_specs=[pl.BlockSpec((2 * blk, 2 * cols), lambda i: (i, 0))] * len(parts)
        + [
            pl.BlockSpec((4, 9, blk, cols), lambda i: (0, 0, i, 0)),
            pl.BlockSpec((2 * blk, 2 * cols), lambda i: (i, 0)),
        ],
        out_specs=[
            pl.BlockSpec((2 * blk, 2 * cols), lambda i: (i, 0)),
            pl.BlockSpec((rows + 16, cols), lambda i: (0, 0)),
            pl.BlockSpec((2, rows + 16, 128), lambda i: (0, 0, 0)),
        ],
        out_shape=[
            jax.ShapeDtypeStruct((2 * rows, 2 * cols), f32),
            jax.ShapeDtypeStruct((rows + 16, cols), f32),
            jax.ShapeDtypeStruct((2, rows + 16, 128), f32),
        ],
        scratch_shapes=[
            pltpu.VMEM((9, rows, cols), f32),
            pltpu.VMEM((2 * cols, 2 * cols), bf16),
            pltpu.VMEM((2 * cols // 128, 2 * blk, 128), f32),
            pltpu.VMEM((3, rows + 16, cols), f32),
        ],
        compiler_params=pltpu.CompilerParams(vmem_limit_bytes=vmem),
        name="back",
    )(*parts, coef, xi)
    size = lax.axis_size("gy")
    right = [(i, i + 1) for i in range(size - 1)]
    left = [(j, i) for i, j in right]
    from_left = lax.ppermute(side[1, 7 : 9 + rows, 127], "gy", right)
    from_right = lax.ppermute(side[0, 7 : 9 + rows, 0], "gy", left)
    main = main[7 : 9 + rows]
    ends = jnp.pad(from_left[:, None], ((0, 0), (0, cols - 1))) + jnp.pad(
        from_right[:, None], ((0, 0), (cols - 1, 0))
    )
    size = lax.axis_size("gx")
    down = [(i, i + 1) for i in range(size - 1)]
    up = [(j, i) for i, j in down]
    from_above = lax.ppermute(main[-1:] + ends[-1:], "gx", down)
    from_below = lax.ppermute(main[:1] + ends[:1], "gx", up)
    result = (
        main[1:-1]
        + ends[1:-1]
        + jnp.pad(from_above, ((0, rows - 1), (0, 0)))
        + jnp.pad(from_below, ((rows - 1, 0), (0, 0)))
    )
    return grad, result


def facet_kernel(
    blk, number, sel, weights, counts, *refs
):
    tiles = refs[:number]
    ku_ref, kv_ref, data_ref, out_ref, lik_ref, sums, dsum, held, sems = refs[number:]
    step = pl.program_id(0)

    @pl.when(step == 0)
    def _():
        for s in range(held.shape[0]):
            for i in range(number):

                @pl.when(sel[s] == i)
                def _():
                    pltpu.make_async_copy(tiles[i], held.at[s], sems.at[s]).start()

        lik_ref[...] = jnp.zeros_like(lik_ref)
        dsum[...] = jnp.zeros_like(dsum)
        total = jnp.zeros(dsum.shape, f32)
        for s in range(held.shape[0]):
            pltpu.make_async_copy(tiles[0], held.at[s], sems.at[s]).wait()
            total += weights[s] * held[s].astype(f32)
        sums[...] = total.astype(bf16)

    count = counts[0] - step * blk

    @pl.when(count > 0)
    def _():
        ku, kv = ku_ref[0, 0], kv_ref[0, 0]
        amp = jnp.dot(ku, sums[...], preferred_element_type=f32).astype(bf16)
        vis = lax.dot_general(amp, kv, (((1,), (1,)), ((), ())), preferred_element_type=f32)
        live = lax.broadcasted_iota(jnp.int32, vis.shape, 0) < count
        resid = jnp.where(live, vis - data_ref[0, 0].astype(f32), 0.0)
        lik_ref[...] += jnp.sum((resid * resid).reshape(blk // 8, 8, vis.shape[1]), axis=0)
        dvis = (inv_noise * resid).astype(bf16)
        damp = jnp.dot(dvis, kv, preferred_element_type=f32).astype(bf16)
        dsum[...] += lax.dot_general(ku, damp, (((0,), (0,)), ((), ())), preferred_element_type=f32)

    @pl.when(step == pl.num_programs(0) - 1)
    def _():
        out_ref[...] = dsum[...].astype(bf16)


def facet(f, tiles, ku, kv, data, sel, weights, count):
    bins, side = ku.shape[2:]
    blk = 256
    slots = sel.shape[0]
    return pl.pallas_call(
        functools.partial(facet_kernel, blk, len(tiles)),
        grid_spec=pltpu.PrefetchScalarGridSpec(
            num_scalar_prefetch=3,
            grid=(bins // blk,),
            in_specs=[pl.BlockSpec(memory_space=pl.ANY)] * len(tiles)
            + [
                pl.BlockSpec((1, 1, blk, side), lambda i, *_: (0, f, i, 0)),
                pl.BlockSpec((1, 1, bins, side), lambda i, *_: (0, f, 0, 0)),
                pl.BlockSpec((1, 1, blk, bins), lambda i, *_: (0, f, i, 0)),
            ],
            out_specs=[
                pl.BlockSpec((side, side), lambda i, *_: (0, 0)),
                pl.BlockSpec((8, bins), lambda i, *_: (0, 0)),
            ],
            scratch_shapes=[
                pltpu.VMEM((side, side), bf16),
                pltpu.VMEM((side, side), f32),
                pltpu.VMEM((slots, side, side), bf16),
                pltpu.SemaphoreType.DMA((slots,)),
            ],
        ),
        out_shape=[
            jax.ShapeDtypeStruct((side, side), bf16),
            jax.ShapeDtypeStruct((8, bins), f32),
        ],
        compiler_params=pltpu.CompilerParams(vmem_limit_bytes=vmem),
        name="facet",
    )(sel, weights, count, *tiles, ku, kv, data)


def mix_kernel(number, scale, *refs):
    dsums, outs = refs[:number], refs[number:]
    for d, out in enumerate(outs):
        total = None
        for f, dsum in enumerate(dsums):
            term = scale[d, f] * dsum[...].astype(f32)
            total = term if total is None else total + term
        out[...] = total.astype(bf16)


def mixed(dsums, scale):
    rows, cols = dsums[0].shape
    blk = 128
    return pl.pallas_call(
        functools.partial(mix_kernel, len(dsums)),
        grid_spec=pltpu.PrefetchScalarGridSpec(
            num_scalar_prefetch=1,
            grid=(rows // blk,),
            in_specs=[pl.BlockSpec((blk, cols), lambda i, _: (i, 0))] * len(dsums),
            out_specs=[pl.BlockSpec((blk, cols), lambda i, _: (i, 0))] * scale.shape[0],
        ),
        out_shape=[jax.ShapeDtypeStruct((rows, cols), bf16)] * scale.shape[0],
        compiler_params=pltpu.CompilerParams(vmem_limit_bytes=vmem),
        name="mixed",
    )(scale, *dsums)


def chip_shift(x, hop):
    size = lax.axis_size("gy")
    return lax.ppermute(x, "gy", [(i, (i + 2 * hop) % size) for i in range(size)])


def swapped(x):
    return lax.ppermute(x, "gy", [(i, i ^ 1) for i in range(lax.axis_size("gy"))])


def summed(x):
    for axis in ("gy", "gx"):
        size = lax.axis_size(axis)
        hop = 1
        while hop < size:
            x += lax.ppermute(x, axis, [(i, i ^ hop) for i in range(size)])
            hop *= 2
    return x


def body(
    xi_coarse,
    xi_middle,
    xi_fine,
    coef_middle,
    coef_fine,
    kern_u,
    kern_v,
    vis_data,
    facet_tiles,
    facet_weight,
    facet_count,
):
    side = xi_fine.shape[0]
    level_middle, sq_middle = refine(widen(xi_coarse), coef_middle, xi_middle, f32)
    sky, sq_fine = refine(widen(level_middle), coef_fine, xi_fine, bf16)
    lists, weights, counts = facet_tiles[0], facet_weight[0], facet_count[0]
    number = lists.shape[0]
    size = lax.axis_size("gy")
    chips = size // 2
    me = lax.axis_index("gy")
    ids = jnp.arange(size, dtype=jnp.int32)
    mixing = jnp.sum(
        weights[:, :, None] * (lists[:, :, None] == ids[None, None, :]).astype(f32), axis=1
    )
    order = 2 * ((me // 2 + jnp.arange(chips, dtype=jnp.int32)) % chips) + me % 2
    scale = jnp.concatenate([mixing, swapped(mixing)])[:, order].T
    mine = [sky] + [chip_shift(sky, hop) for hop in range(1, chips)]
    tiles = mine + [swapped(tile) for tile in mine]
    sel = (me // 2 - lists // 2) % chips + jnp.where(lists % 2 == me % 2, 0, chips)
    dsums, theirs, likelihood = [], [], 0.0
    for f in range(number):
        dsum, lik = facet(
            f, tiles, kern_u, kern_v, vis_data, sel[f], weights[f], counts[f : f + 1]
        )
        dsums.append(dsum)
        theirs.append(swapped(dsum))
        likelihood += jnp.sum(lik)
    parts = mixed(dsums + theirs, scale)
    parts = [parts[0]] + [chip_shift(parts[hop], hop) for hop in range(1, chips)]
    potential = 0.5 * (jnp.sum(xi_coarse * xi_coarse) + jnp.sum(sq_middle) + jnp.sum(sq_fine))
    potential = summed((potential + 0.5 * inv_noise * likelihood)[None])
    parts, potential = lax.optimization_barrier((parts, potential))
    grad_fine, dmiddle = back(parts, coef_fine, xi_fine)
    grad_middle, dcoarse = back([dmiddle], coef_middle, xi_middle)
    grad_coarse = dcoarse + xi_coarse
    cells = lax.axis_size("gx") * lax.axis_size("gy") * side * side
    return (grad_coarse, grad_middle, grad_fine, potential[0] / cells)


def solution(mesh):
    placed = (
        P("gx", "gy"),
        P("gx", "gy"),
        P("gx", "gy"),
        P(None, None, "gx", "gy"),
        P(None, None, "gx", "gy"),
        P("gx", "gy", None, None),
        P("gx", "gy", None, None),
        P("gx", "gy", None, None),
        P("gx", "gy", None),
        P("gx", "gy", None),
        P("gx", "gy"),
    )
    return jax.shard_map(
        body,
        mesh=mesh,
        in_specs=placed,
        out_specs=(P("gx", "gy"), P("gx", "gy"), P("gx", "gy"), P()),
        check_vma=False,
    )
```

```python
import functools

import jax
import jax.numpy as jnp
from jax import lax
from jax.experimental import pallas as pl
from jax.experimental.pallas import tpu as pltpu
from jax.sharding import PartitionSpec as P

inv_noise = 0.125
vmem = 24 * 1024 * 1024
f32 = jnp.float32
bf16 = jnp.bfloat16


def extended(x, sides, width):
    for axis, dim in sides:
        size, length = (lax.axis_size(axis), x.shape[dim])
        up = [(i, (i + 1) % size) for i in range(size - 1)]
        down = [(j, i) for i, j in up]
        last = lax.slice_in_dim(x, length - width, length, axis=dim)
        leading = lax.slice_in_dim(x, 0, width, axis=dim)
        before = lax.ppermute(last, axis, up)
        after = lax.ppermute(leading, axis, down)
        x = jnp.concatenate([before, x, after], axis=dim)
    return x


def widen(field):
    return extended(field, (("gx", 0), ("gy", 1)), 1)


def halves(x):
    high = x.astype(bf16)
    return high, (x - high.astype(f32)).astype(bf16)


def interleaver(cols, transposed):
    shape = (2 * cols, 2 * cols)
    split = lax.broadcasted_iota(jnp.int32, shape, 1 if transposed else 0)
    whole = lax.broadcasted_iota(jnp.int32, shape, 0 if transposed else 1)
    place = jnp.where(split >= cols, 2 * (split - cols) + 1, 2 * split)
    return (place == whole).astype(f32).astype(bf16)


def folded(x):
    rows, cols = x.shape
    x = jnp.sum(x.reshape(rows // 8, 8, cols), axis=0)
    return sum(x[:, i : i + 128] for i in range(0, cols, 128))


def refine_kernel(first, pad_ref, coef_ref, xi_ref, out_ref, sq_ref, win, perm, lhs, mix):
    rows, cols = win.shape[1:]
    for near in range(9):
        r, c = near // 3, near % 3
        win[near] = pad_ref[r : r + rows, c : c + cols]
    perm[...] = interleaver(cols, False)

    def part(i, carry):
        r0 = pl.multiple_of(i * 16, 16)
        total = [jnp.zeros((16, cols), f32) for _ in range(4)]
        for near in range(9):
            w = win[near, pl.ds(r0, 16), :]
            for child in range(4):
                total[child] += coef_ref[child, near, pl.ds(r0, 16), :].astype(f32) * w
        for child in range(4):
            a, b = child // 2, child % 2
            high, low = halves(total[child])
            lhs[pl.ds(2 * a * rows + r0, 16), b * cols : (b + 1) * cols] = high
            lhs[pl.ds((2 * a + 1) * rows + r0, 16), b * cols : (b + 1) * cols] = low
        return carry

    lax.fori_loop(0, rows // 16, part, 0)
    field = jnp.dot(lhs[...], perm[...], preferred_element_type=f32)
    xi = xi_ref[...]
    for tile in range(2 * cols // 128):
        lanes = slice(tile * 128, (tile + 1) * 128)
        for a in range(2):
            mix[tile, pl.ds(a, rows, stride=2), :] = (
                field[2 * a * rows : (2 * a + 1) * rows, lanes]
                + field[(2 * a + 1) * rows : (2 * a + 2) * rows, lanes]
            )
        out_ref[:, lanes] = (mix[tile] + xi[:, lanes]).astype(out_ref.dtype)
    square = folded(xi * xi)
    if first:
        square += folded(win[4] * win[4])
    sq_ref[...] = square


whole = pl.BlockSpec(memory_space=pltpu.VMEM)
scalar = pl.BlockSpec(memory_space=pltpu.SMEM)


def refine(padded, coef, xi, dtype, first):
    rows, cols = coef.shape[2:]
    return pl.pallas_call(
        functools.partial(refine_kernel, first),
        in_specs=[whole] * 3,
        out_specs=[whole] * 2,
        out_shape=[
            jax.ShapeDtypeStruct((2 * rows, 2 * cols), dtype),
            jax.ShapeDtypeStruct((8, 128), f32),
        ],
        scratch_shapes=[
            pltpu.VMEM((9, rows, cols), f32),
            pltpu.VMEM((2 * cols, 2 * cols), bf16),
            pltpu.VMEM((4 * rows, 2 * cols), bf16),
            pltpu.VMEM((2 * cols // 128, 2 * rows, 128), f32),
        ],
        compiler_params=pltpu.CompilerParams(vmem_limit_bytes=vmem),
        name="refine",
    )(padded, coef, xi)


def back_kernel(number, *refs):
    parts = refs[:number]
    coef_ref, xi_ref, grad_ref, main_ref, cols_ref, total_ref, terms, perm, mix, rowed = refs[number:]
    rows, cols = terms.shape[1:]
    perm[...] = interleaver(cols, True)
    g = parts[0][: 2 * rows].astype(f32)
    for part in parts[1:]:
        g += part[: 2 * rows].astype(f32)
    grad_ref[...] = g + xi_ref[...]
    if parts[0].shape[0] > 2 * rows:
        rest = sum(part[2 * rows :, :128].astype(f32) for part in parts)
        total_ref[...] = rest[:8] + rest[8:16] + rest[16:24]
    else:
        total_ref[...] = jnp.zeros_like(total_ref)
    high, low = halves(g)
    split = jnp.dot(high, perm[...], preferred_element_type=f32)
    split += jnp.dot(low, perm[...], preferred_element_type=f32)
    for tile in range(2 * cols // 128):
        mix[tile] = split[:, tile * 128 : (tile + 1) * 128]

    def part(i, carry):
        r0 = pl.multiple_of(i * 16, 16)
        quads = []
        for a in range(2):
            for b in range(2):
                tiles = range(b * cols // 128, (b + 1) * cols // 128)
                lines = [mix[t, pl.ds(2 * r0 + a, 16, stride=2), :] for t in tiles]
                quads.append(jnp.concatenate(lines, axis=1))
        for near in range(9):
            total = jnp.zeros((16, cols), f32)
            for child in range(4):
                total += coef_ref[child, near, pl.ds(r0, 16), :].astype(f32) * quads[child]
            terms[near, pl.ds(r0, 16), :] = total
        return carry

    lax.fori_loop(0, rows // 16, part, 0)
    rowed[...] = jnp.zeros_like(rowed)
    for near in range(9):
        r, c = near // 3, near % 3
        rowed[c, 7 + r : 7 + r + rows, :] += terms[near]
    lane = lax.broadcasted_iota(jnp.int32, (rows + 16, cols), 1)
    from_left = pltpu.roll(rowed[2], 1, 1)
    from_right = pltpu.roll(rowed[0], cols - 1, 1)
    main_ref[...] = (
        rowed[1]
        + jnp.where(lane == 0, 0.0, from_left)
        + jnp.where(lane == cols - 1, 0.0, from_right)
    )
    cols_ref[0] = rowed[0, :, :128]
    cols_ref[1] = rowed[2, :, cols - 128 :]


def back(parts, coef, xi):
    rows, cols = coef.shape[2:]
    grad, main, side, total = pl.pallas_call(
        functools.partial(back_kernel, len(parts)),
        in_specs=[whole] * (len(parts) + 2),
        out_specs=[whole] * 4,
        out_shape=[
            jax.ShapeDtypeStruct((2 * rows, 2 * cols), f32),
            jax.ShapeDtypeStruct((rows + 16, cols), f32),
            jax.ShapeDtypeStruct((2, rows + 16, 128), f32),
            jax.ShapeDtypeStruct((8, 128), f32),
        ],
        scratch_shapes=[
            pltpu.VMEM((9, rows, cols), f32),
            pltpu.VMEM((2 * cols, 2 * cols), bf16),
            pltpu.VMEM((2 * cols // 128, 2 * rows, 128), f32),
            pltpu.VMEM((3, rows + 16, cols), f32),
        ],
        compiler_params=pltpu.CompilerParams(vmem_limit_bytes=vmem),
        name="back",
    )(*parts, coef, xi)
    size = lax.axis_size("gy")
    right = [(i, i + 1) for i in range(size - 1)]
    left = [(j, i) for i, j in right]
    from_left = lax.ppermute(side[1, 7 : 9 + rows, 127], "gy", right)
    from_right = lax.ppermute(side[0, 7 : 9 + rows, 0], "gy", left)
    main = main[7 : 9 + rows]
    ends = jnp.pad(from_left[:, None], ((0, 0), (0, cols - 1))) + jnp.pad(
        from_right[:, None], ((0, 0), (cols - 1, 0))
    )
    size = lax.axis_size("gx")
    down = [(i, i + 1) for i in range(size - 1)]
    up = [(j, i) for i, j in down]
    from_above = lax.ppermute(main[-1:] + ends[-1:], "gx", down)
    from_below = lax.ppermute(main[:1] + ends[:1], "gx", up)
    result = (
        main[1:-1]
        + ends[1:-1]
        + jnp.pad(from_above, ((0, rows - 1), (0, 0)))
        + jnp.pad(from_below, ((rows - 1, 0), (0, 0)))
    )
    return grad, result, total


def facet_kernel(f, blk, number, sel, weights, counts, *refs):
    tiles = refs[:number]
    ku_ref, kv_ref, data_ref, out_ref, lik_ref, sums, dsum = refs[number:]
    slots = sel.shape[1]
    for s in range(slots):
        for i in range(number):

            @pl.when(sel[f, s] == i)
            def _():
                term = weights[f, s] * tiles[i][...].astype(f32)
                if s > 0:
                    term += dsum[...]
                if s < slots - 1:
                    dsum[...] = term
                else:
                    sums[...] = term.astype(bf16)

    lik_ref[...] = jnp.zeros_like(lik_ref)
    for step in range(ku_ref.shape[2] // blk):
        rows = slice(step * blk, (step + 1) * blk)
        count = counts[f] - step * blk

        @pl.when(count > 0)
        def _():
            ku, kv = ku_ref[0, f, rows], kv_ref[0, f]
            amp = jnp.dot(ku, sums[...], preferred_element_type=f32).astype(bf16)
            vis = lax.dot_general(amp, kv, (((1,), (1,)), ((), ())), preferred_element_type=f32)
            live = lax.broadcasted_iota(jnp.int32, vis.shape, 0) < count
            resid = jnp.where(live, vis - data_ref[0, f, rows].astype(f32), 0.0)
            lik_ref[...] += inv_noise * folded(resid * resid)
            dvis = (inv_noise * resid).astype(bf16)
            damp = jnp.dot(dvis, kv, preferred_element_type=f32).astype(bf16)
            part = lax.dot_general(ku, damp, (((0,), (0,)), ((), ())), preferred_element_type=f32)
            if step == 0:
                dsum[...] = part
            else:
                dsum[...] += part

    out_ref[...] = dsum[...].astype(bf16)


def facet(f, tiles, ku, kv, data, sel, weights, counts):
    bins, side = ku.shape[2:]
    blk = 512
    return pl.pallas_call(
        functools.partial(facet_kernel, f, blk, len(tiles)),
        in_specs=[scalar] * 3 + [whole] * (len(tiles) + 3),
        out_specs=[whole] * 2,
        out_shape=[
            jax.ShapeDtypeStruct((side, side), bf16),
            jax.ShapeDtypeStruct((8, 128), f32),
        ],
        scratch_shapes=[pltpu.VMEM((side, side), bf16), pltpu.VMEM((side, side), f32)],
        compiler_params=pltpu.CompilerParams(vmem_limit_bytes=vmem),
        name="facet",
    )(sel, weights, counts, *tiles, ku, kv, data)


def mix_kernel(number, squares, scale, *refs):
    dsums, sums, outs = refs[:number], refs[number : number + squares], refs[number + squares :]
    total = 0.5 * sum(x[...] for x in sums)
    high = total.astype(bf16).astype(f32)
    middle = (total - high).astype(bf16).astype(f32)
    low = total - high - middle
    side = dsums[0].shape[0]
    for d, out in enumerate(outs):
        value = None
        for f, dsum in enumerate(dsums):
            term = scale[d, f] * dsum[...].astype(f32)
            value = term if value is None else value + term
        out[:side] = value.astype(bf16)
        out[side:] = jnp.zeros((32, out.shape[1]), bf16)
        out[side : side + 16, :128] = jnp.concatenate([high, middle]).astype(bf16)
        out[side + 16 :, :128] = jnp.concatenate([low, jnp.zeros_like(low)]).astype(bf16)


def mixed(dsums, scale, sums):
    rows, cols = dsums[0].shape
    return pl.pallas_call(
        functools.partial(mix_kernel, len(dsums), len(sums)),
        in_specs=[scalar] + [whole] * (len(dsums) + len(sums)),
        out_specs=[whole] * scale.shape[0],
        out_shape=[jax.ShapeDtypeStruct((rows + 32, cols), bf16)] * scale.shape[0],
        compiler_params=pltpu.CompilerParams(vmem_limit_bytes=vmem),
        name="mixed",
    )(scale, *dsums, *sums)


def chip_shift(x, hop):
    size = lax.axis_size("gy")
    return lax.ppermute(x, "gy", [(i, (i + 2 * hop) % size) for i in range(size)])


def swapped(x):
    return lax.ppermute(x, "gy", [(i, i ^ 1) for i in range(lax.axis_size("gy"))])


def body(
    xi_coarse,
    xi_middle,
    xi_fine,
    coef_middle,
    coef_fine,
    kern_u,
    kern_v,
    vis_data,
    facet_tiles,
    facet_weight,
    facet_count,
):
    side = xi_fine.shape[0]
    level_middle, sq_middle = refine(widen(xi_coarse), coef_middle, xi_middle, f32, True)
    sky, sq_fine = refine(widen(level_middle), coef_fine, xi_fine, bf16, False)
    lists, weights, counts = facet_tiles[0], facet_weight[0], facet_count[0]
    number = lists.shape[0]
    size = lax.axis_size("gy")
    chips = size // 2
    me = lax.axis_index("gy")
    ids = jnp.arange(size, dtype=jnp.int32)
    mixing = jnp.sum(
        weights[:, :, None] * (lists[:, :, None] == ids[None, None, :]).astype(f32), axis=1
    )
    order = 2 * ((me // 2 + jnp.arange(chips, dtype=jnp.int32)) % chips) + me % 2
    scale = jnp.concatenate([mixing, swapped(mixing)])[:, order].T
    mine = [sky] + [chip_shift(sky, hop) for hop in range(1, chips)]
    tiles = mine + [swapped(tile) for tile in mine]
    sel = (me // 2 - lists // 2) % chips + jnp.where(lists % 2 == me % 2, 0, chips)
    dsums, theirs, sums = [], [], [sq_middle, sq_fine]
    for f in range(number):
        dsum, lik = facet(f, tiles, kern_u, kern_v, vis_data, sel, weights, counts)
        dsums.append(dsum)
        theirs.append(swapped(dsum))
        sums.append(lik)
    parts = mixed(dsums + theirs, scale, sums)
    parts = [parts[0]] + [chip_shift(parts[hop], hop) for hop in range(1, chips)]
    grad_fine, dmiddle, total = back(parts, coef_fine, xi_fine)
    total = jnp.sum(total)[None]
    total += swapped(total)
    dmiddle, total = lax.optimization_barrier((dmiddle, total))
    grad_middle, dcoarse, _ = back([dmiddle], coef_middle, xi_middle)
    size = lax.axis_size("gx")
    hop = 1
    while hop < size:
        total += lax.ppermute(total, "gx", [(i, i ^ hop) for i in range(size)])
        hop *= 2
    grad_coarse = dcoarse + xi_coarse
    cells = lax.axis_size("gx") * lax.axis_size("gy") * side * side
    return (grad_coarse, grad_middle, grad_fine, total[0] / cells)


def solution(mesh):
    placed = (
        P("gx", "gy"),
        P("gx", "gy"),
        P("gx", "gy"),
        P(None, None, "gx", "gy"),
        P(None, None, "gx", "gy"),
        P("gx", "gy", None, None),
        P("gx", "gy", None, None),
        P("gx", "gy", None, None),
        P("gx", "gy", None),
        P("gx", "gy", None),
        P("gx", "gy"),
    )
    return jax.shard_map(
        body,
        mesh=mesh,
        in_specs=placed,
        out_specs=(P("gx", "gy"), P("gx", "gy"), P("gx", "gy"), P()),
        check_vma=False,
    )
```

```python
import functools

import jax
import jax.numpy as jnp
from jax import lax
from jax.experimental import pallas as pl
from jax.experimental.pallas import tpu as pltpu
from jax.sharding import PartitionSpec as P

inv_noise = 0.125
vmem = 24 * 1024 * 1024
f32 = jnp.float32
bf16 = jnp.bfloat16


def halves(x):
    high = x.astype(bf16)
    return high, (x - high.astype(f32)).astype(bf16)


def interleaver(cols, transposed):
    shape = (2 * cols, 2 * cols)
    split = lax.broadcasted_iota(jnp.int32, shape, 1 if transposed else 0)
    whole = lax.broadcasted_iota(jnp.int32, shape, 0 if transposed else 1)
    place = jnp.where(split >= cols, 2 * (split - cols) + 1, 2 * split)
    return (place == whole).astype(f32).astype(bf16)


def folded(x):
    rows, cols = x.shape
    x = jnp.sum(x.reshape(rows // 8, 8, cols), axis=0)
    return sum(x[:, i : i + 128] for i in range(0, cols, 128))


def row_of(ref, i):
    return ref[i : i + 1, :]


def dot_t(x, y, dims):
    return lax.dot_general(x, y, (dims, ((), ())), preferred_element_type=f32)


def moved(x, perm):
    high, low = halves(x)
    return jnp.dot(high, perm, preferred_element_type=f32) + jnp.dot(
        low, perm, preferred_element_type=f32
    )


def ends_placed(first, last, cols):
    rows = jnp.concatenate([first, first, last, last, jnp.zeros((4, first.shape[1]), f32)])
    high = rows.astype(bf16).astype(f32)
    index = lax.broadcasted_iota(jnp.int32, rows.shape, 0)
    rows = jnp.where(index % 2 == 0, high, rows - high).astype(bf16)
    shape = (8, cols)
    index = lax.broadcasted_iota(jnp.int32, shape, 0)
    lane = lax.broadcasted_iota(jnp.int32, shape, 1)
    place = ((index < 2) & (lane == 0)) | ((index >= 2) & (index < 4) & (lane == cols - 1))
    return dot_t(rows, place.astype(f32).astype(bf16), ((0,), (0,)))


def weighed(win, coef_ref, perm, lhs, mix, rows, cols):
    def part(i, carry):
        r0 = pl.multiple_of(i * 16, 16)
        total = [jnp.zeros((16, cols), f32) for _ in range(4)]
        for near in range(9):
            w = win[near, pl.ds(r0, 16), :]
            for child in range(4):
                total[child] += coef_ref[child, near, pl.ds(r0, 16), :].astype(f32) * w
        for child in range(4):
            a, b = child // 2, child % 2
            high, low = halves(total[child])
            lhs[pl.ds(2 * a * rows + r0, 16), b * cols : (b + 1) * cols] = high
            lhs[pl.ds((2 * a + 1) * rows + r0, 16), b * cols : (b + 1) * cols] = low
        return carry

    lax.fori_loop(0, rows // 16, part, 0)
    field = jnp.dot(lhs[...], perm[...], preferred_element_type=f32)
    for tile in range(2 * cols // 128):
        lanes = slice(tile * 128, (tile + 1) * 128)
        for a in range(2):
            mix[tile, pl.ds(a, rows, stride=2), :] = (
                field[2 * a * rows : (2 * a + 1) * rows, lanes]
                + field[(2 * a + 1) * rows : (2 * a + 2) * rows, lanes]
            )


def sky_kernel(
    wide,
    above,
    below,
    lefts,
    rights,
    to_left,
    to_right,
    coef_middle,
    xi_middle,
    coef_fine,
    xi_fine,
    sky_ref,
    sq_ref,
    win,
    perm,
    lhs,
    mix,
    shifted,
    fine_win,
    fine_perm,
    fine_lhs,
    fine_mix,
):
    rows, cols = win.shape[1:]
    for near in range(9):
        r, c = near // 3, near % 3
        win[near] = wide[1 + r : 1 + r + rows, 1 + c : 1 + c + cols]
    perm[...] = interleaver(cols, False)
    fine_perm[...] = interleaver(2 * cols, False)
    weighed(win, coef_middle, perm, lhs, mix, rows, cols)

    def across(message, top):
        out = []
        for b in range(2):
            line = row_of(message, 20 + b)
            for near in range(9):
                r, c = near // 3, near % 3
                line += row_of(message, 9 * b + near) * wide[top + r : top + r + 1, 1 + c : 1 + c + cols]
            out.append(line)
        return jnp.concatenate(out, axis=1)

    def along(message, fields):
        out = []
        for a in range(2):
            line = row_of(message, 20 + a)[:, 1 : rows + 3]
            for near in range(9):
                r, c = near // 3, near % 3
                line += row_of(message, 9 * a + near)[:, 1 : rows + 3] * fields[c][:, r : r + rows + 2]
            out.append(line)
        inner = jnp.concatenate([line[:, 1 : rows + 1] for line in out], axis=1)
        return inner, out[1][:, :1], out[0][:, rows + 1 :]

    top, bottom = across(above, 0), across(below, rows + 1)
    left, top_left, bottom_left = along(
        lefts, [row_of(lefts, 18), row_of(lefts, 19), row_of(to_left, 18)]
    )
    right, top_right, bottom_right = along(
        rights, [row_of(to_right, 19), row_of(rights, 18), row_of(rights, 19)]
    )
    lines = jnp.concatenate([top, bottom, left, right, jnp.zeros((4, 2 * cols), f32)])
    lines = moved(lines, perm[...])
    xi = xi_middle[...]
    last = 8 + 2 * rows
    for tile in range(2 * cols // 128):
        lanes = slice(tile * 128, (tile + 1) * 128)
        shifted[1, 8:last, lanes] = mix[tile] + xi[:, lanes]
    shifted[1, 7:8, :] = lines[0:1]
    shifted[1, last : last + 1, :] = lines[1:2]
    placed = ends_placed(lines[2:3], lines[3:4], 2 * cols)
    for side, lane, turn, first, final in (
        (0, 0, 1, top_left, bottom_left),
        (2, 2 * cols - 1, 2 * cols - 1, top_right, bottom_right),
    ):
        turned = pltpu.roll(shifted[1, 8:last, :], turn, 1)
        here = lax.broadcasted_iota(jnp.int32, turned.shape, 1) == lane
        shifted[side, 8:last, :] = jnp.where(here, placed, turned)
        ends = jnp.concatenate([lines[0:2], jnp.zeros((6, 2 * cols), f32)])
        ends = pltpu.roll(ends, turn, 1)
        here = lax.broadcasted_iota(jnp.int32, (1, 2 * cols), 1) == lane
        shifted[side, 7:8, :] = jnp.where(here, first, ends[0:1])
        shifted[side, last : last + 1, :] = jnp.where(here, final, ends[1:2])
    for near in range(9):
        r, c = near // 3, near % 3
        fine_win[near] = shifted[c, 7 + r : 7 + r + 2 * rows, :]
    weighed(fine_win, coef_fine, fine_perm, fine_lhs, fine_mix, 2 * rows, 2 * cols)
    for tile in range(4 * cols // 128):
        lanes = slice(tile * 128, (tile + 1) * 128)
        sky_ref[:, lanes] = (fine_mix[tile] + xi_fine[:, lanes]).astype(bf16)
    sq_ref[...] = (
        folded(win[4] * win[4]) + folded(xi * xi) + folded(xi_fine[...] * xi_fine[...])
    )


def neighbours(axis):
    size = lax.axis_size(axis)
    ahead = [(i, i + 1) for i in range(size - 1)]
    return ahead, [(j, i) for i, j in ahead]


def halo(xi_coarse, xi_middle, coef_middle):
    rows, cols = xi_coarse.shape
    down, up = neighbours("gx")
    right, left = neighbours("gy")

    def edge(a, row, near):
        return jnp.concatenate(
            [
                coef_middle[2 * a : 2 * a + 2, :, row].reshape(18, cols).astype(f32),
                near,
                xi_middle[2 * row + a].reshape(cols, 2).T,
            ]
        )

    above = lax.ppermute(edge(1, rows - 1, xi_coarse[-2:]), "gx", down)
    below = lax.ppermute(edge(0, 0, xi_coarse[:2]), "gx", up)

    def inside(b, col, near):
        return jnp.concatenate(
            [
                coef_middle[b::2, :, :, col].reshape(18, rows).astype(f32),
                near.T,
                xi_middle[:, 2 * col + b].reshape(rows, 2).T,
            ]
        )

    sides = inside(0, 0, xi_coarse[:, :2]), inside(1, cols - 1, xi_coarse[:, -2:])
    sides = lax.optimization_barrier(sides)

    def edges(b, col, first, side):
        zero = jnp.zeros((18,), f32)
        upper = jnp.stack(
            [
                jnp.concatenate([zero, above[18, first : first + 2], zero[:2]]),
                jnp.concatenate(
                    [
                        zero[:9],
                        above[9 * b : 9 * b + 9, col],
                        above[19, first : first + 2],
                        zero[:1],
                        above[20 + b : 21 + b, col],
                    ]
                ),
            ],
            axis=1,
        )
        lower = jnp.stack(
            [
                jnp.concatenate(
                    [
                        below[9 * b : 9 * b + 9, col],
                        zero[:9],
                        below[18, first : first + 2],
                        below[20 + b : 21 + b, col],
                        zero[:1],
                    ]
                ),
                jnp.concatenate([zero, below[19, first : first + 2], zero[:2]]),
            ],
            axis=1,
        )
        return jnp.concatenate([upper, side, lower], axis=1)

    to_left = edges(0, 0, 0, sides[0])
    to_right = edges(1, cols - 1, cols - 2, sides[1])
    lefts = lax.ppermute(to_right, "gy", right)
    rights = lax.ppermute(to_left, "gy", left)
    tall = jnp.concatenate([above[18:20], xi_coarse, below[18:20]])
    wide = jnp.concatenate([lefts[18:20].T, tall, rights[18:20].T], axis=1)
    return wide, above, below, lefts, rights, to_left, to_right


whole = pl.BlockSpec(memory_space=pltpu.VMEM)
scalar = pl.BlockSpec(memory_space=pltpu.SMEM)


def sky_of(halos, coef_middle, xi_middle, coef_fine, xi_fine):
    rows, cols = coef_middle.shape[2:]
    return pl.pallas_call(
        sky_kernel,
        in_specs=[whole] * 11,
        out_specs=[whole] * 2,
        out_shape=[
            jax.ShapeDtypeStruct((4 * rows, 4 * cols), bf16),
            jax.ShapeDtypeStruct((8, 128), f32),
        ],
        scratch_shapes=[
            pltpu.VMEM((9, rows, cols), f32),
            pltpu.VMEM((2 * cols, 2 * cols), bf16),
            pltpu.VMEM((4 * rows, 2 * cols), bf16),
            pltpu.VMEM((2 * cols // 128, 2 * rows, 128), f32),
            pltpu.VMEM((3, 2 * rows + 16, 2 * cols), f32),
            pltpu.VMEM((9, 2 * rows, 2 * cols), f32),
            pltpu.VMEM((4 * cols, 4 * cols), bf16),
            pltpu.VMEM((8 * rows, 4 * cols), bf16),
            pltpu.VMEM((4 * cols // 128, 4 * rows, 128), f32),
        ],
        compiler_params=pltpu.CompilerParams(vmem_limit_bytes=vmem),
        name="sky",
    )(*halos, coef_middle, xi_middle, coef_fine, xi_fine)


def spread(mix, coef_ref, terms, rows, cols):
    def part(i, carry):
        r0 = pl.multiple_of(i * 16, 16)
        quads = []
        for a in range(2):
            for b in range(2):
                tiles = range(b * cols // 128, (b + 1) * cols // 128)
                lines = [mix[t, pl.ds(2 * r0 + a, 16, stride=2), :] for t in tiles]
                quads.append(jnp.concatenate(lines, axis=1))
        for near in range(9):
            total = jnp.zeros((16, cols), f32)
            for child in range(4):
                total += coef_ref[child, near, pl.ds(r0, 16), :].astype(f32) * quads[child]
            terms[near, pl.ds(r0, 16), :] = total
        return carry

    lax.fori_loop(0, rows // 16, part, 0)


def joined(rowed, cols):
    lane = lax.broadcasted_iota(jnp.int32, rowed.shape[1:], 1)
    main = (
        rowed[1]
        + jnp.where(lane == 0, 0.0, pltpu.roll(rowed[2], 1, 1))
        + jnp.where(lane == cols - 1, 0.0, pltpu.roll(rowed[0], cols - 1, 1))
    )
    lane = lax.broadcasted_iota(jnp.int32, (8, cols), 1)
    outside = []
    for c, col in ((0, 0), (2, cols - 1)):
        pick = (lane == col).astype(f32).astype(bf16)
        high, low = halves(rowed[c])
        out = dot_t(pick, high, ((1,), (1,))) + dot_t(pick, low, ((1,), (1,)))
        outside.append(out[:1])
    return main, outside[0], outside[1]


def adjoint_kernel(number, *refs):
    parts = refs[:number]
    (
        above,
        below,
        lefts,
        rights,
        coef_middle,
        coef_fine,
        xi_fine,
        grad_ref,
        middle_ref,
        coarse_ref,
        left_ref,
        right_ref,
        upper_ref,
        lower_ref,
        total_ref,
        fine_perm,
        fine_mix,
        fine_terms,
        fine_rowed,
        perm,
        mix,
        terms,
        rowed,
    ) = refs[number:]
    rows, cols = terms.shape[1:]
    fine_perm[...] = interleaver(2 * cols, True)
    perm[...] = interleaver(cols, True)
    g = parts[0][: 4 * rows].astype(f32)
    for part in parts[1:]:
        g += part[: 4 * rows].astype(f32)
    grad_ref[...] = g + xi_fine[...]
    rest = sum(part[4 * rows :, :128].astype(f32) for part in parts)
    total_ref[...] = rest[:8] + rest[8:16] + rest[16:24]
    split = moved(g, fine_perm[...])
    for tile in range(4 * cols // 128):
        fine_mix[tile] = split[:, tile * 128 : (tile + 1) * 128]
    spread(fine_mix, coef_fine, fine_terms, 2 * rows, 2 * cols)
    fine_rowed[...] = jnp.zeros_like(fine_rowed)
    for near in range(9):
        r, c = near // 3, near % 3
        fine_rowed[c, 7 + r : 7 + r + 2 * rows, :] += fine_terms[near]
    main, left, right = joined(fine_rowed, 2 * cols)
    last = 8 + 2 * rows
    inner = main[8:last]
    middle_ref[...] = inner
    split = moved(inner, perm[...])
    for tile in range(2 * cols // 128):
        mix[tile] = split[:, tile * 128 : (tile + 1) * 128]
    spread(mix, coef_middle, terms, rows, cols)
    ring_above, ring_below = main[7:8], main[last : last + 1]
    lines = [ring_above, ring_below, left[:, 8:last], right[:, 8:last]]
    lines = moved(jnp.concatenate(lines + [jnp.zeros((4, 2 * cols), f32)]), perm[...])
    rowed[...] = jnp.zeros_like(rowed)
    for near in range(9):
        r, c = near // 3, near % 3
        rowed[c, 7 + r : 7 + r + rows, :] += terms[near]
    for line, message, top in ((0, above, 6), (1, below, 7 + rows)):
        for near in range(9):
            r, c = near // 3, near % 3
            term = row_of(message, near) * lines[line : line + 1, :cols]
            term += row_of(message, 9 + near) * lines[line : line + 1, cols:]
            rowed[c, top + r : top + r + 1, :] += term

    def along(line, ends, message):
        empty = jnp.zeros((1, 1), f32)
        first = [empty, lines[line : line + 1, :rows], ends[:, last : last + 1]]
        second = [ends[:, 7:8], lines[line : line + 1, cols : cols + rows], empty]
        first, second = jnp.concatenate(first, axis=1), jnp.concatenate(second, axis=1)
        out = []
        for c in range(3):
            total = jnp.zeros((1, rows + 4), f32)
            for r in range(3):
                near = 3 * r + c
                term = row_of(message, near)[:, 1 : rows + 3] * first
                term += row_of(message, 9 + near)[:, 1 : rows + 3] * second
                pads = [jnp.zeros((1, n), f32) for n in (r, 2 - r) if n]
                pieces = [term] + pads if r == 0 else pads[:1] + [term] + pads[1:]
                total += jnp.concatenate(pieces, axis=1)
            out.append(total)
        return out

    outer_left = along(2, left, lefts)
    outer_right = along(3, right, rights)
    main, near_left, near_right = joined(rowed, cols)
    coarse_ref[...] = main[8 : 8 + rows] + ends_placed(
        outer_left[2][:, 2 : rows + 2], outer_right[0][:, 2 : rows + 2], cols
    )
    lane = lax.broadcasted_iota(jnp.int32, (1, cols), 1)
    for ref, first, line in ((upper_ref, 6, ring_above), (lower_ref, 8 + rows, ring_below)):
        ref[...] = jnp.zeros_like(ref)
        for i in range(2):
            at = first - 6 + i
            ref[i : i + 1, :cols] = (
                main[first + i : first + i + 1]
                + jnp.where(lane == 0, outer_left[2][:, at : at + 1], 0.0)
                + jnp.where(lane == cols - 1, outer_right[0][:, at : at + 1], 0.0)
            )
        ref[2:3, :] = line
    for ref, far, close, beyond, ends in (
        (left_ref, outer_left[0], outer_left[1], near_left, left),
        (right_ref, outer_right[2], outer_right[1], near_right, right),
    ):
        ref[...] = jnp.zeros_like(ref)
        ref[0:1, : rows + 4] = far
        ref[1:2, : rows + 4] = close + beyond[:, 6 : rows + 10]
        ref[2:3, : 2 * rows + 2] = ends[:, 7 : 2 * rows + 9]


def final_kernel(middle, coarse, from_left, from_right, from_above, from_below, xi_middle, xi_coarse, middle_out, coarse_out):
    rows, cols = coarse.shape
    middle_out[...] = (
        middle[...]
        + xi_middle[...]
        + ends_placed(from_left[2:3, 1 : 2 * rows + 1], from_right[2:3, 1 : 2 * rows + 1], 2 * cols)
    )
    middle_out[:1] += from_above[2:3]
    middle_out[2 * rows - 1 :] += from_below[2:3]
    inner = slice(2, rows + 2)
    outer = ends_placed(from_left[1:2, inner], from_right[1:2, inner], cols)
    second = ends_placed(from_left[0:1, inner], from_right[0:1, inner], cols)
    lane = lax.broadcasted_iota(jnp.int32, second.shape, 1)
    second = jnp.where(lane == 1, pltpu.roll(second, 1, 1), 0.0) + jnp.where(
        lane == cols - 2, pltpu.roll(second, cols - 1, 1), 0.0
    )
    coarse_out[...] = coarse[...] + xi_coarse[...] + outer + second
    coarse_out[:2] += from_above[0:2, :cols]
    coarse_out[rows - 2 :] += from_below[0:2, :cols]


def adjoint(parts, halos, coef_middle, xi_middle, coef_fine, xi_fine, xi_coarse):
    rows, cols = coef_middle.shape[2:]
    _, above, below, lefts, rights, _, _ = halos
    shape = lambda *dims: jax.ShapeDtypeStruct(dims, f32)
    long = 2 * rows + 128
    grad_fine, middle, coarse, to_left, to_right, upper, lower, total = pl.pallas_call(
        functools.partial(adjoint_kernel, len(parts)),
        in_specs=[whole] * (len(parts) + 7),
        out_specs=[whole] * 8,
        out_shape=[
            shape(4 * rows, 4 * cols),
            shape(2 * rows, 2 * cols),
            shape(rows, cols),
            shape(8, long),
            shape(8, long),
            shape(8, 2 * cols),
            shape(8, 2 * cols),
            shape(8, 128),
        ],
        scratch_shapes=[
            pltpu.VMEM((4 * cols, 4 * cols), bf16),
            pltpu.VMEM((4 * cols // 128, 4 * rows, 128), f32),
            pltpu.VMEM((9, 2 * rows, 2 * cols), f32),
            pltpu.VMEM((3, 2 * rows + 128, 2 * cols), f32),
            pltpu.VMEM((2 * cols, 2 * cols), bf16),
            pltpu.VMEM((2 * cols // 128, 2 * rows, 128), f32),
            pltpu.VMEM((9, rows, cols), f32),
            pltpu.VMEM((3, rows + 128, cols), f32),
        ],
        compiler_params=pltpu.CompilerParams(vmem_limit_bytes=vmem),
        name="adjoint",
    )(*parts, above, below, lefts, rights, coef_middle, coef_fine, xi_fine)
    right, left = neighbours("gy")
    down, up = neighbours("gx")
    from_left = lax.ppermute(to_right, "gy", right)
    from_right = lax.ppermute(to_left, "gy", left)

    def corners(rows_out, at, end):
        first = jnp.stack([from_left[1, at : at + 2], from_left[0, at : at + 2]], axis=1)
        last = jnp.stack([from_right[0, at : at + 2], from_right[1, at : at + 2]], axis=1)
        pair = jnp.pad(first, ((0, 0), (0, 2 * cols - 2))) + jnp.pad(
            last, ((0, 0), (cols - 2, cols))
        )
        line = jnp.pad(from_left[2:3, end : end + 1], ((0, 0), (0, 2 * cols - 1))) + jnp.pad(
            from_right[2:3, end : end + 1], ((0, 0), (2 * cols - 1, 0))
        )
        return rows_out + jnp.pad(jnp.concatenate([pair, line]), ((0, 5), (0, 0)))

    from_below = lax.ppermute(corners(upper, 0, 0), "gx", up)
    from_above = lax.ppermute(corners(lower, rows + 2, 2 * rows + 1), "gx", down)
    grad_middle, grad_coarse = pl.pallas_call(
        final_kernel,
        in_specs=[whole] * 8,
        out_specs=[whole] * 2,
        out_shape=[shape(2 * rows, 2 * cols), shape(rows, cols)],
        compiler_params=pltpu.CompilerParams(vmem_limit_bytes=vmem),
        name="final",
    )(middle, coarse, from_left, from_right, from_above, from_below, xi_middle, xi_coarse)
    return grad_coarse, grad_middle, grad_fine, total


def facet_kernel(f, blk, number, sel, weights, counts, *refs):
    tiles = refs[:number]
    ku_ref, kv_ref, data_ref, out_ref, lik_ref, sums, dsum = refs[number:]
    slots = sel.shape[1]
    for s in range(slots):
        for i in range(number):

            @pl.when(sel[f, s] == i)
            def _():
                term = weights[f, s] * tiles[i][...].astype(f32)
                if s > 0:
                    term += dsum[...]
                if s < slots - 1:
                    dsum[...] = term
                else:
                    sums[...] = term.astype(bf16)

    lik_ref[...] = jnp.zeros_like(lik_ref)
    for step in range(ku_ref.shape[2] // blk):
        rows = slice(step * blk, (step + 1) * blk)
        count = counts[f] - step * blk

        @pl.when(count > 0)
        def _():
            ku, kv = ku_ref[0, f, rows], kv_ref[0, f]
            amp = jnp.dot(ku, sums[...], preferred_element_type=f32).astype(bf16)
            vis = lax.dot_general(amp, kv, (((1,), (1,)), ((), ())), preferred_element_type=f32)
            live = lax.broadcasted_iota(jnp.int32, vis.shape, 0) < count
            resid = jnp.where(live, vis - data_ref[0, f, rows].astype(f32), 0.0)
            lik_ref[...] += inv_noise * folded(resid * resid)
            dvis = (inv_noise * resid).astype(bf16)
            damp = jnp.dot(dvis, kv, preferred_element_type=f32).astype(bf16)
            part = lax.dot_general(ku, damp, (((0,), (0,)), ((), ())), preferred_element_type=f32)
            if step == 0:
                dsum[...] = part
            else:
                dsum[...] += part

    out_ref[...] = dsum[...].astype(bf16)


def facet(f, tiles, ku, kv, data, sel, weights, counts):
    bins, side = ku.shape[2:]
    blk = 512
    return pl.pallas_call(
        functools.partial(facet_kernel, f, blk, len(tiles)),
        in_specs=[scalar] * 3 + [whole] * (len(tiles) + 3),
        out_specs=[whole] * 2,
        out_shape=[
            jax.ShapeDtypeStruct((side, side), bf16),
            jax.ShapeDtypeStruct((8, 128), f32),
        ],
        scratch_shapes=[pltpu.VMEM((side, side), bf16), pltpu.VMEM((side, side), f32)],
        compiler_params=pltpu.CompilerParams(vmem_limit_bytes=vmem),
        name="facet",
    )(sel, weights, counts, *tiles, ku, kv, data)


def mix_kernel(number, squares, scale, *refs):
    dsums, sums, outs = refs[:number], refs[number : number + squares], refs[number + squares :]
    total = 0.5 * sum(x[...] for x in sums)
    high = total.astype(bf16).astype(f32)
    middle = (total - high).astype(bf16).astype(f32)
    low = total - high - middle
    side = dsums[0].shape[0]
    for d, out in enumerate(outs):
        value = None
        for f, dsum in enumerate(dsums):
            term = scale[d, f] * dsum[...].astype(f32)
            value = term if value is None else value + term
        out[:side] = value.astype(bf16)
        out[side:] = jnp.zeros((32, out.shape[1]), bf16)
        out[side : side + 16, :128] = jnp.concatenate([high, middle]).astype(bf16)
        out[side + 16 :, :128] = jnp.concatenate([low, jnp.zeros_like(low)]).astype(bf16)


def mixed(dsums, scale, sums):
    rows, cols = dsums[0].shape
    return pl.pallas_call(
        functools.partial(mix_kernel, len(dsums), len(sums)),
        in_specs=[scalar] + [whole] * (len(dsums) + len(sums)),
        out_specs=[whole] * scale.shape[0],
        out_shape=[jax.ShapeDtypeStruct((rows + 32, cols), bf16)] * scale.shape[0],
        compiler_params=pltpu.CompilerParams(vmem_limit_bytes=vmem),
        name="mixed",
    )(scale, *dsums, *sums)


def chip_shift(x, hop):
    size = lax.axis_size("gy")
    return lax.ppermute(x, "gy", [(i, (i + 2 * hop) % size) for i in range(size)])


def swapped(x):
    return lax.ppermute(x, "gy", [(i, i ^ 1) for i in range(lax.axis_size("gy"))])


def body(
    xi_coarse,
    xi_middle,
    xi_fine,
    coef_middle,
    coef_fine,
    kern_u,
    kern_v,
    vis_data,
    facet_tiles,
    facet_weight,
    facet_count,
):
    side = xi_fine.shape[0]
    halos = halo(xi_coarse, xi_middle, coef_middle)
    sky, squares = sky_of(halos, coef_middle, xi_middle, coef_fine, xi_fine)
    lists, weights, counts = facet_tiles[0], facet_weight[0], facet_count[0]
    number = lists.shape[0]
    size = lax.axis_size("gy")
    chips = size // 2
    me = lax.axis_index("gy")
    ids = jnp.arange(size, dtype=jnp.int32)
    mixing = jnp.sum(
        weights[:, :, None] * (lists[:, :, None] == ids[None, None, :]).astype(f32), axis=1
    )
    order = 2 * ((me // 2 + jnp.arange(chips, dtype=jnp.int32)) % chips) + me % 2
    scale = jnp.concatenate([mixing, swapped(mixing)])[:, order].T
    mine = [sky] + [chip_shift(sky, hop) for hop in range(1, chips)]
    tiles = mine + [swapped(tile) for tile in mine]
    sel = (me // 2 - lists // 2) % chips + jnp.where(lists % 2 == me % 2, 0, chips)
    dsums, theirs, sums = [], [], [squares]
    for f in range(number):
        dsum, lik = facet(f, tiles, kern_u, kern_v, vis_data, sel, weights, counts)
        dsums.append(dsum)
        theirs.append(swapped(dsum))
        sums.append(lik)
    parts = mixed(dsums + theirs, scale, sums)
    parts = [parts[0]] + [chip_shift(parts[hop], hop) for hop in range(1, chips)]
    grad_coarse, grad_middle, grad_fine, total = adjoint(
        parts, halos, coef_middle, xi_middle, coef_fine, xi_fine, xi_coarse
    )
    total = jnp.sum(total)[None]
    total += swapped(total)
    size = lax.axis_size("gx")
    hop = 1
    while hop < size:
        total += lax.ppermute(total, "gx", [(i, i ^ hop) for i in range(size)])
        hop *= 2
    cells = lax.axis_size("gx") * lax.axis_size("gy") * side * side
    return (grad_coarse, grad_middle, grad_fine, total[0] / cells)


def solution(mesh):
    placed = (
        P("gx", "gy"),
        P("gx", "gy"),
        P("gx", "gy"),
        P(None, None, "gx", "gy"),
        P(None, None, "gx", "gy"),
        P("gx", "gy", None, None),
        P("gx", "gy", None, None),
        P("gx", "gy", None, None),
        P("gx", "gy", None),
        P("gx", "gy", None),
        P("gx", "gy"),
    )
    return jax.shard_map(
        body,
        mesh=mesh,
        in_specs=placed,
        out_specs=(P("gx", "gy"), P("gx", "gy"), P("gx", "gy"), P()),
        check_vma=False,
    )
```

```python
import functools

import jax
import jax.numpy as jnp
from jax import lax
from jax.experimental import pallas as pl
from jax.experimental.pallas import tpu as pltpu
from jax.sharding import PartitionSpec as P

inv_noise = 0.125
vmem = 32 * 1024 * 1024
f32 = jnp.float32
bf16 = jnp.bfloat16


def halves(x):
    high = x.astype(bf16)
    return high, (x - high.astype(f32)).astype(bf16)


def interleaver(cols, transposed):
    shape = (2 * cols, 2 * cols)
    split = lax.broadcasted_iota(jnp.int32, shape, 1 if transposed else 0)
    whole = lax.broadcasted_iota(jnp.int32, shape, 0 if transposed else 1)
    place = jnp.where(split >= cols, 2 * (split - cols) + 1, 2 * split)
    return (place == whole).astype(f32).astype(bf16)


def folded(x):
    rows, cols = x.shape
    x = jnp.sum(x.reshape(rows // 8, 8, cols), axis=0)
    return sum(x[:, i : i + 128] for i in range(0, cols, 128))


def row_of(ref, i):
    return ref[i : i + 1, :]


def dot_t(x, y, dims):
    return lax.dot_general(x, y, (dims, ((), ())), preferred_element_type=f32)


def moved(x, perm):
    high, low = halves(x)
    return jnp.dot(high, perm, preferred_element_type=f32) + jnp.dot(
        low, perm, preferred_element_type=f32
    )


def ends_placed(first, last, cols):
    rows = jnp.concatenate([first, first, last, last, jnp.zeros((4, first.shape[1]), f32)])
    high = rows.astype(bf16).astype(f32)
    index = lax.broadcasted_iota(jnp.int32, rows.shape, 0)
    rows = jnp.where(index % 2 == 0, high, rows - high).astype(bf16)
    shape = (8, cols)
    index = lax.broadcasted_iota(jnp.int32, shape, 0)
    lane = lax.broadcasted_iota(jnp.int32, shape, 1)
    place = ((index < 2) & (lane == 0)) | ((index >= 2) & (index < 4) & (lane == cols - 1))
    return dot_t(rows, place.astype(f32).astype(bf16), ((0,), (0,)))


def weighed(win, coef_ref, perm, lhs, mix, rows, cols):
    def part(i, carry):
        r0 = pl.multiple_of(i * 16, 16)
        total = [jnp.zeros((16, cols), f32) for _ in range(4)]
        for near in range(9):
            w = win[near, pl.ds(r0, 16), :]
            for child in range(4):
                total[child] += coef_ref[child, near, pl.ds(r0, 16), :].astype(f32) * w
        for child in range(4):
            a, b = child // 2, child % 2
            high, low = halves(total[child])
            lhs[pl.ds(2 * a * rows + r0, 16), b * cols : (b + 1) * cols] = high
            lhs[pl.ds((2 * a + 1) * rows + r0, 16), b * cols : (b + 1) * cols] = low
        return carry

    lax.fori_loop(0, rows // 16, part, 0)
    field = jnp.dot(lhs[...], perm[...], preferred_element_type=f32)
    for tile in range(2 * cols // 128):
        lanes = slice(tile * 128, (tile + 1) * 128)
        for a in range(2):
            mix[tile, pl.ds(a, rows, stride=2), :] = (
                field[2 * a * rows : (2 * a + 1) * rows, lanes]
                + field[(2 * a + 1) * rows : (2 * a + 2) * rows, lanes]
            )


def fetched(pairs, sems):
    copies = [pltpu.make_async_copy(src, dst, sems.at[i]) for i, (src, dst) in enumerate(pairs)]
    for copy in copies:
        copy.start()
    return copies


def columns_beside(field, left, right):
    rows, cols = field.shape[1:]
    placed = ends_placed(left, right, cols)
    lane = lax.broadcasted_iota(jnp.int32, (rows, cols), 1)
    here = field[1]
    field[0] = jnp.where(lane == 0, placed, pltpu.roll(here, 1, 1))
    field[2] = jnp.where(lane == cols - 1, placed, pltpu.roll(here, cols - 1, 1))


def sky_kernel(*refs):
    sources, (sky_ref, sq_ref), held, rest = refs[:11], refs[11:13], refs[13:24], refs[24:]
    win, perm, lhs, mix, near_coarse, shifted, fine_win, fine_perm, fine_lhs, fine_mix, sems = rest
    copies = fetched(zip(sources, held), sems)
    xi_coarse, above, below, lefts, rights, to_left, to_right = held[:7]
    coef_middle, xi_middle, coef_fine, xi_fine = held[7:]
    rows, cols = win.shape[1:]
    perm[...] = interleaver(cols, False)
    fine_perm[...] = interleaver(2 * cols, False)
    near_coarse[...] = jnp.zeros_like(near_coarse)
    for copy in copies[:8]:
        copy.wait()
    near_coarse[1, 6:8] = above[18:20]
    near_coarse[1, 8 : 8 + rows] = xi_coarse[...]
    near_coarse[1, 8 + rows : 10 + rows] = below[18:20]
    pad = jnp.zeros((1, 6), f32)
    beside = [
        jnp.concatenate([pad, row_of(x, i)[:, : rows + 4], pad], axis=1)
        for x, i in ((lefts, 19), (rights, 18))
    ]
    columns_beside(near_coarse, *beside)
    for near in range(9):
        r, c = near // 3, near % 3
        win[near] = near_coarse[c, 7 + r : 7 + r + rows]
    weighed(win, coef_middle, perm, lhs, mix, rows, cols)

    def across(message, top):
        out = []
        for b in range(2):
            line = row_of(message, 20 + b)
            for near in range(9):
                r, c = near // 3, near % 3
                line += row_of(message, 9 * b + near) * near_coarse[c, top + r : top + r + 1]
            out.append(line)
        return jnp.concatenate(out, axis=1)

    def along(message, fields):
        out = []
        for a in range(2):
            line = row_of(message, 20 + a)[:, 1 : rows + 3]
            for near in range(9):
                r, c = near // 3, near % 3
                line += row_of(message, 9 * a + near)[:, 1 : rows + 3] * fields[c][:, r : r + rows + 2]
            out.append(line)
        inner = jnp.concatenate([line[:, 1 : rows + 1] for line in out], axis=1)
        return inner, out[1][:, :1], out[0][:, rows + 1 :]

    top, bottom = across(above, 6), across(below, rows + 7)
    left, top_left, bottom_left = along(
        lefts, [row_of(lefts, 18), row_of(lefts, 19), row_of(to_left, 18)]
    )
    right, top_right, bottom_right = along(
        rights, [row_of(to_right, 19), row_of(rights, 18), row_of(rights, 19)]
    )
    lines = jnp.concatenate([top, bottom, left, right, jnp.zeros((4, 2 * cols), f32)])
    lines = moved(lines, perm[...])
    copies[8].wait()
    xi = xi_middle[...]
    last = 8 + 2 * rows
    shifted[1] = jnp.zeros(shifted.shape[1:], f32)
    for tile in range(2 * cols // 128):
        lanes = slice(tile * 128, (tile + 1) * 128)
        shifted[1, 8:last, lanes] = mix[tile] + xi[:, lanes]
    shifted[1, 7:8, :] = lines[0:1]
    shifted[1, last : last + 1, :] = lines[1:2]
    pad = jnp.zeros((1, 7), f32)
    beside = [
        jnp.concatenate([pad, first, line, final, pad], axis=1)
        for first, line, final in (
            (top_left, lines[2:3], bottom_left),
            (top_right, lines[3:4], bottom_right),
        )
    ]
    columns_beside(shifted, *beside)
    for near in range(9):
        r, c = near // 3, near % 3
        fine_win[near] = shifted[c, 7 + r : 7 + r + 2 * rows, :]
    copies[9].wait()
    weighed(fine_win, coef_fine, fine_perm, fine_lhs, fine_mix, 2 * rows, 2 * cols)
    copies[10].wait()
    for tile in range(4 * cols // 128):
        lanes = slice(tile * 128, (tile + 1) * 128)
        sky_ref[:, lanes] = (fine_mix[tile] + xi_fine[:, lanes]).astype(bf16)
    sq_ref[...] = (
        folded(win[4] * win[4]) + folded(xi * xi) + folded(xi_fine[...] * xi_fine[...])
    )


def sides_kernel(above, below, left_side, right_side, to_left, to_right):
    rows, cols = left_side.shape[1], above.shape[1]
    for out, side, b, col, first in (
        (to_left, left_side, 0, 0, 0),
        (to_right, right_side, 1, cols - 1, cols - 2),
    ):
        out[...] = jnp.zeros_like(out)
        out[:, 2 : rows + 2] = side[...]
        out[9:18, 1:2] = above[9 * b : 9 * b + 9, col : col + 1]
        out[21:22, 1:2] = above[20 + b : 21 + b, col : col + 1]
        out[0:9, rows + 2 : rows + 3] = below[9 * b : 9 * b + 9, col : col + 1]
        out[20:21, rows + 2 : rows + 3] = below[20 + b : 21 + b, col : col + 1]
        for k in range(2):
            at = slice(first + k, first + k + 1)
            for i in range(2):
                out[18 + k : 19 + k, i : i + 1] = above[18 + i : 19 + i, at]
                lane = rows + 2 + i
                out[18 + k : 19 + k, lane : lane + 1] = below[18 + i : 19 + i, at]


def neighbours(axis):
    size = lax.axis_size(axis)
    ahead = [(i, i + 1) for i in range(size - 1)]
    return ahead, [(j, i) for i, j in ahead]


def halo(xi_coarse, xi_middle, coef_middle, extra):
    rows, cols = xi_coarse.shape
    down, up = neighbours("gx")
    right, left = neighbours("gy")

    def edge(a, row, near):
        return jnp.concatenate(
            [
                coef_middle[2 * a : 2 * a + 2, :, row].reshape(18, cols).astype(f32),
                near,
                xi_middle[2 * row + a].reshape(cols, 2).T,
            ]
        )

    above = lax.ppermute(edge(1, rows - 1, xi_coarse[-2:]), "gx", down)
    below = lax.ppermute(edge(0, 0, xi_coarse[:2]), "gx", up)

    def inside(b, col, near):
        return jnp.concatenate(
            [
                coef_middle[b::2, :, :, col].reshape(18, rows).astype(f32),
                near.T,
                xi_middle[:, 2 * col + b].reshape(rows, 2).T,
            ]
        )

    sides = inside(0, 0, xi_coarse[:, :2]), inside(1, cols - 1, xi_coarse[:, -2:])
    sides, extra = lax.optimization_barrier((sides, extra))

    to_left, to_right = pl.pallas_call(
        sides_kernel,
        in_specs=[whole] * 4,
        out_specs=[whole] * 2,
        out_shape=[jax.ShapeDtypeStruct((22, rows + 4), f32)] * 2,
        name="sides",
    )(above, below, *sides)
    lefts = lax.ppermute(to_right, "gy", right)
    rights = lax.ppermute(to_left, "gy", left)
    return (above, below, lefts, rights, to_left, to_right), extra


whole = pl.BlockSpec(memory_space=pltpu.VMEM)
scalar = pl.BlockSpec(memory_space=pltpu.SMEM)
anywhere = pl.BlockSpec(memory_space=pl.ANY)


def sky_of(halos, xi_coarse, coef_middle, xi_middle, coef_fine, xi_fine):
    rows, cols = coef_middle.shape[2:]
    operands = (xi_coarse, *halos, coef_middle, xi_middle, coef_fine, xi_fine)
    return pl.pallas_call(
        sky_kernel,
        in_specs=[anywhere] * 11,
        out_specs=[whole] * 2,
        out_shape=[
            jax.ShapeDtypeStruct((4 * rows, 4 * cols), bf16),
            jax.ShapeDtypeStruct((8, 128), f32),
        ],
        scratch_shapes=[pltpu.VMEM(x.shape, x.dtype) for x in operands]
        + [
            pltpu.VMEM((9, rows, cols), f32),
            pltpu.VMEM((2 * cols, 2 * cols), bf16),
            pltpu.VMEM((4 * rows, 2 * cols), bf16),
            pltpu.VMEM((2 * cols // 128, 2 * rows, 128), f32),
            pltpu.VMEM((3, rows + 16, cols), f32),
            pltpu.VMEM((3, 2 * rows + 16, 2 * cols), f32),
            pltpu.VMEM((9, 2 * rows, 2 * cols), f32),
            pltpu.VMEM((4 * cols, 4 * cols), bf16),
            pltpu.VMEM((8 * rows, 4 * cols), bf16),
            pltpu.VMEM((4 * cols // 128, 4 * rows, 128), f32),
            pltpu.SemaphoreType.DMA((11,)),
        ],
        compiler_params=pltpu.CompilerParams(vmem_limit_bytes=vmem),
        name="sky",
    )(*operands)


def spread(mix, coef_ref, terms, rows, cols):
    def part(i, carry):
        r0 = pl.multiple_of(i * 16, 16)
        quads = []
        for a in range(2):
            for b in range(2):
                tiles = range(b * cols // 128, (b + 1) * cols // 128)
                lines = [mix[t, pl.ds(2 * r0 + a, 16, stride=2), :] for t in tiles]
                quads.append(jnp.concatenate(lines, axis=1))
        for near in range(9):
            total = jnp.zeros((16, cols), f32)
            for child in range(4):
                total += coef_ref[child, near, pl.ds(r0, 16), :].astype(f32) * quads[child]
            terms[near, pl.ds(r0, 16), :] = total
        return carry

    lax.fori_loop(0, rows // 16, part, 0)


def joined(rowed, cols):
    lane = lax.broadcasted_iota(jnp.int32, rowed.shape[1:], 1)
    main = (
        rowed[1]
        + jnp.where(lane == 0, 0.0, pltpu.roll(rowed[2], 1, 1))
        + jnp.where(lane == cols - 1, 0.0, pltpu.roll(rowed[0], cols - 1, 1))
    )
    lane = lax.broadcasted_iota(jnp.int32, (8, cols), 1)
    outside = []
    for c, col in ((0, 0), (2, cols - 1)):
        pick = (lane == col).astype(f32).astype(bf16)
        high, low = halves(rowed[c])
        out = dot_t(pick, high, ((1,), (1,))) + dot_t(pick, low, ((1,), (1,)))
        outside.append(out[:1])
    return main, outside[0], outside[1]


def adjoint_kernel(number, *refs):
    parts, sources, outs = refs[:number], refs[number : number + 9], refs[number + 9 : number + 17]
    held, rest = refs[number + 17 : number + 26], refs[number + 26 :]
    grad_ref, middle_ref, coarse_ref, left_ref, right_ref, upper_ref, lower_ref, total_ref = outs
    fine_perm, fine_mix, fine_terms, fine_rowed, perm, mix, terms, rowed, sems = rest
    copies = fetched(zip(sources, held), sems)
    xi_fine, coef_fine, coef_middle, above, below, lefts, rights, xi_middle, xi_coarse = held
    rows, cols = terms.shape[1:]
    fine_perm[...] = interleaver(2 * cols, True)
    perm[...] = interleaver(cols, True)
    g = parts[0][: 4 * rows].astype(f32)
    for part in parts[1:]:
        g += part[: 4 * rows].astype(f32)
    copies[0].wait()
    grad_ref[...] = g + xi_fine[...]
    tail = sum(part[4 * rows :, :128].astype(f32) for part in parts)
    total_ref[...] = tail[:8] + tail[8:16] + tail[16:24]
    split = moved(g, fine_perm[...])
    for tile in range(4 * cols // 128):
        fine_mix[tile] = split[:, tile * 128 : (tile + 1) * 128]
    copies[1].wait()
    spread(fine_mix, coef_fine, fine_terms, 2 * rows, 2 * cols)
    fine_rowed[...] = jnp.zeros_like(fine_rowed)
    for near in range(9):
        r, c = near // 3, near % 3
        fine_rowed[c, 7 + r : 7 + r + 2 * rows, :] += fine_terms[near]
    main, left, right = joined(fine_rowed, 2 * cols)
    last = 8 + 2 * rows
    inner = main[8:last]
    for copy in copies[2:]:
        copy.wait()
    middle_ref[...] = inner + xi_middle[...]
    split = moved(inner, perm[...])
    for tile in range(2 * cols // 128):
        mix[tile] = split[:, tile * 128 : (tile + 1) * 128]
    spread(mix, coef_middle, terms, rows, cols)
    ring_above, ring_below = main[7:8], main[last : last + 1]
    lines = [ring_above, ring_below, left[:, 8:last], right[:, 8:last]]
    lines = moved(jnp.concatenate(lines + [jnp.zeros((4, 2 * cols), f32)]), perm[...])
    rowed[...] = jnp.zeros_like(rowed)
    for near in range(9):
        r, c = near // 3, near % 3
        rowed[c, 7 + r : 7 + r + rows, :] += terms[near]
    for line, message, top in ((0, above, 6), (1, below, 7 + rows)):
        for near in range(9):
            r, c = near // 3, near % 3
            term = row_of(message, near) * lines[line : line + 1, :cols]
            term += row_of(message, 9 + near) * lines[line : line + 1, cols:]
            rowed[c, top + r : top + r + 1, :] += term

    def along(line, ends, message):
        empty = jnp.zeros((1, 1), f32)
        first = [empty, lines[line : line + 1, :rows], ends[:, last : last + 1]]
        second = [ends[:, 7:8], lines[line : line + 1, cols : cols + rows], empty]
        first, second = jnp.concatenate(first, axis=1), jnp.concatenate(second, axis=1)
        out = []
        for c in range(3):
            total = jnp.zeros((1, rows + 4), f32)
            for r in range(3):
                near = 3 * r + c
                term = row_of(message, near)[:, 1 : rows + 3] * first
                term += row_of(message, 9 + near)[:, 1 : rows + 3] * second
                pads = [jnp.zeros((1, n), f32) for n in (r, 2 - r) if n]
                pieces = [term] + pads if r == 0 else pads[:1] + [term] + pads[1:]
                total += jnp.concatenate(pieces, axis=1)
            out.append(total)
        return out

    outer_left = along(2, left, lefts)
    outer_right = along(3, right, rights)
    main, near_left, near_right = joined(rowed, cols)
    coarse_ref[...] = (
        main[8 : 8 + rows]
        + xi_coarse[...]
        + ends_placed(outer_left[2][:, 2 : rows + 2], outer_right[0][:, 2 : rows + 2], cols)
    )
    lane = lax.broadcasted_iota(jnp.int32, (1, cols), 1)
    for ref, first, line in ((upper_ref, 6, ring_above), (lower_ref, 8 + rows, ring_below)):
        ref[...] = jnp.zeros_like(ref)
        for i in range(2):
            at = first - 6 + i
            ref[i : i + 1, :cols] = (
                main[first + i : first + i + 1]
                + jnp.where(lane == 0, outer_left[2][:, at : at + 1], 0.0)
                + jnp.where(lane == cols - 1, outer_right[0][:, at : at + 1], 0.0)
            )
        ref[2:3, :] = line
    for ref, far, close, beyond, ends in (
        (left_ref, outer_left[0], outer_left[1], near_left, left),
        (right_ref, outer_right[2], outer_right[1], near_right, right),
    ):
        ref[...] = jnp.zeros_like(ref)
        ref[0:1, : rows + 4] = far
        ref[1:2, : rows + 4] = close + beyond[:, 6 : rows + 10]
        ref[2:3, : 2 * rows + 2] = ends[:, 7 : 2 * rows + 9]


def corners_kernel(upper, lower, from_left, from_right, total, other, upper_out, lower_out, total_out):
    rows, cols = lower.shape[1] // 2, lower.shape[1] // 2
    for ref, out, at, end in ((upper, upper_out, 0, 0), (lower, lower_out, rows + 2, 2 * rows + 1)):
        out[...] = ref[...]
        for i in range(2):
            here = slice(at + i, at + i + 1)
            out[i : i + 1, 0:1] += from_left[1:2, here]
            out[i : i + 1, 1:2] += from_left[0:1, here]
            out[i : i + 1, cols - 2 : cols - 1] += from_right[0:1, here]
            out[i : i + 1, cols - 1 : cols] += from_right[1:2, here]
        out[2:3, 0:1] += from_left[2:3, end : end + 1]
        out[2:3, 2 * cols - 1 :] += from_right[2:3, end : end + 1]
    total_out[...] = total[...] + other[...]


def final_kernel(
    cells,
    middle,
    coarse,
    from_left,
    from_right,
    from_above,
    from_below,
    total,
    other,
    middle_out,
    coarse_out,
    total_out,
):
    rows, cols = coarse.shape
    middle_out[...] = middle[...] + ends_placed(
        from_left[2:3, 1 : 2 * rows + 1], from_right[2:3, 1 : 2 * rows + 1], 2 * cols
    )
    middle_out[:1] += from_above[2:3]
    middle_out[2 * rows - 1 :] += from_below[2:3]
    inner = slice(2, rows + 2)
    outer = ends_placed(from_left[1:2, inner], from_right[1:2, inner], cols)
    second = ends_placed(from_left[0:1, inner], from_right[0:1, inner], cols)
    lane = lax.broadcasted_iota(jnp.int32, second.shape, 1)
    second = jnp.where(lane == 1, pltpu.roll(second, 1, 1), 0.0) + jnp.where(
        lane == cols - 2, pltpu.roll(second, cols - 1, 1), 0.0
    )
    coarse_out[...] = coarse[...] + outer + second
    coarse_out[:2] += from_above[0:2, :cols]
    coarse_out[rows - 2 :] += from_below[0:2, :cols]
    both = total[...] + other[...]
    both = jnp.sum(jnp.sum(both, axis=1, keepdims=True), axis=0, keepdims=True)
    total_out[...] = both * (1.0 / cells)


def adjoint(parts, halos, coef_middle, xi_middle, coef_fine, xi_fine, xi_coarse):
    rows, cols = coef_middle.shape[2:]
    above, below, lefts, rights, _, _ = halos
    shape = lambda *dims: jax.ShapeDtypeStruct(dims, f32)
    long = 2 * rows + 128
    operands = (
        xi_fine,
        coef_fine,
        coef_middle,
        above,
        below,
        lefts,
        rights,
        xi_middle,
        xi_coarse,
    )
    grad_fine, middle, coarse, to_left, to_right, upper, lower, total = pl.pallas_call(
        functools.partial(adjoint_kernel, len(parts)),
        in_specs=[whole] * len(parts) + [anywhere] * 9,
        out_specs=[whole] * 8,
        out_shape=[
            shape(4 * rows, 4 * cols),
            shape(2 * rows, 2 * cols),
            shape(rows, cols),
            shape(8, long),
            shape(8, long),
            shape(8, 2 * cols),
            shape(8, 2 * cols),
            shape(8, 128),
        ],
        scratch_shapes=[pltpu.VMEM(x.shape, x.dtype) for x in operands]
        + [
            pltpu.VMEM((4 * cols, 4 * cols), bf16),
            pltpu.VMEM((4 * cols // 128, 4 * rows, 128), f32),
            pltpu.VMEM((9, 2 * rows, 2 * cols), f32),
            pltpu.VMEM((3, 2 * rows + 128, 2 * cols), f32),
            pltpu.VMEM((2 * cols, 2 * cols), bf16),
            pltpu.VMEM((2 * cols // 128, 2 * rows, 128), f32),
            pltpu.VMEM((9, rows, cols), f32),
            pltpu.VMEM((3, rows + 128, cols), f32),
            pltpu.SemaphoreType.DMA((9,)),
        ],
        compiler_params=pltpu.CompilerParams(vmem_limit_bytes=vmem),
        name="adjoint",
    )(*parts, *operands)
    right, left = neighbours("gy")
    down, up = neighbours("gx")
    from_left = lax.ppermute(to_right, "gy", right)
    from_right = lax.ppermute(to_left, "gy", left)

    size = lax.axis_size("gx")
    hops = [1 << i for i in range(size.bit_length()) if 1 << i < size]

    def across(x, hop):
        return lax.ppermute(x, "gx", [(i, i ^ hop) for i in range(size)])

    other = across(total, hops[0])
    upper, lower, total = pl.pallas_call(
        corners_kernel,
        in_specs=[whole] * 6,
        out_specs=[whole] * 3,
        out_shape=[shape(8, 2 * cols), shape(8, 2 * cols), shape(8, 128)],
        name="corners",
    )(upper, lower, from_left, from_right, total, other)
    from_below = lax.ppermute(upper, "gx", up)
    from_above = lax.ppermute(lower, "gx", down)
    for hop in hops[1:-1]:
        total += across(total, hop)
    other = across(total, hops[-1])
    cells = size * lax.axis_size("gy") * 16 * rows * cols
    grad_middle, grad_coarse, total = pl.pallas_call(
        functools.partial(final_kernel, cells),
        in_specs=[whole] * 8,
        out_specs=[whole] * 3,
        out_shape=[shape(2 * rows, 2 * cols), shape(rows, cols), shape(1, 1)],
        compiler_params=pltpu.CompilerParams(vmem_limit_bytes=vmem),
        name="final",
    )(middle, coarse, from_left, from_right, from_above, from_below, total, other)
    return grad_coarse, grad_middle, grad_fine, total.reshape(())


def in_three(x):
    high = x.astype(bf16).astype(f32)
    middle = (x - high).astype(bf16).astype(f32)
    return jnp.concatenate([high, middle, x - high - middle, jnp.zeros_like(x)]).astype(bf16)


def from_three(x):
    x = x.astype(f32)
    return x[:8] + x[8:16] + x[16:24]


def facets_kernel(blk, ints, weights, *refs):
    number, slots = weights.shape
    tiles, rest = refs[:-14], refs[-14:]
    ku_hbm, kv_hbm, data_hbm, squares, out_ref = rest[:5]
    held, ku, kv, data, sums, dsum, total, sems, tile_sems = rest[5:]
    bins, side = ku.shape[1:]

    def inputs(f):
        for s in range(slots):
            for i, tile in enumerate(tiles):

                @pl.when(ints[f, s] == i)
                def _():
                    pltpu.make_async_copy(tile, held.at[f, s], tile_sems.at[f, s]).start()

        pairs = ((ku_hbm, ku), (kv_hbm, kv), (data_hbm, data))
        copies = [
            pltpu.make_async_copy(src.at[0, f], dst.at[f], sems.at[f, i])
            for i, (src, dst) in enumerate(pairs)
        ]
        for copy in copies:
            copy.start()
        return copies

    def work(f, step):
        rows = slice(step * blk, (step + 1) * blk)
        count = ints[f, slots] - step * blk

        @pl.when(count > 0)
        def _():
            amp = jnp.dot(ku[f, rows], sums[...], preferred_element_type=f32).astype(bf16)
            vis = dot_t(amp, kv[f], ((1,), (1,)))
            live = lax.broadcasted_iota(jnp.int32, vis.shape, 0) < count
            resid = jnp.where(live, vis - data[f, rows].astype(f32), 0.0)
            total[...] += 0.5 * inv_noise * folded(resid * resid)
            dvis = (inv_noise * resid).astype(bf16)
            damp = jnp.dot(dvis, kv[f], preferred_element_type=f32).astype(bf16)
            part = dot_t(ku[f, rows], damp, ((0,), (0,)))
            if step == 0:
                dsum[...] = part
            else:
                dsum[...] += part

    copies = [inputs(0)]
    total[...] = 0.5 * squares[...]
    for f in range(number):
        for s in range(slots):
            pltpu.make_async_copy(tiles[0], held.at[f, s], tile_sems.at[f, s]).wait()
        copies[f][0].wait()
        if f + 1 < number:
            copies.append(inputs(f + 1))
        mixture = weights[f, 0] * held[f, 0].astype(f32)
        for s in range(1, slots):
            mixture += weights[f, s] * held[f, s].astype(f32)
        sums[...] = mixture.astype(bf16)
        copies[f][1].wait()
        copies[f][2].wait()
        for step in range(bins // blk):
            work(f, step)
        out_ref[f * side : (f + 1) * side] = dsum[...].astype(bf16)
    out_ref[number * side :] = jnp.zeros((32, side), bf16)
    out_ref[number * side :, :128] = in_three(total[...])


def facets(tiles, ku, kv, data, ints, weights, squares):
    number, bins, side = ku.shape[1:]
    slots = weights.shape[1]
    return pl.pallas_call(
        functools.partial(facets_kernel, 512),
        in_specs=[scalar] * 2 + [anywhere] * (len(tiles) + 3) + [whole],
        out_specs=whole,
        out_shape=jax.ShapeDtypeStruct((number * side + 32, side), bf16),
        scratch_shapes=[
            pltpu.VMEM((number, slots, side, side), bf16),
            pltpu.VMEM((number, bins, side), bf16),
            pltpu.VMEM((number, bins, side), bf16),
            pltpu.VMEM((number, bins, bins), bf16),
            pltpu.VMEM((side, side), bf16),
            pltpu.VMEM((side, side), f32),
            pltpu.VMEM((8, 128), f32),
            pltpu.SemaphoreType.DMA((number, 3)),
            pltpu.SemaphoreType.DMA((number, slots)),
        ],
        compiler_params=pltpu.CompilerParams(vmem_limit_bytes=vmem),
        name="facets",
    )(ints, weights, *tiles, ku, kv, data, squares)


def mix_kernel(scale, mine, theirs, *outs):
    side = outs[0].shape[1]
    number = mine.shape[0] // side
    total = in_three(from_three(mine[number * side :, :128]) + from_three(theirs[number * side :, :128]))
    for d, out in enumerate(outs):
        value = None
        for f in range(2 * number):
            ref, at = (mine, f) if f < number else (theirs, f - number)
            term = scale[d, f] * ref[at * side : (at + 1) * side].astype(f32)
            value = term if value is None else value + term
        out[:side] = value.astype(bf16)
        out[side:] = jnp.zeros((32, side), bf16)
        out[side:, :128] = total


def mixed(mine, theirs, scale):
    side = mine.shape[1]
    return pl.pallas_call(
        mix_kernel,
        in_specs=[scalar, whole, whole],
        out_specs=[whole] * scale.shape[0],
        out_shape=[jax.ShapeDtypeStruct((side + 32, side), bf16)] * scale.shape[0],
        compiler_params=pltpu.CompilerParams(vmem_limit_bytes=vmem),
        name="mixed",
    )(scale, mine, theirs)


def chip_shift(x, hop):
    size = lax.axis_size("gy")
    return lax.ppermute(x, "gy", [(i, (i + 2 * hop) % size) for i in range(size)])


def swapped(x):
    return lax.ppermute(x, "gy", [(i, i ^ 1) for i in range(lax.axis_size("gy"))])


def body(
    xi_coarse,
    xi_middle,
    xi_fine,
    coef_middle,
    coef_fine,
    kern_u,
    kern_v,
    vis_data,
    facet_tiles,
    facet_weight,
    facet_count,
):
    lists, weights, counts = facet_tiles[0], facet_weight[0], facet_count[0]
    size = lax.axis_size("gy")
    chips = size // 2
    me = lax.axis_index("gy")
    ids = jnp.arange(size, dtype=jnp.int32)
    mixing = jnp.sum(
        weights[:, :, None] * (lists[:, :, None] == ids[None, None, :]).astype(f32), axis=1
    )
    order = 2 * ((me // 2 + jnp.arange(chips, dtype=jnp.int32)) % chips) + me % 2
    scale = jnp.concatenate([mixing, swapped(mixing)])[:, order].T
    sel = (me // 2 - lists // 2) % chips + jnp.where(lists % 2 == me % 2, 0, chips)
    ints = jnp.concatenate([sel, counts[:, None]], axis=1)
    halos, (scale, ints, weights) = halo(
        xi_coarse, xi_middle, coef_middle, (scale, ints, weights)
    )
    sky, squares = sky_of(halos, xi_coarse, coef_middle, xi_middle, coef_fine, xi_fine)
    mine = [sky] + [chip_shift(sky, hop) for hop in range(1, chips)]
    tiles = mine + [swapped(tile) for tile in mine]
    dsums = facets(tiles, kern_u, kern_v, vis_data, ints, weights, squares)
    parts = mixed(dsums, swapped(dsums), scale)
    parts = [parts[0]] + [chip_shift(parts[hop], hop) for hop in range(1, chips)]
    return adjoint(parts, halos, coef_middle, xi_middle, coef_fine, xi_fine, xi_coarse)


def solution(mesh):
    placed = (
        P("gx", "gy"),
        P("gx", "gy"),
        P("gx", "gy"),
        P(None, None, "gx", "gy"),
        P(None, None, "gx", "gy"),
        P("gx", "gy", None, None),
        P("gx", "gy", None, None),
        P("gx", "gy", None, None),
        P("gx", "gy", None),
        P("gx", "gy", None),
        P("gx", "gy"),
    )
    return jax.shard_map(
        body,
        mesh=mesh,
        in_specs=placed,
        out_specs=(P("gx", "gy"), P("gx", "gy"), P("gx", "gy"), P()),
        check_vma=False,
    )
```

```python
import functools

import jax
import jax.numpy as jnp
from jax import lax
from jax.experimental import pallas as pl
from jax.experimental.pallas import tpu as pltpu
from jax.sharding import PartitionSpec as P

inv_noise = 0.125
long_work = pl.CostEstimate(flops=40_000_000_000, transcendentals=0, bytes_accessed=64_000_000)
border = 8
vmem = 32 * 1024 * 1024
f32 = jnp.float32
bf16 = jnp.bfloat16


def halves(x):
    high = x.astype(bf16)
    return high, (x - high.astype(f32)).astype(bf16)


def interleaver(cols, transposed):
    shape = (2 * cols, 2 * cols)
    split = lax.broadcasted_iota(jnp.int32, shape, 1 if transposed else 0)
    whole = lax.broadcasted_iota(jnp.int32, shape, 0 if transposed else 1)
    place = jnp.where(split >= cols, 2 * (split - cols) + 1, 2 * split)
    return (place == whole).astype(f32).astype(bf16)


def folded(x):
    rows, cols = x.shape
    x = jnp.sum(x.reshape(rows // 8, 8, cols), axis=0)
    return sum(x[:, i : i + 128] for i in range(0, cols, 128))


def row_of(ref, i):
    return ref[i : i + 1, :]


def dot_t(x, y, dims):
    return lax.dot_general(x, y, (dims, ((), ())), preferred_element_type=f32)


def moved(x, perm):
    high, low = halves(x)
    return jnp.dot(high, perm, preferred_element_type=f32) + jnp.dot(
        low, perm, preferred_element_type=f32
    )


def ends_placed(first, last, cols):
    rows = jnp.concatenate([first, first, last, last, jnp.zeros((4, first.shape[1]), f32)])
    high = rows.astype(bf16).astype(f32)
    index = lax.broadcasted_iota(jnp.int32, rows.shape, 0)
    rows = jnp.where(index % 2 == 0, high, rows - high).astype(bf16)
    shape = (8, cols)
    index = lax.broadcasted_iota(jnp.int32, shape, 0)
    lane = lax.broadcasted_iota(jnp.int32, shape, 1)
    place = ((index < 2) & (lane == 0)) | ((index >= 2) & (index < 4) & (lane == cols - 1))
    return dot_t(rows, place.astype(f32).astype(bf16), ((0,), (0,)))


def weighed(win, coef_ref, perm, lhs, mix, rows, cols):
    def part(i, carry):
        r0 = pl.multiple_of(i * 16, 16)
        total = [jnp.zeros((16, cols), f32) for _ in range(4)]
        for near in range(9):
            w = win[near, pl.ds(r0, 16), :]
            for child in range(4):
                total[child] += coef_ref[child, near, pl.ds(r0, 16), :].astype(f32) * w
        for child in range(4):
            a, b = child // 2, child % 2
            high, low = halves(total[child])
            lhs[pl.ds(2 * a * rows + r0, 16), b * cols : (b + 1) * cols] = high
            lhs[pl.ds((2 * a + 1) * rows + r0, 16), b * cols : (b + 1) * cols] = low
        return carry

    lax.fori_loop(0, rows // 16, part, 0)
    field = jnp.dot(lhs[...], perm[...], preferred_element_type=f32)
    for tile in range(2 * cols // 128):
        lanes = slice(tile * 128, (tile + 1) * 128)
        for a in range(2):
            mix[tile, pl.ds(a, rows, stride=2), :] = (
                field[2 * a * rows : (2 * a + 1) * rows, lanes]
                + field[(2 * a + 1) * rows : (2 * a + 2) * rows, lanes]
            )


def fetched(pairs, sems):
    copies = [pltpu.make_async_copy(src, dst, sems.at[i]) for i, (src, dst) in enumerate(pairs)]
    for copy in copies:
        copy.start()
    return copies


def columns_beside(field, left, right):
    rows, cols = field.shape[1:]
    placed = ends_placed(left, right, cols)
    lane = lax.broadcasted_iota(jnp.int32, (rows, cols), 1)
    here = field[1]
    field[0] = jnp.where(lane == 0, placed, pltpu.roll(here, 1, 1))
    field[2] = jnp.where(lane == cols - 1, placed, pltpu.roll(here, cols - 1, 1))


def strips_of(tile, out):
    rows, cols = tile.shape
    first, last = tile[: 2 * border].astype(f32), tile[rows - 2 * border :].astype(f32)
    out[: 2 * border] = jnp.concatenate([first[:border], last[border:]]).astype(bf16)
    index = lax.broadcasted_iota(jnp.int32, (2 * border, cols), 0)
    lane = lax.broadcasted_iota(jnp.int32, (2 * border, cols), 1)
    pick = lane == jnp.where(index < border, index, index + cols - 2 * border)
    pick = pick.astype(f32).astype(bf16)
    out[2 * border : 4 * border] = dot_t(pick, tile[...], ((1,), (1,))).astype(bf16)


def columns_of(strip):
    index = lax.broadcasted_iota(jnp.int32, (2 * border, 128), 0)
    lane = lax.broadcasted_iota(jnp.int32, (2 * border, 128), 1)
    out = []
    for place in (
        (index < border) & (lane == index),
        (index >= border) & (lane == index + 128 - 2 * border),
    ):
        out.append(dot_t(strip, place.astype(f32).astype(bf16), ((0,), (0,))))
    return out


def stretch(out, side, over, under, b, lane, first):
    rows = side.shape[1]
    out[...] = jnp.zeros_like(out)
    out[:, 2 : rows + 2] = side[...]
    out[9:18, 1:2] = over[9 * b : 9 * b + 9, lane : lane + 1]
    out[21:22, 1:2] = over[20 + b : 21 + b, lane : lane + 1]
    out[0:9, rows + 2 : rows + 3] = under[9 * b : 9 * b + 9, lane : lane + 1]
    out[20:21, rows + 2 : rows + 3] = under[20 + b : 21 + b, lane : lane + 1]
    for k in range(2):
        at = slice(first + k, first + k + 1)
        for i in range(2):
            out[18 + k : 19 + k, i : i + 1] = over[18 + i : 19 + i, at]
            end = rows + 2 + i
            out[18 + k : 19 + k, end : end + 1] = under[18 + i : 19 + i, at]


def sky_kernel(alone, *refs):
    count = 5 if alone else 11
    sources, refs = refs[:count], refs[count:]
    outs, refs = (refs[:1], refs[1:]) if alone else (refs[:5], refs[5:])
    held, rest = refs[:11], refs[11:]
    win, perm, lhs, mix, near_coarse, shifted, fine_win, fine_perm, fine_lhs, fine_mix = rest[:10]
    lefts, rights, to_left, to_right, sems = rest[10:]
    sky_ref = outs[0]
    if alone:
        for ref in held[1:7]:
            ref[...] = jnp.zeros_like(ref)
        copies = fetched(zip(sources, (held[0],) + tuple(held[7:])), sems)
    else:
        copies = fetched(zip(sources, held), sems)
    xi_coarse, over, under, left_in, right_in, left_side, right_side = held[:7]
    coef_middle, xi_middle, coef_fine, xi_fine = held[7:]
    rows, cols = win.shape[1:]
    perm[...] = interleaver(cols, False)
    fine_perm[...] = interleaver(2 * cols, False)
    near_coarse[...] = jnp.zeros_like(near_coarse)
    for copy in copies[:-3]:
        copy.wait()
    above, below = over[:, 2 : cols + 2], under[:, 2 : cols + 2]
    stretch(lefts, left_in, over, under, 1, 1, 0)
    stretch(rights, right_in, over, under, 0, cols + 2, cols + 2)
    stretch(to_left, left_side, over, under, 0, 2, 2)
    stretch(to_right, right_side, over, under, 1, cols + 1, cols)
    near_coarse[1, 6:8] = above[18:20]
    near_coarse[1, 8 : 8 + rows] = xi_coarse[...]
    near_coarse[1, 8 + rows : 10 + rows] = below[18:20]
    pad = jnp.zeros((1, 6), f32)
    beside = [
        jnp.concatenate([pad, row_of(x, i)[:, : rows + 4], pad], axis=1)
        for x, i in ((lefts, 19), (rights, 18))
    ]
    columns_beside(near_coarse, *beside)
    for near in range(9):
        r, c = near // 3, near % 3
        win[near] = near_coarse[c, 7 + r : 7 + r + rows]
    weighed(win, coef_middle, perm, lhs, mix, rows, cols)

    def across(message, top):
        out = []
        for b in range(2):
            line = row_of(message, 20 + b)
            for near in range(9):
                r, c = near // 3, near % 3
                line += row_of(message, 9 * b + near) * near_coarse[c, top + r : top + r + 1]
            out.append(line)
        return jnp.concatenate(out, axis=1)

    def along(message, fields):
        out = []
        for a in range(2):
            line = row_of(message, 20 + a)[:, 1 : rows + 3]
            for near in range(9):
                r, c = near // 3, near % 3
                line += row_of(message, 9 * a + near)[:, 1 : rows + 3] * fields[c][:, r : r + rows + 2]
            out.append(line)
        inner = jnp.concatenate([line[:, 1 : rows + 1] for line in out], axis=1)
        return inner, out[1][:, :1], out[0][:, rows + 1 :]

    top, bottom = across(above, 6), across(below, rows + 7)
    left, top_left, bottom_left = along(
        lefts, [row_of(lefts, 18), row_of(lefts, 19), row_of(to_left, 18)]
    )
    right, top_right, bottom_right = along(
        rights, [row_of(to_right, 19), row_of(rights, 18), row_of(rights, 19)]
    )
    lines = jnp.concatenate([top, bottom, left, right, jnp.zeros((4, 2 * cols), f32)])
    lines = moved(lines, perm[...])
    copies[-3].wait()
    xi = xi_middle[...]
    last = 8 + 2 * rows
    shifted[1] = jnp.zeros(shifted.shape[1:], f32)
    for tile in range(2 * cols // 128):
        lanes = slice(tile * 128, (tile + 1) * 128)
        shifted[1, 8:last, lanes] = mix[tile] + xi[:, lanes]
    shifted[1, 7:8, :] = lines[0:1]
    shifted[1, last : last + 1, :] = lines[1:2]
    pad = jnp.zeros((1, 7), f32)
    beside = [
        jnp.concatenate([pad, first, line, final, pad], axis=1)
        for first, line, final in (
            (top_left, lines[2:3], bottom_left),
            (top_right, lines[3:4], bottom_right),
        )
    ]
    columns_beside(shifted, *beside)
    for near in range(9):
        r, c = near // 3, near % 3
        fine_win[near] = shifted[c, 7 + r : 7 + r + 2 * rows, :]
    copies[-2].wait()
    weighed(fine_win, coef_fine, fine_perm, fine_lhs, fine_mix, 2 * rows, 2 * cols)
    copies[-1].wait()
    for tile in range(4 * cols // 128):
        lanes = slice(tile * 128, (tile + 1) * 128)
        sky_ref[:, lanes] = (fine_mix[tile] + xi_fine[:, lanes]).astype(bf16)
    if alone:
        return
    strips_ref, sq_ref, lefts_ref, rights_ref = outs[1:]
    lefts_ref[...] = lefts[...]
    rights_ref[...] = rights[...]
    strips_of(sky_ref, strips_ref)
    sq_ref[...] = (
        folded(win[4] * win[4]) + folded(xi * xi) + folded(xi_fine[...] * xi_fine[...])
    )


def sides_kernel(left_in, right_in, first_side, last_side, to_above, to_below):
    rows = left_in.shape[1]
    stretch(to_above, first_side, left_in, right_in, 0, 0, 0)
    stretch(to_below, last_side, left_in, right_in, 1, rows - 1, rows - 2)


def neighbours(axis):
    size = lax.axis_size(axis)
    ahead = [(i, i + 1) for i in range(size - 1)]
    return ahead, [(j, i) for i, j in ahead]


def halo_sides(xi_coarse, xi_middle, coef_middle):
    rows, cols = xi_coarse.shape

    def inside(b, col, near):
        return jnp.concatenate(
            [
                coef_middle[b::2, :, :, col].reshape(18, rows).astype(f32),
                near.T,
                xi_middle[:, 2 * col + b].reshape(rows, 2).T,
            ]
        )

    return inside(0, 0, xi_coarse[:, :2]), inside(1, cols - 1, xi_coarse[:, -2:])


def halo_rows(xi_coarse, xi_middle, coef_middle, left_in, right_in):
    rows, cols = xi_coarse.shape

    def edge(a, row, near):
        return jnp.concatenate(
            [
                coef_middle[2 * a : 2 * a + 2, :, row].reshape(18, cols).astype(f32),
                near,
                xi_middle[2 * row + a].reshape(cols, 2).T,
            ]
        )

    to_above, to_below = pl.pallas_call(
        sides_kernel,
        in_specs=[whole] * 4,
        out_specs=[whole] * 2,
        out_shape=[jax.ShapeDtypeStruct((22, cols + 4), f32)] * 2,
        cost_estimate=long_work,
        name="sides",
    )(left_in, right_in, edge(0, 0, xi_coarse[:2]), edge(1, rows - 1, xi_coarse[-2:]))
    down, up = neighbours("gx")
    return lax.ppermute(to_below, "gx", down), lax.ppermute(to_above, "gx", up)


whole = pl.BlockSpec(memory_space=pltpu.VMEM)
scalar = pl.BlockSpec(memory_space=pltpu.SMEM)
anywhere = pl.BlockSpec(memory_space=pltpu.HBM)


def sky_of(halos, xi_coarse, coef_middle, xi_middle, coef_fine, xi_fine):
    rows, cols = coef_middle.shape[2:]
    alone = halos is None
    given = (coef_middle, xi_middle, coef_fine, xi_fine)
    operands = (xi_coarse, *given) if alone else (xi_coarse, *halos, *given)
    message = [(22, cols + 4)] * 2 + [(22, rows)] * 4
    return pl.pallas_call(
        functools.partial(sky_kernel, alone),
        in_specs=[anywhere] * len(operands),
        out_specs=[whole] * (1 if alone else 5),
        out_shape=[
            jax.ShapeDtypeStruct((4 * rows, 4 * cols), bf16),
            jax.ShapeDtypeStruct((4 * border, 4 * cols), bf16),
            jax.ShapeDtypeStruct((8, 128), f32),
            jax.ShapeDtypeStruct((22, rows + 4), f32),
            jax.ShapeDtypeStruct((22, rows + 4), f32),
        ][: 1 if alone else 5],
        scratch_shapes=[pltpu.VMEM(xi_coarse.shape, f32)]
        + [pltpu.VMEM(shape, f32) for shape in message]
        + [pltpu.VMEM(x.shape, x.dtype) for x in given]
        + [
            pltpu.VMEM((9, rows, cols), f32),
            pltpu.VMEM((2 * cols, 2 * cols), bf16),
            pltpu.VMEM((4 * rows, 2 * cols), bf16),
            pltpu.VMEM((2 * cols // 128, 2 * rows, 128), f32),
            pltpu.VMEM((3, rows + 16, cols), f32),
            pltpu.VMEM((3, 2 * rows + 16, 2 * cols), f32),
            pltpu.VMEM((9, 2 * rows, 2 * cols), f32),
            pltpu.VMEM((4 * cols, 4 * cols), bf16),
            pltpu.VMEM((8 * rows, 4 * cols), bf16),
            pltpu.VMEM((4 * cols // 128, 4 * rows, 128), f32),
            *[pltpu.VMEM((22, rows + 4), f32) for _ in range(4)],
            pltpu.SemaphoreType.DMA((11,)),
        ],
        compiler_params=pltpu.CompilerParams(vmem_limit_bytes=60 * 1024 * 1024),
        name="sky",
    )(*operands)


def spread(mix, coef_ref, terms, rows, cols):
    def part(i, carry):
        r0 = pl.multiple_of(i * 16, 16)
        quads = []
        for a in range(2):
            for b in range(2):
                tiles = range(b * cols // 128, (b + 1) * cols // 128)
                lines = [mix[t, pl.ds(2 * r0 + a, 16, stride=2), :] for t in tiles]
                quads.append(jnp.concatenate(lines, axis=1))
        for near in range(9):
            total = jnp.zeros((16, cols), f32)
            for child in range(4):
                total += coef_ref[child, near, pl.ds(r0, 16), :].astype(f32) * quads[child]
            terms[near, pl.ds(r0, 16), :] = total
        return carry

    lax.fori_loop(0, rows // 16, part, 0)


def joined(rowed, cols):
    lane = lax.broadcasted_iota(jnp.int32, rowed.shape[1:], 1)
    main = (
        rowed[1]
        + jnp.where(lane == 0, 0.0, pltpu.roll(rowed[2], 1, 1))
        + jnp.where(lane == cols - 1, 0.0, pltpu.roll(rowed[0], cols - 1, 1))
    )
    lane = lax.broadcasted_iota(jnp.int32, (8, cols), 1)
    outside = []
    for c, col in ((0, 0), (2, cols - 1)):
        pick = (lane == col).astype(f32).astype(bf16)
        high, low = halves(rowed[c])
        out = dot_t(pick, high, ((1,), (1,))) + dot_t(pick, low, ((1,), (1,)))
        outside.append(out[:1])
    return main, outside[0], outside[1]


def adjoint_kernel(edge, number, *refs):
    count = 6 if edge else 9
    parts, sources = refs[:number], refs[number : number + count]
    outs, refs = refs[number + count :][: 5 if edge else 3], refs[number + count :][5 if edge else 3 :]
    held, rest = refs[:count], refs[count:]
    fine_perm, fine_mix, fine_terms, fine_rowed, perm, mix, terms, rowed, full, sems, out_sem = rest
    copies = fetched(zip(sources, held), sems)
    coef_fine, coef_middle, over, under, lefts, rights = held[:6]
    if edge:
        left_ref, right_ref, upper_ref, lower_ref, total_ref = outs
    else:
        grad_ref, middle_ref, coarse_ref = outs
        xi_fine, xi_middle, xi_coarse = held[6:]
    rows, cols = terms.shape[1:]
    fine_perm[...] = interleaver(2 * cols, True)
    perm[...] = interleaver(cols, True)
    g = parts[0][...].astype(f32)
    for part in parts[1:]:
        g += part[...].astype(f32)
    if edge:
        tail = g[4 * border :, :128]
        total_ref[...] = tail[:8] + tail[8:16] + tail[16:24]
        high, low = halves(g[2 * border : 4 * border])
        left, right = [x + y for x, y in zip(columns_of(high), columns_of(low))]
        full[...] = jnp.zeros_like(full)
        full[:, :128] = left
        full[:, 4 * cols - 128 :] = right
        full[:border] = g[:border]
        full[4 * rows - border :] = g[border : 2 * border]
        g = full[...]
    else:
        copies[6].wait()
        full[...] = g + xi_fine[...]
        leaving = pltpu.make_async_copy(full, grad_ref, out_sem)
        leaving.start()
    split = moved(g, fine_perm[...])
    for tile in range(4 * cols // 128):
        fine_mix[tile] = split[:, tile * 128 : (tile + 1) * 128]
    copies[0].wait()
    spread(fine_mix, coef_fine, fine_terms, 2 * rows, 2 * cols)
    fine_rowed[...] = jnp.zeros_like(fine_rowed)
    for near in range(9):
        r, c = near // 3, near % 3
        fine_rowed[c, 7 + r : 7 + r + 2 * rows, :] += fine_terms[near]
    main, left, right = joined(fine_rowed, 2 * cols)
    last = 8 + 2 * rows
    inner = main[8:last]
    for copy in copies[1:6] + copies[7:]:
        copy.wait()
    above, below = over[:, 2 : cols + 2], under[:, 2 : cols + 2]
    if not edge:
        middle_ref[...] = inner + xi_middle[...]
    split = moved(inner, perm[...])
    for tile in range(2 * cols // 128):
        mix[tile] = split[:, tile * 128 : (tile + 1) * 128]
    spread(mix, coef_middle, terms, rows, cols)
    ring_above, ring_below = main[7:8], main[last : last + 1]
    lines = [ring_above, ring_below, left[:, 8:last], right[:, 8:last]]
    lines = moved(jnp.concatenate(lines + [jnp.zeros((4, 2 * cols), f32)]), perm[...])
    rowed[...] = jnp.zeros_like(rowed)
    for near in range(9):
        r, c = near // 3, near % 3
        rowed[c, 7 + r : 7 + r + rows, :] += terms[near]
    for line, message, top in ((0, above, 6), (1, below, 7 + rows)):
        for near in range(9):
            r, c = near // 3, near % 3
            term = row_of(message, near) * lines[line : line + 1, :cols]
            term += row_of(message, 9 + near) * lines[line : line + 1, cols:]
            rowed[c, top + r : top + r + 1, :] += term

    def along(line, ends, message):
        empty = jnp.zeros((1, 1), f32)
        first = [empty, lines[line : line + 1, :rows], ends[:, last : last + 1]]
        second = [ends[:, 7:8], lines[line : line + 1, cols : cols + rows], empty]
        first, second = jnp.concatenate(first, axis=1), jnp.concatenate(second, axis=1)
        out = []
        for c in range(3):
            total = jnp.zeros((1, rows + 4), f32)
            for r in range(3):
                near = 3 * r + c
                term = row_of(message, near)[:, 1 : rows + 3] * first
                term += row_of(message, 9 + near)[:, 1 : rows + 3] * second
                pads = [jnp.zeros((1, n), f32) for n in (r, 2 - r) if n]
                pieces = [term] + pads if r == 0 else pads[:1] + [term] + pads[1:]
                total += jnp.concatenate(pieces, axis=1)
            out.append(total)
        return out

    outer_left = along(2, left, lefts)
    outer_right = along(3, right, rights)
    main, near_left, near_right = joined(rowed, cols)
    if not edge:
        coarse_ref[...] = (
            main[8 : 8 + rows]
            + xi_coarse[...]
            + ends_placed(outer_left[2][:, 2 : rows + 2], outer_right[0][:, 2 : rows + 2], cols)
        )
        leaving.wait()
        return
    sides = []
    for ref, far, close, beyond, ends in (
        (left_ref, outer_left[0], outer_left[1], near_left, left),
        (right_ref, outer_right[2], outer_right[1], near_right, right),
    ):
        close += beyond[:, 6 : rows + 10]
        ends = ends[:, 7 : 2 * rows + 9]
        ref[...] = jnp.zeros_like(ref)
        ref[0:1, : rows + 4] = far
        ref[1:2, : rows + 4] = close
        ref[2:3, : 2 * rows + 2] = ends
        sides.append((far, close, ends))
    lane = lax.broadcasted_iota(jnp.int32, (1, cols), 1)
    (far_left, close_left, ends_left), (far_right, close_right, ends_right) = sides
    for ref, first, line, end in (
        (upper_ref, 6, ring_above, 0),
        (lower_ref, 8 + rows, ring_below, 2 * rows + 1),
    ):
        ref[...] = jnp.zeros_like(ref)
        for i in range(2):
            at = slice(first - 6 + i, first - 5 + i)
            inner = (
                main[first + i : first + i + 1]
                + jnp.where(lane == 0, outer_left[2][:, at], 0.0)
                + jnp.where(lane == cols - 1, outer_right[0][:, at], 0.0)
            )
            pieces = [far_left[:, at], close_left[:, at], inner, close_right[:, at], far_right[:, at]]
            ref[i : i + 1, : cols + 4] = jnp.concatenate(pieces, axis=1)
        pieces = [ends_left[:, end : end + 1], line, ends_right[:, end : end + 1]]
        ref[2:3, : 2 * cols + 2] = jnp.concatenate(pieces, axis=1)


def corners_kernel(rows, cols, left, right, from_above, from_below, total, other, left_out, right_out, total_out):
    for ref, out, far, close, end in (
        (left, left_out, 0, 1, 0),
        (right, right_out, cols + 3, cols + 2, 2 * cols + 1),
    ):
        out[...] = ref[...]
        for rows_in, first, line in ((from_above, 2, 1), (from_below, rows, 2 * rows)):
            for i in range(2):
                at = slice(first + i, first + i + 1)
                out[0:1, at] += rows_in[i : i + 1, far : far + 1]
                out[1:2, at] += rows_in[i : i + 1, close : close + 1]
            out[2:3, line : line + 1] += rows_in[2:3, end : end + 1]
    total_out[...] = total[...] + other[...]


def final_kernel(
    cells,
    middle,
    coarse,
    from_left,
    from_right,
    from_above,
    from_below,
    total,
    other,
    middle_out,
    coarse_out,
    total_out,
):
    rows, cols = coarse.shape
    middle_out[...] = middle[...] + ends_placed(
        from_left[2:3, 1 : 2 * rows + 1], from_right[2:3, 1 : 2 * rows + 1], 2 * cols
    )
    line = slice(1, 2 * cols + 1)
    middle_out[:1] += from_above[2:3, line]
    middle_out[2 * rows - 1 :] += from_below[2:3, line]
    inner = slice(2, rows + 2)
    outer = ends_placed(from_left[1:2, inner], from_right[1:2, inner], cols)
    second = ends_placed(from_left[0:1, inner], from_right[0:1, inner], cols)
    lane = lax.broadcasted_iota(jnp.int32, second.shape, 1)
    second = jnp.where(lane == 1, pltpu.roll(second, 1, 1), 0.0) + jnp.where(
        lane == cols - 2, pltpu.roll(second, cols - 1, 1), 0.0
    )
    coarse_out[...] = coarse[...] + outer + second
    line = slice(2, cols + 2)
    coarse_out[:2] += from_above[0:2, line]
    coarse_out[rows - 2 :] += from_below[0:2, line]
    both = total[...] + other[...]
    both = jnp.sum(jnp.sum(both, axis=1, keepdims=True), axis=0, keepdims=True)
    total_out[...] = both * (1.0 / cells)


def shape(*dims):
    return jax.ShapeDtypeStruct(dims, f32)


def adjoint(edge, parts, sides, fields):
    rows, cols = fields[1].shape[2:]
    xi_coarse, coef_middle, xi_middle, coef_fine, xi_fine = fields
    wide = 2 * rows + 128
    operands = (coef_fine, coef_middle, *sides)
    if edge:
        outs = [shape(8, wide)] * 2 + [shape(8, 2 * cols + 128)] * 2 + [shape(8, 128)]
    else:
        operands += (xi_fine, xi_middle, xi_coarse)
        outs = [shape(4 * rows, 4 * cols), shape(2 * rows, 2 * cols), shape(rows, cols)]
    return pl.pallas_call(
        functools.partial(adjoint_kernel, edge, len(parts)),
        in_specs=[whole] * len(parts) + [anywhere] * len(operands),
        out_specs=[whole] * len(outs) if edge else [anywhere, whole, whole],
        out_shape=outs,
        scratch_shapes=[pltpu.VMEM(x.shape, x.dtype) for x in operands]
        + [
            pltpu.VMEM((4 * cols, 4 * cols), bf16),
            pltpu.VMEM((4 * cols // 128, 4 * rows, 128), f32),
            pltpu.VMEM((9, 2 * rows, 2 * cols), f32),
            pltpu.VMEM((3, 2 * rows + 128, 2 * cols), f32),
            pltpu.VMEM((2 * cols, 2 * cols), bf16),
            pltpu.VMEM((2 * cols // 128, 2 * rows, 128), f32),
            pltpu.VMEM((9, rows, cols), f32),
            pltpu.VMEM((3, rows + 128, cols), f32),
            pltpu.VMEM((4 * rows, 4 * cols), f32),
            pltpu.SemaphoreType.DMA((len(operands),)),
            pltpu.SemaphoreType.DMA,
        ],
        compiler_params=pltpu.CompilerParams(vmem_limit_bytes=vmem),
        cost_estimate=long_work if edge else None,
        name="adjoint",
    )(*parts, *operands)


def in_three(x):
    high = x.astype(bf16).astype(f32)
    middle = (x - high).astype(bf16).astype(f32)
    return jnp.concatenate([high, middle, x - high - middle, jnp.zeros_like(x)]).astype(bf16)


def from_three(x):
    x = x.astype(f32)
    return x[:8] + x[8:16] + x[16:24]


def facets_kernel(blk, early, chips, ints, weights, *refs):
    number, slots = weights.shape
    tiles, strips, rest = refs[: 2 * chips], refs[2 * chips : 2 * chips + 2], refs[2 * chips + 2 :]
    ku_hbm, kv_hbm, data_hbm, squares, out_ref = rest[:5]
    held, held_strips, ku, kv, data, sums, dsum, total, sems, tile_sems, strip_sems = rest[5:]
    bins, side = ku.shape[1:]

    def inputs(f):
        for s in range(slots):
            for i, tile in enumerate(tiles):

                @pl.when(ints[f, s] == i)
                def _():
                    pltpu.make_async_copy(tile, held.at[f, s], tile_sems.at[f, s]).start()
                    hop = i % chips
                    if 1 <= hop <= early:
                        height = 4 * border
                        strip = strips[i // chips].at[(hop - 1) * height : hop * height]
                        pltpu.make_async_copy(
                            strip, held_strips.at[f, s], strip_sems.at[f, s]
                        ).start()

        pairs = ((ku_hbm, ku), (kv_hbm, kv), (data_hbm, data))
        copies = [
            pltpu.make_async_copy(src.at[0, f], dst.at[f], sems.at[f, i])
            for i, (src, dst) in enumerate(pairs)
        ]
        for copy in copies:
            copy.start()
        return copies

    def patch(f, s):
        hop = lax.rem(ints[f, s], chips)

        @pl.when((hop >= 1) & (hop <= early))
        def _():
            strip = strips[0].at[: 4 * border]
            pltpu.make_async_copy(strip, held_strips.at[f, s], strip_sems.at[f, s]).wait()
            tile, strip = held.at[f, s], held_strips.at[f, s]
            lines = strip[: 2 * border].astype(f32)
            top, bottom = tile[: 2 * border].astype(f32), tile[side - 2 * border :].astype(f32)
            tile[: 2 * border] = jnp.concatenate([lines[:border], top[border:]]).astype(bf16)
            tile[side - 2 * border :] = jnp.concatenate([bottom[:border], lines[border:]]).astype(
                bf16
            )
            lane = lax.broadcasted_iota(jnp.int32, (side, 128), 1)
            left, right = columns_of(strip[2 * border :])
            for cells, inside, start in (
                (left, lane < border, 0),
                (right, lane >= 128 - border, side - 128),
            ):
                here = tile[:, start : start + 128].astype(f32)
                tile[:, start : start + 128] = jnp.where(inside, cells, here).astype(bf16)

    def work(f, step):
        rows = slice(step * blk, (step + 1) * blk)
        count = ints[f, slots] - step * blk

        @pl.when(count > 0)
        def _():
            amp = jnp.dot(ku[f, rows], sums[...], preferred_element_type=f32).astype(bf16)
            vis = dot_t(amp, kv[f], ((1,), (1,)))
            live = lax.broadcasted_iota(jnp.int32, vis.shape, 0) < count
            resid = jnp.where(live, vis - data[f, rows].astype(f32), 0.0)
            total[...] += 0.5 * inv_noise * folded(resid * resid)
            dvis = (inv_noise * resid).astype(bf16)
            damp = jnp.dot(dvis, kv[f], preferred_element_type=f32).astype(bf16)
            part = dot_t(ku[f, rows], damp, ((0,), (0,)))
            if step == 0:
                dsum[...] = part
            else:
                dsum[...] += part

    copies = [inputs(0)]
    total[...] = 0.5 * squares[...]
    for f in range(number):
        for s in range(slots):
            pltpu.make_async_copy(tiles[0], held.at[f, s], tile_sems.at[f, s]).wait()
            patch(f, s)
        copies[f][0].wait()
        if f + 1 < number:
            copies.append(inputs(f + 1))
        mixture = weights[f, 0] * held[f, 0].astype(f32)
        for s in range(1, slots):
            mixture += weights[f, s] * held[f, s].astype(f32)
        sums[...] = mixture.astype(bf16)
        copies[f][1].wait()
        copies[f][2].wait()
        for step in range(bins // blk):
            work(f, step)
        out_ref[f * side : (f + 1) * side] = dsum[...].astype(bf16)
    out_ref[number * side :] = jnp.zeros((32, side), bf16)
    out_ref[number * side :, :128] = in_three(total[...])


def facets(tiles, strips, ku, kv, data, ints, weights, squares):
    number, bins, side = ku.shape[1:]
    slots = weights.shape[1]
    return pl.pallas_call(
        functools.partial(
            facets_kernel, 512, strips[0].shape[0] // (4 * border), len(tiles) // 2
        ),
        in_specs=[scalar] * 2 + [anywhere] * (len(tiles) + len(strips) + 3) + [whole],
        out_specs=whole,
        out_shape=jax.ShapeDtypeStruct((number * side + 32, side), bf16),
        scratch_shapes=[
            pltpu.VMEM((number, slots, side, side), bf16),
            pltpu.VMEM((number, slots, 4 * border, side), bf16),
            pltpu.VMEM((number, bins, side), bf16),
            pltpu.VMEM((number, bins, side), bf16),
            pltpu.VMEM((number, bins, bins), bf16),
            pltpu.VMEM((side, side), bf16),
            pltpu.VMEM((side, side), f32),
            pltpu.VMEM((8, 128), f32),
            pltpu.SemaphoreType.DMA((number, 3)),
            pltpu.SemaphoreType.DMA((number, slots)),
            pltpu.SemaphoreType.DMA((number, slots)),
        ],
        compiler_params=pltpu.CompilerParams(vmem_limit_bytes=60 * 1024 * 1024),
        name="facets",
    )(ints, weights, *tiles, *strips, ku, kv, data, squares)


def mix_kernel(scale, mine, theirs, *outs):
    side = outs[0].shape[1]
    number = mine.shape[0] // side
    for d, out in enumerate(outs):
        value = None
        for f in range(2 * number):
            ref, at = (mine, f) if f < number else (theirs, f - number)
            term = scale[d, f] * ref[at * side : (at + 1) * side].astype(f32)
            value = term if value is None else value + term
        out[...] = value.astype(bf16)


def mix_strips_kernel(scale, mine, theirs, *refs):
    outs, strips = refs[:-1], refs[-1]
    side = outs[0].shape[1]
    number = mine.shape[0] // side
    for f in range(2 * number):
        ref, at = (mine, f) if f < number else (theirs, f - number)
        strips_of(ref.at[at * side : (at + 1) * side], strips.at[f])
    total = from_three(mine[number * side :, :128]) + from_three(theirs[number * side :, :128])
    for d, out in enumerate(outs):
        value = None
        for f in range(2 * number):
            term = scale[d, f] * strips[f].astype(f32)
            value = term if value is None else value + term
        out[: 4 * border] = value.astype(bf16)
        out[4 * border :] = jnp.zeros((32, side), bf16)
        out[4 * border :, :128] = in_three(total)


def mixed(mine, theirs, scale, strips):
    side = mine.shape[1]
    rows = 4 * border + 32 if strips else side
    kept = [pltpu.VMEM((scale.shape[1], 4 * border, side), bf16)] if strips else []
    return pl.pallas_call(
        mix_strips_kernel if strips else mix_kernel,
        in_specs=[scalar, whole, whole],
        out_specs=[whole] * scale.shape[0],
        out_shape=[jax.ShapeDtypeStruct((rows, side), bf16)] * scale.shape[0],
        scratch_shapes=kept,
        compiler_params=pltpu.CompilerParams(vmem_limit_bytes=vmem),
        name="mixed",
    )(scale, mine, theirs)


def chip_shift(x, hop):
    size = lax.axis_size("gy")
    return lax.ppermute(x, "gy", [(i, (i + 2 * hop) % size) for i in range(size)])


def swapped(x):
    return lax.ppermute(x, "gy", [(i, i ^ 1) for i in range(lax.axis_size("gy"))])


def body(
    xi_coarse,
    xi_middle,
    xi_fine,
    coef_middle,
    coef_fine,
    kern_u,
    kern_v,
    vis_data,
    facet_tiles,
    facet_weight,
    facet_count,
):
    lists, weights, counts = facet_tiles[0], facet_weight[0], facet_count[0]
    size = lax.axis_size("gy")
    chips = size // 2
    me = lax.axis_index("gy")
    ids = jnp.arange(size, dtype=jnp.int32)
    mixing = jnp.sum(
        weights[:, :, None] * (lists[:, :, None] == ids[None, None, :]).astype(f32), axis=1
    )
    order = 2 * ((me // 2 + jnp.arange(chips, dtype=jnp.int32)) % chips) + me % 2
    scale = jnp.concatenate([mixing, swapped(mixing)])[:, order].T
    sel = (me // 2 - lists // 2) % chips + jnp.where(lists % 2 == me % 2, 0, chips)
    ints = jnp.concatenate([sel, counts[:, None]], axis=1)
    fields = (xi_coarse, coef_middle, xi_middle, coef_fine, xi_fine)
    right, left = neighbours("gy")
    down, up = neighbours("gx")
    sides = halo_sides(xi_coarse, xi_middle, coef_middle)
    left_in = lax.ppermute(sides[1], "gy", right)
    right_in = lax.ppermute(sides[0], "gy", left)
    (first,) = sky_of(None, *fields)
    first, left_in, right_in, around = lax.optimization_barrier(
        (first, left_in, right_in, (xi_coarse, xi_middle, coef_middle))
    )
    hops = range(1, chips)
    early = range(1, min(3, chips))
    mine = {hop: chip_shift(first, hop) for hop in early}
    above, below = halo_rows(*around, left_in, right_in)
    sky, strips, squares, lefts, rights = sky_of((above, below, left_in, right_in, *sides), *fields)
    strips = jnp.concatenate([chip_shift(strips, hop) for hop in early])
    sky, strips, mine, scale, ints, weights = lax.optimization_barrier(
        (sky, strips, mine, scale, ints, weights)
    )
    for hop in hops[len(early) :]:
        mine[hop] = chip_shift(sky, hop)
    mine = [sky] + [mine[hop] for hop in hops]
    tiles = mine + [swapped(tile) for tile in mine]
    strips = [strips, swapped(strips)]
    dsums = facets(tiles, strips, kern_u, kern_v, vis_data, ints, weights, squares)
    theirs = swapped(dsums)
    strips = mixed(dsums, theirs, scale, True)
    strips, dsums, theirs = lax.optimization_barrier((strips, dsums, theirs))
    edges = [strips[0]] + [chip_shift(strips[hop], hop) for hop in hops]
    parts = mixed(dsums, theirs, scale, False)
    edges, parts = lax.optimization_barrier((edges, parts))
    parts = [parts[0]] + [chip_shift(parts[hop], hop) for hop in hops]
    around = (above, below, lefts, rights)
    to_left, to_right, upper, lower, total = adjoint(True, edges, around, fields)
    size = lax.axis_size("gx")
    steps = [1 << i for i in range(size.bit_length()) if 1 << i < size]

    def across(x, hop):
        return lax.ppermute(x, "gx", [(i, i ^ hop) for i in range(size)])

    from_below = lax.ppermute(upper, "gx", up)
    from_above = lax.ppermute(lower, "gx", down)
    other = across(total, steps[0])
    rows, cols = xi_coarse.shape
    to_left, to_right, total = pl.pallas_call(
        functools.partial(corners_kernel, rows, cols),
        in_specs=[whole] * 6,
        out_specs=[whole] * 3,
        out_shape=[shape(*to_left.shape), shape(*to_right.shape), shape(8, 128)],
        name="corners",
    )(to_left, to_right, from_above, from_below, total, other)
    for hop in steps[1:-1]:
        total += across(total, hop)
    other = across(total, steps[-1])
    parts, to_left, to_right = lax.optimization_barrier((parts, to_left, to_right))
    from_left = lax.ppermute(to_right, "gy", right)
    from_right = lax.ppermute(to_left, "gy", left)
    grad_fine, middle, coarse = adjoint(False, parts, around, fields)
    cells = size * lax.axis_size("gy") * 16 * rows * cols
    grad_middle, grad_coarse, total = pl.pallas_call(
        functools.partial(final_kernel, cells),
        in_specs=[whole] * 8,
        out_specs=[whole] * 3,
        out_shape=[shape(2 * rows, 2 * cols), shape(rows, cols), shape(1, 1)],
        compiler_params=pltpu.CompilerParams(vmem_limit_bytes=vmem),
        name="final",
    )(middle, coarse, from_left, from_right, from_above, from_below, total, other)
    return grad_coarse, grad_middle, grad_fine, total.reshape(())


def solution(mesh):
    placed = (
        P("gx", "gy"),
        P("gx", "gy"),
        P("gx", "gy"),
        P(None, None, "gx", "gy"),
        P(None, None, "gx", "gy"),
        P("gx", "gy", None, None),
        P("gx", "gy", None, None),
        P("gx", "gy", None, None),
        P("gx", "gy", None),
        P("gx", "gy", None),
        P("gx", "gy"),
    )
    return jax.shard_map(
        body,
        mesh=mesh,
        in_specs=placed,
        out_specs=(P("gx", "gy"), P("gx", "gy"), P("gx", "gy"), P()),
        check_vma=False,
    )
```

```python
import functools

import jax
import jax.numpy as jnp
from jax import lax
from jax.experimental import pallas as pl
from jax.experimental.pallas import tpu as pltpu
from jax.sharding import PartitionSpec as P

inv_noise = 0.125
long_work = pl.CostEstimate(flops=40_000_000_000, transcendentals=0, bytes_accessed=64_000_000)
border = 8
vmem = 32 * 1024 * 1024
f32 = jnp.float32
bf16 = jnp.bfloat16


def halves(x):
    high = x.astype(bf16)
    return high, (x - high.astype(f32)).astype(bf16)


def interleaver(cols, transposed):
    shape = (2 * cols, 2 * cols)
    split = lax.broadcasted_iota(jnp.int32, shape, 1 if transposed else 0)
    whole = lax.broadcasted_iota(jnp.int32, shape, 0 if transposed else 1)
    place = jnp.where(split >= cols, 2 * (split - cols) + 1, 2 * split)
    return (place == whole).astype(f32).astype(bf16)


def folded(x):
    rows, cols = x.shape
    x = jnp.sum(x.reshape(rows // 8, 8, cols), axis=0)
    return sum(x[:, i : i + 128] for i in range(0, cols, 128))


def row_of(ref, i):
    return ref[i : i + 1, :]


def dot_t(x, y, dims):
    return lax.dot_general(x, y, (dims, ((), ())), preferred_element_type=f32)


def moved(x, perm):
    high, low = halves(x)
    return jnp.dot(high, perm, preferred_element_type=f32) + jnp.dot(
        low, perm, preferred_element_type=f32
    )


def ends_placed(first, last, cols):
    rows = jnp.concatenate([first, first, last, last, jnp.zeros((4, first.shape[1]), f32)])
    high = rows.astype(bf16).astype(f32)
    index = lax.broadcasted_iota(jnp.int32, rows.shape, 0)
    rows = jnp.where(index % 2 == 0, high, rows - high).astype(bf16)
    shape = (8, cols)
    index = lax.broadcasted_iota(jnp.int32, shape, 0)
    lane = lax.broadcasted_iota(jnp.int32, shape, 1)
    place = ((index < 2) & (lane == 0)) | ((index >= 2) & (index < 4) & (lane == cols - 1))
    return dot_t(rows, place.astype(f32).astype(bf16), ((0,), (0,)))


def weighed(win, coef_ref, perm, lhs, mix, rows, cols, chunks=()):
    def part(i, carry):
        r0 = pl.multiple_of(i * 16, 16)
        total = [jnp.zeros((16, cols), f32) for _ in range(4)]
        for near in range(9):
            w = win[near, pl.ds(r0, 16), :]
            for child in range(4):
                total[child] += coef_ref[child, near, pl.ds(r0, 16), :].astype(f32) * w
        for child in range(4):
            a, b = child // 2, child % 2
            high, low = halves(total[child])
            lhs[pl.ds(2 * a * rows + r0, 16), b * cols : (b + 1) * cols] = high
            lhs[pl.ds((2 * a + 1) * rows + r0, 16), b * cols : (b + 1) * cols] = low
        return carry

    in_chunks(part, rows, chunks)
    field = jnp.dot(lhs[...], perm[...], preferred_element_type=f32)
    for tile in range(2 * cols // 128):
        lanes = slice(tile * 128, (tile + 1) * 128)
        for a in range(2):
            mix[tile, pl.ds(a, rows, stride=2), :] = (
                field[2 * a * rows : (2 * a + 1) * rows, lanes]
                + field[(2 * a + 1) * rows : (2 * a + 2) * rows, lanes]
            )


def fetched(pairs, sems, first=0):
    copies = [
        pltpu.make_async_copy(src, dst, sems.at[first + i]) for i, (src, dst) in enumerate(pairs)
    ]
    for copy in copies:
        copy.start()
    return copies


def chunked(source, target, sems):
    number, rows = sems.shape[0], source.shape[2] // sems.shape[0]
    copies = []
    for i in range(number):
        at = slice(i * rows, (i + 1) * rows)
        copies.append(pltpu.make_async_copy(source.at[:, :, at], target.at[:, :, at], sems.at[i]))
        copies[i].start()
    return copies


def in_chunks(part, rows, chunks):
    steps = rows // 16
    if not chunks:
        lax.fori_loop(0, steps, part, 0)
    for i, copy in enumerate(chunks):
        copy.wait()
        lax.fori_loop(i * steps // len(chunks), (i + 1) * steps // len(chunks), part, 0)


def columns_beside(field, left, right):
    rows, cols = field.shape[1:]
    placed = ends_placed(left, right, cols)
    lane = lax.broadcasted_iota(jnp.int32, (rows, cols), 1)
    here = field[1]
    field[0] = jnp.where(lane == 0, placed, pltpu.roll(here, 1, 1))
    field[2] = jnp.where(lane == cols - 1, placed, pltpu.roll(here, cols - 1, 1))


def strips_of(tile, out):
    rows, cols = tile.shape
    first, last = tile[: 2 * border].astype(f32), tile[rows - 2 * border :].astype(f32)
    out[: 2 * border] = jnp.concatenate([first[:border], last[border:]]).astype(bf16)
    index = lax.broadcasted_iota(jnp.int32, (2 * border, cols), 0)
    lane = lax.broadcasted_iota(jnp.int32, (2 * border, cols), 1)
    pick = lane == jnp.where(index < border, index, index + cols - 2 * border)
    pick = pick.astype(f32).astype(bf16)
    out[2 * border : 4 * border] = dot_t(pick, tile[...], ((1,), (1,))).astype(bf16)


def columns_of(strip):
    index = lax.broadcasted_iota(jnp.int32, (2 * border, 128), 0)
    lane = lax.broadcasted_iota(jnp.int32, (2 * border, 128), 1)
    out = []
    for place in (
        (index < border) & (lane == index),
        (index >= border) & (lane == index + 128 - 2 * border),
    ):
        out.append(dot_t(strip, place.astype(f32).astype(bf16), ((0,), (0,))))
    return out


def stretch(out, side, over, under, b, lane, first):
    rows = side.shape[1]
    out[...] = jnp.zeros_like(out)
    out[:, 2 : rows + 2] = side[...]
    out[9:18, 1:2] = over[9 * b : 9 * b + 9, lane : lane + 1]
    out[21:22, 1:2] = over[20 + b : 21 + b, lane : lane + 1]
    out[0:9, rows + 2 : rows + 3] = under[9 * b : 9 * b + 9, lane : lane + 1]
    out[20:21, rows + 2 : rows + 3] = under[20 + b : 21 + b, lane : lane + 1]
    for k in range(2):
        at = slice(first + k, first + k + 1)
        for i in range(2):
            out[18 + k : 19 + k, i : i + 1] = over[18 + i : 19 + i, at]
            end = rows + 2 + i
            out[18 + k : 19 + k, end : end + 1] = under[18 + i : 19 + i, at]


def sky_kernel(alone, *refs):
    count = 5 if alone else 11
    sources, refs = refs[:count], refs[count:]
    outs, refs = (refs[:1], refs[1:]) if alone else (refs[:5], refs[5:])
    held, rest = refs[:11], refs[11:]
    win, perm, lhs, mix, near_coarse, shifted, fine_win, fine_perm, fine_lhs, fine_mix = rest[:10]
    lefts, rights, to_left, to_right, sems, chunk_sems = rest[10:]
    sky_ref = outs[0]
    if alone:
        for ref in held[1:7]:
            ref[...] = jnp.zeros_like(ref)
        held_here = (held[0], *held[7:])
    else:
        held_here = held
    copies = fetched(zip(sources[:-2], held_here[:-2]), sems)
    chunks = chunked(sources[-2], held_here[-2], chunk_sems)
    copies += fetched(zip(sources[-1:], held_here[-1:]), sems, len(copies))
    xi_coarse, over, under, left_in, right_in, left_side, right_side = held[:7]
    coef_middle, xi_middle, coef_fine, xi_fine = held[7:]
    rows, cols = win.shape[1:]
    perm[...] = interleaver(cols, False)
    fine_perm[...] = interleaver(2 * cols, False)
    near_coarse[...] = jnp.zeros_like(near_coarse)
    for copy in copies[:-2]:
        copy.wait()
    above, below = over[:, 2 : cols + 2], under[:, 2 : cols + 2]
    if alone:
        for ref in (lefts, rights):
            ref[...] = jnp.zeros_like(ref)
    else:
        stretch(lefts, left_in, over, under, 1, 1, 0)
        stretch(rights, right_in, over, under, 0, cols + 2, cols + 2)
        stretch(to_left, left_side, over, under, 0, 2, 2)
        stretch(to_right, right_side, over, under, 1, cols + 1, cols)
    near_coarse[1, 6:8] = above[18:20]
    near_coarse[1, 8 : 8 + rows] = xi_coarse[...]
    near_coarse[1, 8 + rows : 10 + rows] = below[18:20]
    pad = jnp.zeros((1, 6), f32)
    beside = [
        jnp.concatenate([pad, row_of(x, i)[:, : rows + 4], pad], axis=1)
        for x, i in ((lefts, 19), (rights, 18))
    ]
    columns_beside(near_coarse, *beside)
    for near in range(9):
        r, c = near // 3, near % 3
        win[near] = near_coarse[c, 7 + r : 7 + r + rows]
    weighed(win, coef_middle, perm, lhs, mix, rows, cols)

    def across(message, top):
        out = []
        for b in range(2):
            line = row_of(message, 20 + b)
            for near in range(9):
                r, c = near // 3, near % 3
                line += row_of(message, 9 * b + near) * near_coarse[c, top + r : top + r + 1]
            out.append(line)
        return jnp.concatenate(out, axis=1)

    def along(message, fields):
        out = []
        for a in range(2):
            line = row_of(message, 20 + a)[:, 1 : rows + 3]
            for near in range(9):
                r, c = near // 3, near % 3
                line += row_of(message, 9 * a + near)[:, 1 : rows + 3] * fields[c][:, r : r + rows + 2]
            out.append(line)
        inner = jnp.concatenate([line[:, 1 : rows + 1] for line in out], axis=1)
        return inner, out[1][:, :1], out[0][:, rows + 1 :]

    if alone:
        empty = jnp.zeros((1, 1), f32)
        top = bottom = left = right = jnp.zeros((1, 2 * cols), f32)
        top_left = bottom_left = top_right = bottom_right = empty
    else:
        top, bottom = across(above, 6), across(below, rows + 7)
        left, top_left, bottom_left = along(
            lefts, [row_of(lefts, 18), row_of(lefts, 19), row_of(to_left, 18)]
        )
        right, top_right, bottom_right = along(
            rights, [row_of(to_right, 19), row_of(rights, 18), row_of(rights, 19)]
        )
    lines = jnp.concatenate([top, bottom, left, right, jnp.zeros((4, 2 * cols), f32)])
    lines = moved(lines, perm[...])
    copies[-2].wait()
    xi = xi_middle[...]
    last = 8 + 2 * rows
    shifted[1] = jnp.zeros(shifted.shape[1:], f32)
    for tile in range(2 * cols // 128):
        lanes = slice(tile * 128, (tile + 1) * 128)
        shifted[1, 8:last, lanes] = mix[tile] + xi[:, lanes]
    shifted[1, 7:8, :] = lines[0:1]
    shifted[1, last : last + 1, :] = lines[1:2]
    pad = jnp.zeros((1, 7), f32)
    beside = [
        jnp.concatenate([pad, first, line, final, pad], axis=1)
        for first, line, final in (
            (top_left, lines[2:3], bottom_left),
            (top_right, lines[3:4], bottom_right),
        )
    ]
    columns_beside(shifted, *beside)
    for near in range(9):
        r, c = near // 3, near % 3
        fine_win[near] = shifted[c, 7 + r : 7 + r + 2 * rows, :]
    weighed(fine_win, coef_fine, fine_perm, fine_lhs, fine_mix, 2 * rows, 2 * cols, chunks)
    copies[-1].wait()
    for tile in range(4 * cols // 128):
        lanes = slice(tile * 128, (tile + 1) * 128)
        sky_ref[:, lanes] = (fine_mix[tile] + xi_fine[:, lanes]).astype(bf16)
    if alone:
        return
    strips_ref, sq_ref, lefts_ref, rights_ref = outs[1:]
    lefts_ref[...] = lefts[...]
    rights_ref[...] = rights[...]
    strips_of(sky_ref, strips_ref)
    sq_ref[...] = (
        folded(win[4] * win[4]) + folded(xi * xi) + folded(xi_fine[...] * xi_fine[...])
    )


def sides_kernel(left_in, right_in, first_side, last_side, to_above, to_below):
    rows = left_in.shape[1]
    stretch(to_above, first_side, left_in, right_in, 0, 0, 0)
    stretch(to_below, last_side, left_in, right_in, 1, rows - 1, rows - 2)


def neighbours(axis):
    size = lax.axis_size(axis)
    ahead = [(i, i + 1) for i in range(size - 1)]
    return ahead, [(j, i) for i, j in ahead]


def halo_sides(xi_coarse, xi_middle, coef_middle):
    rows, cols = xi_coarse.shape

    def inside(b, col, near):
        return jnp.concatenate(
            [
                coef_middle[b::2, :, :, col].reshape(18, rows).astype(f32),
                near.T,
                xi_middle[:, 2 * col + b].reshape(rows, 2).T,
            ]
        )

    return inside(0, 0, xi_coarse[:, :2]), inside(1, cols - 1, xi_coarse[:, -2:])


def halo_rows(xi_coarse, xi_middle, coef_middle, left_in, right_in):
    rows, cols = xi_coarse.shape

    def edge(a, row, near):
        return jnp.concatenate(
            [
                coef_middle[2 * a : 2 * a + 2, :, row].reshape(18, cols).astype(f32),
                near,
                xi_middle[2 * row + a].reshape(cols, 2).T,
            ]
        )

    to_above, to_below = pl.pallas_call(
        sides_kernel,
        in_specs=[whole] * 4,
        out_specs=[whole] * 2,
        out_shape=[jax.ShapeDtypeStruct((22, cols + 4), f32)] * 2,
        cost_estimate=long_work,
        name="sides",
    )(left_in, right_in, edge(0, 0, xi_coarse[:2]), edge(1, rows - 1, xi_coarse[-2:]))
    down, up = neighbours("gx")
    return lax.ppermute(to_below, "gx", down), lax.ppermute(to_above, "gx", up)


whole = pl.BlockSpec(memory_space=pltpu.VMEM)
scalar = pl.BlockSpec(memory_space=pltpu.SMEM)
anywhere = pl.BlockSpec(memory_space=pltpu.HBM)


def sky_of(halos, xi_coarse, coef_middle, xi_middle, coef_fine, xi_fine):
    rows, cols = coef_middle.shape[2:]
    alone = halos is None
    given = (coef_middle, xi_middle, coef_fine, xi_fine)
    operands = (xi_coarse, *given) if alone else (xi_coarse, *halos, *given)
    message = [(22, cols + 4)] * 2 + [(22, rows)] * 4
    return pl.pallas_call(
        functools.partial(sky_kernel, alone),
        in_specs=[anywhere] * len(operands),
        out_specs=[whole] * (1 if alone else 5),
        out_shape=[
            jax.ShapeDtypeStruct((4 * rows, 4 * cols), bf16),
            jax.ShapeDtypeStruct((4 * border, 4 * cols), bf16),
            jax.ShapeDtypeStruct((8, 128), f32),
            jax.ShapeDtypeStruct((22, rows + 4), f32),
            jax.ShapeDtypeStruct((22, rows + 4), f32),
        ][: 1 if alone else 5],
        scratch_shapes=[pltpu.VMEM(xi_coarse.shape, f32)]
        + [pltpu.VMEM(shape, f32) for shape in message]
        + [pltpu.VMEM(x.shape, x.dtype) for x in given]
        + [
            pltpu.VMEM((9, rows, cols), f32),
            pltpu.VMEM((2 * cols, 2 * cols), bf16),
            pltpu.VMEM((4 * rows, 2 * cols), bf16),
            pltpu.VMEM((2 * cols // 128, 2 * rows, 128), f32),
            pltpu.VMEM((3, rows + 16, cols), f32),
            pltpu.VMEM((3, 2 * rows + 16, 2 * cols), f32),
            pltpu.VMEM((9, 2 * rows, 2 * cols), f32),
            pltpu.VMEM((4 * cols, 4 * cols), bf16),
            pltpu.VMEM((8 * rows, 4 * cols), bf16),
            pltpu.VMEM((4 * cols // 128, 4 * rows, 128), f32),
            *[pltpu.VMEM((22, rows + 4), f32) for _ in range(4)],
            pltpu.SemaphoreType.DMA((11,)),
            pltpu.SemaphoreType.DMA((4,)),
        ],
        compiler_params=pltpu.CompilerParams(vmem_limit_bytes=60 * 1024 * 1024),
        name="sky",
    )(*operands)


def spread(mix, coef_ref, terms, rows, cols, chunks=()):
    def part(i, carry):
        r0 = pl.multiple_of(i * 16, 16)
        quads = []
        for a in range(2):
            for b in range(2):
                tiles = range(b * cols // 128, (b + 1) * cols // 128)
                lines = [mix[t, pl.ds(2 * r0 + a, 16, stride=2), :] for t in tiles]
                quads.append(jnp.concatenate(lines, axis=1))
        for near in range(9):
            total = jnp.zeros((16, cols), f32)
            for child in range(4):
                total += coef_ref[child, near, pl.ds(r0, 16), :].astype(f32) * quads[child]
            terms[near, pl.ds(r0, 16), :] = total
        return carry

    in_chunks(part, rows, chunks)


def joined(rowed, cols):
    lane = lax.broadcasted_iota(jnp.int32, rowed.shape[1:], 1)
    main = (
        rowed[1]
        + jnp.where(lane == 0, 0.0, pltpu.roll(rowed[2], 1, 1))
        + jnp.where(lane == cols - 1, 0.0, pltpu.roll(rowed[0], cols - 1, 1))
    )
    lane = lax.broadcasted_iota(jnp.int32, (8, cols), 1)
    outside = []
    for c, col in ((0, 0), (2, cols - 1)):
        pick = (lane == col).astype(f32).astype(bf16)
        high, low = halves(rowed[c])
        out = dot_t(pick, high, ((1,), (1,))) + dot_t(pick, low, ((1,), (1,)))
        outside.append(out[:1])
    return main, outside[0], outside[1]


def adjoint_kernel(edge, number, cells, *refs):
    count = 6 if edge else 15
    written = 5 if edge else 4
    count += number
    sources, outs, refs = refs[:count], refs[count : count + written], refs[count + written :]
    parts, held, rest = refs[:number], refs[number:count], refs[count:]
    fine_perm, fine_mix, fine_terms, fine_rowed, perm, mix, terms, rowed, full, sems, chunk_sems, out_sem = rest
    arriving = fetched(zip(sources[:number], parts), sems)
    chunks = chunked(sources[number], held[0], chunk_sems)
    copies = [None] + fetched(zip(sources[number + 1 :], held[1:]), sems, number)
    coef_fine, coef_middle, over, under, lefts, rights = held[:6]
    if edge:
        left_ref, right_ref, upper_ref, lower_ref, total_ref = outs
    else:
        grad_ref, middle_ref, coarse_ref, total_ref = outs
        xi_fine, xi_middle, xi_coarse, from_left, from_right, from_above, from_below = held[6:13]
        total, other = held[13:]
    rows, cols = terms.shape[1:]
    fine_perm[...] = interleaver(2 * cols, True)
    perm[...] = interleaver(cols, True)
    for copy in arriving:
        copy.wait()
    g = parts[0][...].astype(f32)
    for part in parts[1:]:
        g += part[...].astype(f32)
    if edge:
        tail = g[4 * border :, :128]
        total_ref[...] = tail[:8] + tail[8:16] + tail[16:24]
        high, low = halves(g[2 * border : 4 * border])
        left, right = [x + y for x, y in zip(columns_of(high), columns_of(low))]
        full[...] = jnp.zeros_like(full)
        full[:, :128] = left
        full[:, 4 * cols - 128 :] = right
        full[:border] = g[:border]
        full[4 * rows - border :] = g[border : 2 * border]
        g = full[...]
    else:
        copies[6].wait()
        full[...] = g + xi_fine[...]
        leaving = pltpu.make_async_copy(full, grad_ref, out_sem)
        leaving.start()
    split = moved(g, fine_perm[...])
    for tile in range(4 * cols // 128):
        fine_mix[tile] = split[:, tile * 128 : (tile + 1) * 128]
    spread(fine_mix, coef_fine, fine_terms, 2 * rows, 2 * cols, chunks)
    fine_rowed[...] = jnp.zeros_like(fine_rowed)
    for near in range(9):
        r, c = near // 3, near % 3
        fine_rowed[c, 7 + r : 7 + r + 2 * rows, :] += fine_terms[near]
    main, left, right = joined(fine_rowed, 2 * cols)
    last = 8 + 2 * rows
    inner = main[8:last]
    for copy in copies[1:6] + copies[7:]:
        copy.wait()
    above, below = over[:, 2 : cols + 2], under[:, 2 : cols + 2]
    if not edge:
        line = slice(1, 2 * rows + 1)
        middle_ref[...] = (
            inner
            + xi_middle[...]
            + ends_placed(from_left[2:3, line], from_right[2:3, line], 2 * cols)
        )
        middle_ref[:1] += from_above[2:3, 1 : 2 * cols + 1]
        middle_ref[2 * rows - 1 :] += from_below[2:3, 1 : 2 * cols + 1]
    split = moved(inner, perm[...])
    for tile in range(2 * cols // 128):
        mix[tile] = split[:, tile * 128 : (tile + 1) * 128]
    spread(mix, coef_middle, terms, rows, cols)
    ring_above, ring_below = main[7:8], main[last : last + 1]
    lines = [ring_above, ring_below, left[:, 8:last], right[:, 8:last]]
    lines = moved(jnp.concatenate(lines + [jnp.zeros((4, 2 * cols), f32)]), perm[...])
    rowed[...] = jnp.zeros_like(rowed)
    for near in range(9):
        r, c = near // 3, near % 3
        rowed[c, 7 + r : 7 + r + rows, :] += terms[near]
    for line, message, top in ((0, above, 6), (1, below, 7 + rows)):
        for near in range(9):
            r, c = near // 3, near % 3
            term = row_of(message, near) * lines[line : line + 1, :cols]
            term += row_of(message, 9 + near) * lines[line : line + 1, cols:]
            rowed[c, top + r : top + r + 1, :] += term

    def along(line, ends, message):
        empty = jnp.zeros((1, 1), f32)
        first = [empty, lines[line : line + 1, :rows], ends[:, last : last + 1]]
        second = [ends[:, 7:8], lines[line : line + 1, cols : cols + rows], empty]
        first, second = jnp.concatenate(first, axis=1), jnp.concatenate(second, axis=1)
        out = []
        for c in range(3):
            total = jnp.zeros((1, rows + 4), f32)
            for r in range(3):
                near = 3 * r + c
                term = row_of(message, near)[:, 1 : rows + 3] * first
                term += row_of(message, 9 + near)[:, 1 : rows + 3] * second
                pads = [jnp.zeros((1, n), f32) for n in (r, 2 - r) if n]
                pieces = [term] + pads if r == 0 else pads[:1] + [term] + pads[1:]
                total += jnp.concatenate(pieces, axis=1)
            out.append(total)
        return out

    outer_left = along(2, left, lefts)
    outer_right = along(3, right, rights)
    main, near_left, near_right = joined(rowed, cols)
    if not edge:
        line = slice(2, rows + 2)
        first = outer_left[2][:, line] + from_left[1:2, line]
        last = outer_right[0][:, line] + from_right[1:2, line]
        second = ends_placed(from_left[0:1, line], from_right[0:1, line], cols)
        lane = lax.broadcasted_iota(jnp.int32, second.shape, 1)
        second = jnp.where(lane == 1, pltpu.roll(second, 1, 1), 0.0) + jnp.where(
            lane == cols - 2, pltpu.roll(second, cols - 1, 1), 0.0
        )
        coarse_ref[...] = (
            main[8 : 8 + rows] + xi_coarse[...] + ends_placed(first, last, cols) + second
        )
        coarse_ref[:2] += from_above[0:2, 2 : cols + 2]
        coarse_ref[rows - 2 :] += from_below[0:2, 2 : cols + 2]
        both = total[...] + other[...]
        both = jnp.sum(jnp.sum(both, axis=1, keepdims=True), axis=0, keepdims=True)
        total_ref[...] = both * (1.0 / cells)
        leaving.wait()
        return
    sides = []
    for ref, far, close, beyond, ends in (
        (left_ref, outer_left[0], outer_left[1], near_left, left),
        (right_ref, outer_right[2], outer_right[1], near_right, right),
    ):
        close += beyond[:, 6 : rows + 10]
        ends = ends[:, 7 : 2 * rows + 9]
        ref[...] = jnp.zeros_like(ref)
        ref[0:1, : rows + 4] = far
        ref[1:2, : rows + 4] = close
        ref[2:3, : 2 * rows + 2] = ends
        sides.append((far, close, ends))
    lane = lax.broadcasted_iota(jnp.int32, (1, cols), 1)
    (far_left, close_left, ends_left), (far_right, close_right, ends_right) = sides
    for ref, first, line, end in (
        (upper_ref, 6, ring_above, 0),
        (lower_ref, 8 + rows, ring_below, 2 * rows + 1),
    ):
        ref[...] = jnp.zeros_like(ref)
        for i in range(2):
            at = slice(first - 6 + i, first - 5 + i)
            inner = (
                main[first + i : first + i + 1]
                + jnp.where(lane == 0, outer_left[2][:, at], 0.0)
                + jnp.where(lane == cols - 1, outer_right[0][:, at], 0.0)
            )
            pieces = [far_left[:, at], close_left[:, at], inner, close_right[:, at], far_right[:, at]]
            ref[i : i + 1, : cols + 4] = jnp.concatenate(pieces, axis=1)
        pieces = [ends_left[:, end : end + 1], line, ends_right[:, end : end + 1]]
        ref[2:3, : 2 * cols + 2] = jnp.concatenate(pieces, axis=1)


def corners_kernel(rows, cols, left, right, from_above, from_below, total, other, left_out, right_out, total_out):
    for ref, out, far, close, end in (
        (left, left_out, 0, 1, 0),
        (right, right_out, cols + 3, cols + 2, 2 * cols + 1),
    ):
        out[...] = ref[...]
        for rows_in, first, line in ((from_above, 2, 1), (from_below, rows, 2 * rows)):
            for i in range(2):
                at = slice(first + i, first + i + 1)
                out[0:1, at] += rows_in[i : i + 1, far : far + 1]
                out[1:2, at] += rows_in[i : i + 1, close : close + 1]
            out[2:3, line : line + 1] += rows_in[2:3, end : end + 1]
    total_out[...] = total[...] + other[...]


def shape(*dims):
    return jax.ShapeDtypeStruct(dims, f32)


def adjoint(edge, parts, sides, fields, arrived=(), cells=0):
    rows, cols = fields[1].shape[2:]
    xi_coarse, coef_middle, xi_middle, coef_fine, xi_fine = fields
    wide = 2 * rows + 128
    operands = (coef_fine, coef_middle, *sides)
    if edge:
        outs = [shape(8, wide)] * 2 + [shape(8, 2 * cols + 128)] * 2 + [shape(8, 128)]
    else:
        operands += (xi_fine, xi_middle, xi_coarse, *arrived)
        outs = [shape(4 * rows, 4 * cols), shape(2 * rows, 2 * cols), shape(rows, cols)]
        outs += [shape(1, 1)]
    return pl.pallas_call(
        functools.partial(adjoint_kernel, edge, len(parts), cells),
        in_specs=[anywhere] * (len(parts) + len(operands)),
        out_specs=[whole] * 5 if edge else [anywhere, whole, whole, whole],
        out_shape=outs,
        scratch_shapes=[pltpu.VMEM(x.shape, x.dtype) for x in (*parts, *operands)]
        + [
            pltpu.VMEM((4 * cols, 4 * cols), bf16),
            pltpu.VMEM((4 * cols // 128, 4 * rows, 128), f32),
            pltpu.VMEM((9, 2 * rows, 2 * cols), f32),
            pltpu.VMEM((3, 2 * rows + 128, 2 * cols), f32),
            pltpu.VMEM((2 * cols, 2 * cols), bf16),
            pltpu.VMEM((2 * cols // 128, 2 * rows, 128), f32),
            pltpu.VMEM((9, rows, cols), f32),
            pltpu.VMEM((3, rows + 128, cols), f32),
            pltpu.VMEM((4 * rows, 4 * cols), f32),
            pltpu.SemaphoreType.DMA((len(parts) + len(operands),)),
            pltpu.SemaphoreType.DMA((4,)),
            pltpu.SemaphoreType.DMA,
        ],
        compiler_params=pltpu.CompilerParams(vmem_limit_bytes=60 * 1024 * 1024),
        cost_estimate=long_work if edge else None,
        name="adjoint",
    )(*parts, *operands)


def in_three(x):
    high = x.astype(bf16).astype(f32)
    middle = (x - high).astype(bf16).astype(f32)
    return jnp.concatenate([high, middle, x - high - middle, jnp.zeros_like(x)]).astype(bf16)


def from_three(x):
    x = x.astype(f32)
    return x[:8] + x[8:16] + x[16:24]


def facets_kernel(blk, early, chips, ints, weights, *refs):
    number, slots = weights.shape
    tiles, strips, rest = refs[: 2 * chips], refs[2 * chips : 2 * chips + 2], refs[2 * chips + 2 :]
    ku_hbm, kv_hbm, data_hbm, squares, out_ref = rest[:5]
    held, held_strips, ku, kv, data, sums, dsum, total, sems, tile_sems, strip_sems = rest[5:]
    bins, side = ku.shape[1:]

    def inputs(f):
        for s in range(slots):
            for i, tile in enumerate(tiles):

                @pl.when(ints[f, s] == i)
                def _():
                    pltpu.make_async_copy(tile, held.at[f, s], tile_sems.at[f, s]).start()
                    hop = i % chips
                    if 1 <= hop <= early:
                        height = 4 * border
                        strip = strips[i // chips].at[(hop - 1) * height : hop * height]
                        pltpu.make_async_copy(
                            strip, held_strips.at[f, s], strip_sems.at[f, s]
                        ).start()

        pairs = ((ku_hbm, ku), (kv_hbm, kv), (data_hbm, data))
        copies = [
            pltpu.make_async_copy(src.at[0, f], dst.at[f], sems.at[f, i])
            for i, (src, dst) in enumerate(pairs)
        ]
        for copy in copies:
            copy.start()
        return copies

    def patch(f, s):
        hop = lax.rem(ints[f, s], chips)

        @pl.when((hop >= 1) & (hop <= early))
        def _():
            strip = strips[0].at[: 4 * border]
            pltpu.make_async_copy(strip, held_strips.at[f, s], strip_sems.at[f, s]).wait()
            tile, strip = held.at[f, s], held_strips.at[f, s]
            lines = strip[: 2 * border].astype(f32)
            top, bottom = tile[: 2 * border].astype(f32), tile[side - 2 * border :].astype(f32)
            tile[: 2 * border] = jnp.concatenate([lines[:border], top[border:]]).astype(bf16)
            tile[side - 2 * border :] = jnp.concatenate([bottom[:border], lines[border:]]).astype(
                bf16
            )
            lane = lax.broadcasted_iota(jnp.int32, (side, 128), 1)
            left, right = columns_of(strip[2 * border :])
            for cells, inside, start in (
                (left, lane < border, 0),
                (right, lane >= 128 - border, side - 128),
            ):
                here = tile[:, start : start + 128].astype(f32)
                tile[:, start : start + 128] = jnp.where(inside, cells, here).astype(bf16)

    def work(f, step):
        rows = slice(step * blk, (step + 1) * blk)
        count = ints[f, slots] - step * blk

        @pl.when(count > 0)
        def _():
            amp = jnp.dot(ku[f, rows], sums[...], preferred_element_type=f32).astype(bf16)
            vis = dot_t(amp, kv[f], ((1,), (1,)))
            live = lax.broadcasted_iota(jnp.int32, vis.shape, 0) < count
            resid = jnp.where(live, vis - data[f, rows].astype(f32), 0.0)
            total[...] += 0.5 * inv_noise * folded(resid * resid)
            dvis = (inv_noise * resid).astype(bf16)
            damp = jnp.dot(dvis, kv[f], preferred_element_type=f32).astype(bf16)
            part = dot_t(ku[f, rows], damp, ((0,), (0,)))
            if step == 0:
                dsum[...] = part
            else:
                dsum[...] += part

    copies = [inputs(0)]
    total[...] = 0.5 * squares[...]
    for f in range(number):
        for s in range(slots):
            pltpu.make_async_copy(tiles[0], held.at[f, s], tile_sems.at[f, s]).wait()
            patch(f, s)
        copies[f][0].wait()
        if f + 1 < number:
            copies.append(inputs(f + 1))
        mixture = weights[f, 0] * held[f, 0].astype(f32)
        for s in range(1, slots):
            mixture += weights[f, s] * held[f, s].astype(f32)
        sums[...] = mixture.astype(bf16)
        copies[f][1].wait()
        copies[f][2].wait()
        for step in range(bins // blk):
            work(f, step)
        out_ref[f * side : (f + 1) * side] = dsum[...].astype(bf16)
    out_ref[number * side :] = jnp.zeros((32, side), bf16)
    out_ref[number * side :, :128] = in_three(total[...])


def facets(tiles, strips, ku, kv, data, ints, weights, squares):
    number, bins, side = ku.shape[1:]
    slots = weights.shape[1]
    return pl.pallas_call(
        functools.partial(
            facets_kernel, 512, strips[0].shape[0] // (4 * border), len(tiles) // 2
        ),
        in_specs=[scalar] * 2 + [anywhere] * (len(tiles) + len(strips) + 3) + [whole],
        out_specs=whole,
        out_shape=jax.ShapeDtypeStruct((number * side + 32, side), bf16),
        scratch_shapes=[
            pltpu.VMEM((number, slots, side, side), bf16),
            pltpu.VMEM((number, slots, 4 * border, side), bf16),
            pltpu.VMEM((number, bins, side), bf16),
            pltpu.VMEM((number, bins, side), bf16),
            pltpu.VMEM((number, bins, bins), bf16),
            pltpu.VMEM((side, side), bf16),
            pltpu.VMEM((side, side), f32),
            pltpu.VMEM((8, 128), f32),
            pltpu.SemaphoreType.DMA((number, 3)),
            pltpu.SemaphoreType.DMA((number, slots)),
            pltpu.SemaphoreType.DMA((number, slots)),
        ],
        compiler_params=pltpu.CompilerParams(vmem_limit_bytes=44 * 1024 * 1024),
        name="facets",
    )(ints, weights, *tiles, *strips, ku, kv, data, squares)


def mix_kernel(scale, mine, theirs, *outs):
    side = outs[0].shape[1]
    number = mine.shape[0] // side
    for d, out in enumerate(outs):
        value = None
        for f in range(2 * number):
            ref, at = (mine, f) if f < number else (theirs, f - number)
            term = scale[d, f] * ref[at * side : (at + 1) * side].astype(f32)
            value = term if value is None else value + term
        out[...] = value.astype(bf16)


def mix_strips_kernel(scale, mine, theirs, *refs):
    outs, strips = refs[:-1], refs[-1]
    side = outs[0].shape[1]
    number = mine.shape[0] // side
    for f in range(2 * number):
        ref, at = (mine, f) if f < number else (theirs, f - number)
        strips_of(ref.at[at * side : (at + 1) * side], strips.at[f])
    total = from_three(mine[number * side :, :128]) + from_three(theirs[number * side :, :128])
    for d, out in enumerate(outs):
        value = None
        for f in range(2 * number):
            term = scale[d, f] * strips[f].astype(f32)
            value = term if value is None else value + term
        out[: 4 * border] = value.astype(bf16)
        out[4 * border :] = jnp.zeros((32, side), bf16)
        out[4 * border :, :128] = in_three(total)


def mixed(mine, theirs, scale, strips):
    side = mine.shape[1]
    rows = 4 * border + 32 if strips else side
    kept = [pltpu.VMEM((scale.shape[1], 4 * border, side), bf16)] if strips else []
    return pl.pallas_call(
        mix_strips_kernel if strips else mix_kernel,
        in_specs=[scalar, whole, whole],
        out_specs=[whole] * scale.shape[0],
        out_shape=[jax.ShapeDtypeStruct((rows, side), bf16)] * scale.shape[0],
        scratch_shapes=kept,
        compiler_params=pltpu.CompilerParams(vmem_limit_bytes=vmem),
        name="mixed",
    )(scale, mine, theirs)


def chip_shift(x, hop):
    size = lax.axis_size("gy")
    return lax.ppermute(x, "gy", [(i, (i + 2 * hop) % size) for i in range(size)])


def swapped(x):
    return lax.ppermute(x, "gy", [(i, i ^ 1) for i in range(lax.axis_size("gy"))])


def body(
    xi_coarse,
    xi_middle,
    xi_fine,
    coef_middle,
    coef_fine,
    kern_u,
    kern_v,
    vis_data,
    facet_tiles,
    facet_weight,
    facet_count,
):
    fields = (xi_coarse, coef_middle, xi_middle, coef_fine, xi_fine)
    right, left = neighbours("gy")
    down, up = neighbours("gx")
    sides = halo_sides(xi_coarse, xi_middle, coef_middle)
    left_in = lax.ppermute(sides[1], "gy", right)
    right_in = lax.ppermute(sides[0], "gy", left)
    (first,) = sky_of(None, *fields)
    first, left_in, right_in, around, listed = lax.optimization_barrier(
        (
            first,
            left_in,
            right_in,
            (xi_coarse, xi_middle, coef_middle),
            (facet_tiles[0], facet_weight[0], facet_count[0]),
        )
    )
    lists, weights, counts = listed
    size = lax.axis_size("gy")
    chips = size // 2
    me = lax.axis_index("gy")
    ids = jnp.arange(size, dtype=jnp.int32)
    mixing = jnp.sum(
        weights[:, :, None] * (lists[:, :, None] == ids[None, None, :]).astype(f32), axis=1
    )
    order = 2 * ((me // 2 + jnp.arange(chips, dtype=jnp.int32)) % chips) + me % 2
    scale = jnp.concatenate([mixing, swapped(mixing)])[:, order].T
    sel = (me // 2 - lists // 2) % chips + jnp.where(lists % 2 == me % 2, 0, chips)
    ints = jnp.concatenate([sel, counts[:, None]], axis=1)
    hops = range(1, chips)
    early = range(1, min(3, chips))
    mine = {hop: chip_shift(first, hop) for hop in early}
    above, below = halo_rows(*around, left_in, right_in)
    sky, strips, squares, lefts, rights = sky_of((above, below, left_in, right_in, *sides), *fields)
    strips = jnp.concatenate([chip_shift(strips, hop) for hop in early])
    late = {hop: chip_shift(sky, hop) for hop in hops[len(early) :]}
    strips, mine, scale, ints, weights = lax.optimization_barrier(
        (strips, mine, scale, ints, weights)
    )
    mine |= late
    mine = [sky] + [mine[hop] for hop in hops]
    tiles = mine + [swapped(tile) for tile in mine]
    strips = [strips, swapped(strips)]
    dsums = facets(tiles, strips, kern_u, kern_v, vis_data, ints, weights, squares)
    theirs = swapped(dsums)
    strips = mixed(dsums, theirs, scale, True)
    strips, dsums, theirs = lax.optimization_barrier((strips, dsums, theirs))
    edges = [strips[0]] + [chip_shift(strips[hop], hop) for hop in hops]
    parts = mixed(dsums, theirs, scale, False)
    edges, _ = lax.optimization_barrier((edges, parts))
    parts = [parts[0]] + [chip_shift(parts[hop], hop) for hop in hops]
    around = (above, below, lefts, rights)
    to_left, to_right, upper, lower, total = adjoint(True, edges, around, fields)
    size = lax.axis_size("gx")
    steps = [1 << i for i in range(size.bit_length()) if 1 << i < size]

    def across(x, hop):
        return lax.ppermute(x, "gx", [(i, i ^ hop) for i in range(size)])

    from_below = lax.ppermute(upper, "gx", up)
    from_above = lax.ppermute(lower, "gx", down)
    other = across(total, steps[0])
    rows, cols = xi_coarse.shape
    to_left, to_right, total = pl.pallas_call(
        functools.partial(corners_kernel, rows, cols),
        in_specs=[whole] * 6,
        out_specs=[whole] * 3,
        out_shape=[shape(*to_left.shape), shape(*to_right.shape), shape(8, 128)],
        name="corners",
    )(to_left, to_right, from_above, from_below, total, other)
    for hop in steps[1:-1]:
        total += across(total, hop)
    other = across(total, steps[-1])
    from_left = lax.ppermute(to_right, "gy", right)
    from_right = lax.ppermute(to_left, "gy", left)
    parts, from_left, from_right, other = lax.optimization_barrier(
        (parts, from_left, from_right, other)
    )
    cells = size * lax.axis_size("gy") * 16 * rows * cols
    arrived = (from_left, from_right, from_above, from_below, total, other)
    grad_fine, grad_middle, grad_coarse, total = adjoint(
        False, parts, around, fields, arrived, cells
    )
    return grad_coarse, grad_middle, grad_fine, total.reshape(())


def solution(mesh):
    placed = (
        P("gx", "gy"),
        P("gx", "gy"),
        P("gx", "gy"),
        P(None, None, "gx", "gy"),
        P(None, None, "gx", "gy"),
        P("gx", "gy", None, None),
        P("gx", "gy", None, None),
        P("gx", "gy", None, None),
        P("gx", "gy", None),
        P("gx", "gy", None),
        P("gx", "gy"),
    )
    return jax.shard_map(
        body,
        mesh=mesh,
        in_specs=placed,
        out_specs=(P("gx", "gy"), P("gx", "gy"), P("gx", "gy"), P()),
        check_vma=False,
    )
```

```python
import functools

import jax
import jax.numpy as jnp
from jax import lax
from jax.experimental import pallas as pl
from jax.experimental.pallas import tpu as pltpu
from jax.sharding import PartitionSpec as P

inv_noise = 0.125
long_work = pl.CostEstimate(flops=40_000_000_000, transcendentals=0, bytes_accessed=64_000_000)
border = 8
vmem = 32 * 1024 * 1024
f32 = jnp.float32
bf16 = jnp.bfloat16


def halves(x):
    high = x.astype(bf16)
    return high, (x - high.astype(f32)).astype(bf16)


def interleaver(cols, transposed):
    shape = (2 * cols, 2 * cols)
    split = lax.broadcasted_iota(jnp.int32, shape, 1 if transposed else 0)
    whole = lax.broadcasted_iota(jnp.int32, shape, 0 if transposed else 1)
    place = jnp.where(split >= cols, 2 * (split - cols) + 1, 2 * split)
    return (place == whole).astype(f32).astype(bf16)


def folded(x):
    rows, cols = x.shape
    x = jnp.sum(x.reshape(rows // 8, 8, cols), axis=0)
    return sum(x[:, i : i + 128] for i in range(0, cols, 128))


def row_of(ref, i):
    return ref[i : i + 1, :]


def dot_t(x, y, dims):
    return lax.dot_general(x, y, (dims, ((), ())), preferred_element_type=f32)


def moved(x, perm):
    high, low = halves(x)
    return jnp.dot(high, perm, preferred_element_type=f32) + jnp.dot(
        low, perm, preferred_element_type=f32
    )


def ends_placed(first, last, cols):
    rows = jnp.concatenate([first, first, last, last, jnp.zeros((4, first.shape[1]), f32)])
    high = rows.astype(bf16).astype(f32)
    index = lax.broadcasted_iota(jnp.int32, rows.shape, 0)
    rows = jnp.where(index % 2 == 0, high, rows - high).astype(bf16)
    shape = (8, cols)
    index = lax.broadcasted_iota(jnp.int32, shape, 0)
    lane = lax.broadcasted_iota(jnp.int32, shape, 1)
    place = ((index < 2) & (lane == 0)) | ((index >= 2) & (index < 4) & (lane == cols - 1))
    return dot_t(rows, place.astype(f32).astype(bf16), ((0,), (0,)))


def weighed(win, coef_ref, perm, lhs, mix, rows, cols, chunks=()):
    def part(i, carry):
        r0 = pl.multiple_of(i * 16, 16)
        total = [jnp.zeros((16, cols), f32) for _ in range(4)]
        for near in range(9):
            w = win[near, pl.ds(r0, 16), :]
            for child in range(4):
                total[child] += coef_ref[child, near, pl.ds(r0, 16), :].astype(f32) * w
        for child in range(4):
            a, b = child // 2, child % 2
            high, low = halves(total[child])
            lhs[pl.ds(2 * a * rows + r0, 16), b * cols : (b + 1) * cols] = high
            lhs[pl.ds((2 * a + 1) * rows + r0, 16), b * cols : (b + 1) * cols] = low
        return carry

    in_chunks(part, rows, chunks)
    field = jnp.dot(lhs[...], perm[...], preferred_element_type=f32)
    for tile in range(2 * cols // 128):
        lanes = slice(tile * 128, (tile + 1) * 128)
        for a in range(2):
            mix[tile, pl.ds(a, rows, stride=2), :] = (
                field[2 * a * rows : (2 * a + 1) * rows, lanes]
                + field[(2 * a + 1) * rows : (2 * a + 2) * rows, lanes]
            )


def fetched(pairs, sems, first=0):
    copies = [
        pltpu.make_async_copy(src, dst, sems.at[first + i]) for i, (src, dst) in enumerate(pairs)
    ]
    for copy in copies:
        copy.start()
    return copies


def chunked(source, target, sems):
    number, rows = sems.shape[0], source.shape[2] // sems.shape[0]
    copies = []
    for i in range(number):
        at = slice(i * rows, (i + 1) * rows)
        copies.append(pltpu.make_async_copy(source.at[:, :, at], target.at[:, :, at], sems.at[i]))
        copies[i].start()
    return copies


def in_chunks(part, rows, chunks):
    steps = rows // 16
    if not chunks:
        lax.fori_loop(0, steps, part, 0)
    for i, copy in enumerate(chunks):
        copy.wait()
        lax.fori_loop(i * steps // len(chunks), (i + 1) * steps // len(chunks), part, 0)


def columns_beside(field, left, right):
    rows, cols = field.shape[1:]
    placed = ends_placed(left, right, cols)
    lane = lax.broadcasted_iota(jnp.int32, (rows, cols), 1)
    here = field[1]
    field[0] = jnp.where(lane == 0, placed, pltpu.roll(here, 1, 1))
    field[2] = jnp.where(lane == cols - 1, placed, pltpu.roll(here, cols - 1, 1))


def strips_of(tile, out):
    rows, cols = tile.shape
    first, last = tile[: 2 * border].astype(f32), tile[rows - 2 * border :].astype(f32)
    out[: 2 * border] = jnp.concatenate([first[:border], last[border:]]).astype(bf16)
    index = lax.broadcasted_iota(jnp.int32, (2 * border, cols), 0)
    lane = lax.broadcasted_iota(jnp.int32, (2 * border, cols), 1)
    pick = lane == jnp.where(index < border, index, index + cols - 2 * border)
    pick = pick.astype(f32).astype(bf16)
    out[2 * border : 4 * border] = dot_t(pick, tile[...], ((1,), (1,))).astype(bf16)


def columns_of(strip):
    index = lax.broadcasted_iota(jnp.int32, (2 * border, 128), 0)
    lane = lax.broadcasted_iota(jnp.int32, (2 * border, 128), 1)
    out = []
    for place in (
        (index < border) & (lane == index),
        (index >= border) & (lane == index + 128 - 2 * border),
    ):
        out.append(dot_t(strip, place.astype(f32).astype(bf16), ((0,), (0,))))
    return out


def stretch(out, side, over, under, b, lane, first):
    rows = side.shape[1]
    out[...] = jnp.zeros_like(out)
    out[:, 2 : rows + 2] = side[...]
    out[9:18, 1:2] = over[9 * b : 9 * b + 9, lane : lane + 1]
    out[21:22, 1:2] = over[20 + b : 21 + b, lane : lane + 1]
    out[0:9, rows + 2 : rows + 3] = under[9 * b : 9 * b + 9, lane : lane + 1]
    out[20:21, rows + 2 : rows + 3] = under[20 + b : 21 + b, lane : lane + 1]
    for k in range(2):
        at = slice(first + k, first + k + 1)
        for i in range(2):
            out[18 + k : 19 + k, i : i + 1] = over[18 + i : 19 + i, at]
            end = rows + 2 + i
            out[18 + k : 19 + k, end : end + 1] = under[18 + i : 19 + i, at]


def sky_kernel(alone, *refs):
    count = 5 if alone else 11
    sources, refs = refs[:count], refs[count:]
    outs, refs = (refs[:1], refs[1:]) if alone else (refs[:5], refs[5:])
    held, rest = refs[:11], refs[11:]
    win, perm, lhs, mix, near_coarse, shifted, fine_win, fine_perm, fine_lhs, fine_mix = rest[:10]
    lefts, rights, to_left, to_right, sems, chunk_sems = rest[10:]
    sky_ref = outs[0]
    if alone:
        for ref in held[1:7]:
            ref[...] = jnp.zeros_like(ref)
        held_here = (held[0], *held[7:])
    else:
        held_here = held
    copies = fetched(zip(sources[:-2], held_here[:-2]), sems)
    chunks = chunked(sources[-2], held_here[-2], chunk_sems)
    copies += fetched(zip(sources[-1:], held_here[-1:]), sems, len(copies))
    xi_coarse, over, under, left_in, right_in, left_side, right_side = held[:7]
    coef_middle, xi_middle, coef_fine, xi_fine = held[7:]
    rows, cols = win.shape[1:]
    perm[...] = interleaver(cols, False)
    fine_perm[...] = interleaver(2 * cols, False)
    near_coarse[...] = jnp.zeros_like(near_coarse)
    for copy in copies[:-2]:
        copy.wait()
    above, below = over[:, 2 : cols + 2], under[:, 2 : cols + 2]
    if alone:
        for ref in (lefts, rights):
            ref[...] = jnp.zeros_like(ref)
    else:
        stretch(lefts, left_in, over, under, 1, 1, 0)
        stretch(rights, right_in, over, under, 0, cols + 2, cols + 2)
        stretch(to_left, left_side, over, under, 0, 2, 2)
        stretch(to_right, right_side, over, under, 1, cols + 1, cols)
    near_coarse[1, 6:8] = above[18:20]
    near_coarse[1, 8 : 8 + rows] = xi_coarse[...]
    near_coarse[1, 8 + rows : 10 + rows] = below[18:20]
    pad = jnp.zeros((1, 6), f32)
    beside = [
        jnp.concatenate([pad, row_of(x, i)[:, : rows + 4], pad], axis=1)
        for x, i in ((lefts, 19), (rights, 18))
    ]
    columns_beside(near_coarse, *beside)
    for near in range(9):
        r, c = near // 3, near % 3
        win[near] = near_coarse[c, 7 + r : 7 + r + rows]
    weighed(win, coef_middle, perm, lhs, mix, rows, cols)

    def across(message, top):
        out = []
        for b in range(2):
            line = row_of(message, 20 + b)
            for near in range(9):
                r, c = near // 3, near % 3
                line += row_of(message, 9 * b + near) * near_coarse[c, top + r : top + r + 1]
            out.append(line)
        return jnp.concatenate(out, axis=1)

    def along(message, fields):
        out = []
        for a in range(2):
            line = row_of(message, 20 + a)[:, 1 : rows + 3]
            for near in range(9):
                r, c = near // 3, near % 3
                line += row_of(message, 9 * a + near)[:, 1 : rows + 3] * fields[c][:, r : r + rows + 2]
            out.append(line)
        inner = jnp.concatenate([line[:, 1 : rows + 1] for line in out], axis=1)
        return inner, out[1][:, :1], out[0][:, rows + 1 :]

    if alone:
        empty = jnp.zeros((1, 1), f32)
        top = bottom = left = right = jnp.zeros((1, 2 * cols), f32)
        top_left = bottom_left = top_right = bottom_right = empty
    else:
        top, bottom = across(above, 6), across(below, rows + 7)
        left, top_left, bottom_left = along(
            lefts, [row_of(lefts, 18), row_of(lefts, 19), row_of(to_left, 18)]
        )
        right, top_right, bottom_right = along(
            rights, [row_of(to_right, 19), row_of(rights, 18), row_of(rights, 19)]
        )
    lines = jnp.concatenate([top, bottom, left, right, jnp.zeros((4, 2 * cols), f32)])
    lines = moved(lines, perm[...])
    copies[-2].wait()
    xi = xi_middle[...]
    last = 8 + 2 * rows
    shifted[1] = jnp.zeros(shifted.shape[1:], f32)
    for tile in range(2 * cols // 128):
        lanes = slice(tile * 128, (tile + 1) * 128)
        shifted[1, 8:last, lanes] = mix[tile] + xi[:, lanes]
    shifted[1, 7:8, :] = lines[0:1]
    shifted[1, last : last + 1, :] = lines[1:2]
    pad = jnp.zeros((1, 7), f32)
    beside = [
        jnp.concatenate([pad, first, line, final, pad], axis=1)
        for first, line, final in (
            (top_left, lines[2:3], bottom_left),
            (top_right, lines[3:4], bottom_right),
        )
    ]
    columns_beside(shifted, *beside)
    for near in range(9):
        r, c = near // 3, near % 3
        fine_win[near] = shifted[c, 7 + r : 7 + r + 2 * rows, :]
    weighed(fine_win, coef_fine, fine_perm, fine_lhs, fine_mix, 2 * rows, 2 * cols, chunks)
    copies[-1].wait()
    for tile in range(4 * cols // 128):
        lanes = slice(tile * 128, (tile + 1) * 128)
        sky_ref[:, lanes] = (fine_mix[tile] + xi_fine[:, lanes]).astype(bf16)
    if alone:
        return
    strips_ref, sq_ref, lefts_ref, rights_ref = outs[1:]
    lefts_ref[...] = lefts[...]
    rights_ref[...] = rights[...]
    strips_of(sky_ref, strips_ref)
    sq_ref[...] = (
        folded(win[4] * win[4]) + folded(xi * xi) + folded(xi_fine[...] * xi_fine[...])
    )


def sides_kernel(left_in, right_in, first_side, last_side, to_above, to_below):
    rows = left_in.shape[1]
    stretch(to_above, first_side, left_in, right_in, 0, 0, 0)
    stretch(to_below, last_side, left_in, right_in, 1, rows - 1, rows - 2)


def neighbours(axis):
    size = lax.axis_size(axis)
    ahead = [(i, i + 1) for i in range(size - 1)]
    return ahead, [(j, i) for i, j in ahead]


def halo_sides(xi_coarse, xi_middle, coef_middle):
    rows, cols = xi_coarse.shape

    def inside(b, col, near):
        return jnp.concatenate(
            [
                coef_middle[b::2, :, :, col].reshape(18, rows).astype(f32),
                near.T,
                xi_middle[:, 2 * col + b].reshape(rows, 2).T,
            ]
        )

    return inside(0, 0, xi_coarse[:, :2]), inside(1, cols - 1, xi_coarse[:, -2:])


def halo_rows(xi_coarse, xi_middle, coef_middle, left_in, right_in):
    rows, cols = xi_coarse.shape

    def edge(a, row, near):
        return jnp.concatenate(
            [
                coef_middle[2 * a : 2 * a + 2, :, row].reshape(18, cols).astype(f32),
                near,
                xi_middle[2 * row + a].reshape(cols, 2).T,
            ]
        )

    to_above, to_below = pl.pallas_call(
        sides_kernel,
        in_specs=[whole] * 4,
        out_specs=[whole] * 2,
        out_shape=[jax.ShapeDtypeStruct((22, cols + 4), f32)] * 2,
        cost_estimate=long_work,
        name="sides",
    )(left_in, right_in, edge(0, 0, xi_coarse[:2]), edge(1, rows - 1, xi_coarse[-2:]))
    down, up = neighbours("gx")
    return lax.ppermute(to_below, "gx", down), lax.ppermute(to_above, "gx", up)


whole = pl.BlockSpec(memory_space=pltpu.VMEM)
scalar = pl.BlockSpec(memory_space=pltpu.SMEM)
anywhere = pl.BlockSpec(memory_space=pltpu.HBM)


def sky_of(halos, xi_coarse, coef_middle, xi_middle, coef_fine, xi_fine):
    rows, cols = coef_middle.shape[2:]
    alone = halos is None
    given = (coef_middle, xi_middle, coef_fine, xi_fine)
    operands = (xi_coarse, *given) if alone else (xi_coarse, *halos, *given)
    message = [(22, cols + 4)] * 2 + [(22, rows)] * 4
    return pl.pallas_call(
        functools.partial(sky_kernel, alone),
        in_specs=[anywhere] * len(operands),
        out_specs=[whole] * (1 if alone else 5),
        out_shape=[
            jax.ShapeDtypeStruct((4 * rows, 4 * cols), bf16),
            jax.ShapeDtypeStruct((4 * border, 4 * cols), bf16),
            jax.ShapeDtypeStruct((8, 128), f32),
            jax.ShapeDtypeStruct((22, rows + 4), f32),
            jax.ShapeDtypeStruct((22, rows + 4), f32),
        ][: 1 if alone else 5],
        scratch_shapes=[pltpu.VMEM(xi_coarse.shape, f32)]
        + [pltpu.VMEM(shape, f32) for shape in message]
        + [pltpu.VMEM(x.shape, x.dtype) for x in given]
        + [
            pltpu.VMEM((9, rows, cols), f32),
            pltpu.VMEM((2 * cols, 2 * cols), bf16),
            pltpu.VMEM((4 * rows, 2 * cols), bf16),
            pltpu.VMEM((2 * cols // 128, 2 * rows, 128), f32),
            pltpu.VMEM((3, rows + 16, cols), f32),
            pltpu.VMEM((3, 2 * rows + 16, 2 * cols), f32),
            pltpu.VMEM((9, 2 * rows, 2 * cols), f32),
            pltpu.VMEM((4 * cols, 4 * cols), bf16),
            pltpu.VMEM((8 * rows, 4 * cols), bf16),
            pltpu.VMEM((4 * cols // 128, 4 * rows, 128), f32),
            *[pltpu.VMEM((22, rows + 4), f32) for _ in range(4)],
            pltpu.SemaphoreType.DMA((11,)),
            pltpu.SemaphoreType.DMA((4,)),
        ],
        compiler_params=pltpu.CompilerParams(vmem_limit_bytes=60 * 1024 * 1024),
        name="sky",
    )(*operands)


def spread(mix, coef_ref, terms, rows, cols, chunks=()):
    def part(i, carry):
        r0 = pl.multiple_of(i * 16, 16)
        quads = []
        for a in range(2):
            for b in range(2):
                tiles = range(b * cols // 128, (b + 1) * cols // 128)
                lines = [mix[t, pl.ds(2 * r0 + a, 16, stride=2), :] for t in tiles]
                quads.append(jnp.concatenate(lines, axis=1))
        for near in range(9):
            total = jnp.zeros((16, cols), f32)
            for child in range(4):
                total += coef_ref[child, near, pl.ds(r0, 16), :].astype(f32) * quads[child]
            terms[near, pl.ds(16 + r0, 16), :] = total
        return carry

    in_chunks(part, rows, chunks)


def row_sums(terms, rowed):
    rows = terms.shape[1] - 32
    for near in range(9):
        terms[near, :16] = jnp.zeros((16, terms.shape[2]), f32)
        terms[near, rows + 16 :] = jnp.zeros((16, terms.shape[2]), f32)
    for c in range(3):
        total = terms[c, 9 : rows + 25]
        for r in (1, 2):
            total += terms[3 * r + c, 9 - r : rows + 25 - r]
        rowed[c, : rows + 16] = total
        rowed[c, rows + 16 :] = jnp.zeros((rowed.shape[1] - rows - 16, rowed.shape[2]), f32)


def joined(rowed, cols):
    lane = lax.broadcasted_iota(jnp.int32, rowed.shape[1:], 1)
    main = (
        rowed[1]
        + jnp.where(lane == 0, 0.0, pltpu.roll(rowed[2], 1, 1))
        + jnp.where(lane == cols - 1, 0.0, pltpu.roll(rowed[0], cols - 1, 1))
    )
    lane = lax.broadcasted_iota(jnp.int32, (8, cols), 1)
    outside = []
    for c, col in ((0, 0), (2, cols - 1)):
        pick = (lane == col).astype(f32).astype(bf16)
        high, low = halves(rowed[c])
        out = dot_t(pick, high, ((1,), (1,))) + dot_t(pick, low, ((1,), (1,)))
        outside.append(out[:1])
    return main, outside[0], outside[1]


def adjoint_kernel(edge, number, cells, *refs):
    count = 6 if edge else 15
    written = 5 if edge else 4
    count += number
    sources, outs, refs = refs[:count], refs[count : count + written], refs[count + written :]
    parts, held, rest = refs[:number], refs[number:count], refs[count:]
    fine_perm, fine_mix, fine_terms, fine_rowed, perm, mix, terms, rowed, full, sems, chunk_sems, out_sem = rest
    arriving = fetched(zip(sources[:number], parts), sems)
    chunks = chunked(sources[number], held[0], chunk_sems)
    copies = [None] + fetched(zip(sources[number + 1 :], held[1:]), sems, number)
    coef_fine, coef_middle, over, under, lefts, rights = held[:6]
    if edge:
        left_ref, right_ref, upper_ref, lower_ref, total_ref = outs
    else:
        grad_ref, middle_ref, coarse_ref, total_ref = outs
        xi_fine, xi_middle, xi_coarse, from_left, from_right, from_above, from_below = held[6:13]
        total, other = held[13:]
    rows, cols = terms.shape[1] - 32, terms.shape[2]
    fine_perm[...] = interleaver(2 * cols, True)
    perm[...] = interleaver(cols, True)
    for copy in arriving:
        copy.wait()
    g = parts[0][...].astype(f32)
    for part in parts[1:]:
        g += part[...].astype(f32)
    if edge:
        tail = g[4 * border :, :128]
        total_ref[...] = tail[:8] + tail[8:16] + tail[16:24]
        high, low = halves(g[2 * border : 4 * border])
        left, right = [x + y for x, y in zip(columns_of(high), columns_of(low))]
        full[...] = jnp.zeros_like(full)
        full[:, :128] = left
        full[:, 4 * cols - 128 :] = right
        full[:border] = g[:border]
        full[4 * rows - border :] = g[border : 2 * border]
        g = full[...]
    else:
        copies[6].wait()
        full[...] = g + xi_fine[...]
        leaving = pltpu.make_async_copy(full, grad_ref, out_sem)
        leaving.start()
    split = moved(g, fine_perm[...])
    for tile in range(4 * cols // 128):
        fine_mix[tile] = split[:, tile * 128 : (tile + 1) * 128]
    spread(fine_mix, coef_fine, fine_terms, 2 * rows, 2 * cols, chunks)
    row_sums(fine_terms, fine_rowed)
    main, left, right = joined(fine_rowed, 2 * cols)
    last = 8 + 2 * rows
    inner = main[8:last]
    for copy in copies[1:6] + copies[7:]:
        copy.wait()
    above, below = over[:, 2 : cols + 2], under[:, 2 : cols + 2]
    if not edge:
        line = slice(1, 2 * rows + 1)
        middle_ref[...] = (
            inner
            + xi_middle[...]
            + ends_placed(from_left[2:3, line], from_right[2:3, line], 2 * cols)
        )
        middle_ref[:1] += from_above[2:3, 1 : 2 * cols + 1]
        middle_ref[2 * rows - 1 :] += from_below[2:3, 1 : 2 * cols + 1]
    split = moved(inner, perm[...])
    for tile in range(2 * cols // 128):
        mix[tile] = split[:, tile * 128 : (tile + 1) * 128]
    spread(mix, coef_middle, terms, rows, cols)
    ring_above, ring_below = main[7:8], main[last : last + 1]
    lines = [ring_above, ring_below, left[:, 8:last], right[:, 8:last]]
    lines = moved(jnp.concatenate(lines + [jnp.zeros((4, 2 * cols), f32)]), perm[...])
    row_sums(terms, rowed)
    for line, message, top in ((0, above, 6), (1, below, 7 + rows)):
        for near in range(9):
            r, c = near // 3, near % 3
            term = row_of(message, near) * lines[line : line + 1, :cols]
            term += row_of(message, 9 + near) * lines[line : line + 1, cols:]
            rowed[c, top + r : top + r + 1, :] += term

    def along(line, ends, message):
        empty = jnp.zeros((1, 1), f32)
        first = [empty, lines[line : line + 1, :rows], ends[:, last : last + 1]]
        second = [ends[:, 7:8], lines[line : line + 1, cols : cols + rows], empty]
        first, second = jnp.concatenate(first, axis=1), jnp.concatenate(second, axis=1)
        out = []
        for c in range(3):
            total = jnp.zeros((1, rows + 4), f32)
            for r in range(3):
                near = 3 * r + c
                term = row_of(message, near)[:, 1 : rows + 3] * first
                term += row_of(message, 9 + near)[:, 1 : rows + 3] * second
                pads = [jnp.zeros((1, n), f32) for n in (r, 2 - r) if n]
                pieces = [term] + pads if r == 0 else pads[:1] + [term] + pads[1:]
                total += jnp.concatenate(pieces, axis=1)
            out.append(total)
        return out

    outer_left = along(2, left, lefts)
    outer_right = along(3, right, rights)
    main, near_left, near_right = joined(rowed, cols)
    if not edge:
        line = slice(2, rows + 2)
        first = outer_left[2][:, line] + from_left[1:2, line]
        last = outer_right[0][:, line] + from_right[1:2, line]
        second = ends_placed(from_left[0:1, line], from_right[0:1, line], cols)
        lane = lax.broadcasted_iota(jnp.int32, second.shape, 1)
        second = jnp.where(lane == 1, pltpu.roll(second, 1, 1), 0.0) + jnp.where(
            lane == cols - 2, pltpu.roll(second, cols - 1, 1), 0.0
        )
        coarse_ref[...] = (
            main[8 : 8 + rows] + xi_coarse[...] + ends_placed(first, last, cols) + second
        )
        coarse_ref[:2] += from_above[0:2, 2 : cols + 2]
        coarse_ref[rows - 2 :] += from_below[0:2, 2 : cols + 2]
        both = total[...] + other[...]
        both = jnp.sum(jnp.sum(both, axis=1, keepdims=True), axis=0, keepdims=True)
        total_ref[...] = both * (1.0 / cells)
        leaving.wait()
        return
    sides = []
    for ref, far, close, beyond, ends in (
        (left_ref, outer_left[0], outer_left[1], near_left, left),
        (right_ref, outer_right[2], outer_right[1], near_right, right),
    ):
        close += beyond[:, 6 : rows + 10]
        ends = ends[:, 7 : 2 * rows + 9]
        ref[...] = jnp.zeros_like(ref)
        ref[0:1, : rows + 4] = far
        ref[1:2, : rows + 4] = close
        ref[2:3, : 2 * rows + 2] = ends
        sides.append((far, close, ends))
    lane = lax.broadcasted_iota(jnp.int32, (1, cols), 1)
    (far_left, close_left, ends_left), (far_right, close_right, ends_right) = sides
    for ref, first, line, end in (
        (upper_ref, 6, ring_above, 0),
        (lower_ref, 8 + rows, ring_below, 2 * rows + 1),
    ):
        ref[...] = jnp.zeros_like(ref)
        for i in range(2):
            at = slice(first - 6 + i, first - 5 + i)
            inner = (
                main[first + i : first + i + 1]
                + jnp.where(lane == 0, outer_left[2][:, at], 0.0)
                + jnp.where(lane == cols - 1, outer_right[0][:, at], 0.0)
            )
            pieces = [far_left[:, at], close_left[:, at], inner, close_right[:, at], far_right[:, at]]
            ref[i : i + 1, : cols + 4] = jnp.concatenate(pieces, axis=1)
        pieces = [ends_left[:, end : end + 1], line, ends_right[:, end : end + 1]]
        ref[2:3, : 2 * cols + 2] = jnp.concatenate(pieces, axis=1)


def corners_kernel(rows, cols, left, right, from_above, from_below, total, other, left_out, right_out, total_out):
    for ref, out, far, close, end in (
        (left, left_out, 0, 1, 0),
        (right, right_out, cols + 3, cols + 2, 2 * cols + 1),
    ):
        out[...] = ref[...]
        for rows_in, first, line in ((from_above, 2, 1), (from_below, rows, 2 * rows)):
            for i in range(2):
                at = slice(first + i, first + i + 1)
                out[0:1, at] += rows_in[i : i + 1, far : far + 1]
                out[1:2, at] += rows_in[i : i + 1, close : close + 1]
            out[2:3, line : line + 1] += rows_in[2:3, end : end + 1]
    total_out[...] = total[...] + other[...]


def shape(*dims):
    return jax.ShapeDtypeStruct(dims, f32)


def adjoint(edge, parts, sides, fields, arrived=(), cells=0):
    rows, cols = fields[1].shape[2:]
    xi_coarse, coef_middle, xi_middle, coef_fine, xi_fine = fields
    wide = 2 * rows + 128
    operands = (coef_fine, coef_middle, *sides)
    if edge:
        outs = [shape(8, wide)] * 2 + [shape(8, 2 * cols + 128)] * 2 + [shape(8, 128)]
    else:
        operands += (xi_fine, xi_middle, xi_coarse, *arrived)
        outs = [shape(4 * rows, 4 * cols), shape(2 * rows, 2 * cols), shape(rows, cols)]
        outs += [shape(1, 1)]
    return pl.pallas_call(
        functools.partial(adjoint_kernel, edge, len(parts), cells),
        in_specs=[anywhere] * (len(parts) + len(operands)),
        out_specs=[whole] * 5 if edge else [anywhere, whole, whole, whole],
        out_shape=outs,
        scratch_shapes=[pltpu.VMEM(x.shape, x.dtype) for x in (*parts, *operands)]
        + [
            pltpu.VMEM((4 * cols, 4 * cols), bf16),
            pltpu.VMEM((4 * cols // 128, 4 * rows, 128), f32),
            pltpu.VMEM((9, 2 * rows + 32, 2 * cols), f32),
            pltpu.VMEM((3, 2 * rows + 128, 2 * cols), f32),
            pltpu.VMEM((2 * cols, 2 * cols), bf16),
            pltpu.VMEM((2 * cols // 128, 2 * rows, 128), f32),
            pltpu.VMEM((9, rows + 32, cols), f32),
            pltpu.VMEM((3, rows + 128, cols), f32),
            pltpu.VMEM((4 * rows, 4 * cols), f32),
            pltpu.SemaphoreType.DMA((len(parts) + len(operands),)),
            pltpu.SemaphoreType.DMA((4,)),
            pltpu.SemaphoreType.DMA,
        ],
        compiler_params=pltpu.CompilerParams(vmem_limit_bytes=60 * 1024 * 1024),
        cost_estimate=long_work if edge else None,
        name="adjoint",
    )(*parts, *operands)


def in_three(x):
    high = x.astype(bf16).astype(f32)
    middle = (x - high).astype(bf16).astype(f32)
    return jnp.concatenate([high, middle, x - high - middle, jnp.zeros_like(x)]).astype(bf16)


def from_three(x):
    x = x.astype(f32)
    return x[:8] + x[8:16] + x[16:24]


def facets_kernel(blk, given, ints, weights, *refs):
    number, slots = weights.shape
    tiles, strips, rest = refs[:given], refs[given : given + 2], refs[given + 2 :]
    height = 4 * border
    kinds = strips[0].shape[0] // height
    ku_hbm, kv_hbm, data_hbm, squares, out_ref = rest[:5]
    held, held_strips, ku, kv, data, sums, dsum, total, sems, tile_sems, strip_sems = rest[5:]
    bins, side = ku.shape[1:]

    def inputs(f):
        for s in range(slots):
            for i, tile in enumerate(tiles):

                @pl.when(ints[f, s] == i)
                def _():
                    pltpu.make_async_copy(tile, held.at[f, s], tile_sems.at[f, s]).start()

            for i in range(2 * kinds):

                @pl.when(ints[f, slots + 1 + s] == i + 1)
                def _():
                    first = i % kinds * height
                    strip = strips[i // kinds].at[first : first + height]
                    pltpu.make_async_copy(strip, held_strips.at[f, s], strip_sems.at[f, s]).start()

        pairs = ((ku_hbm, ku), (kv_hbm, kv), (data_hbm, data))
        copies = [
            pltpu.make_async_copy(src.at[0, f], dst.at[f], sems.at[f, i])
            for i, (src, dst) in enumerate(pairs)
        ]
        for copy in copies:
            copy.start()
        return copies

    def patch(f, s):
        @pl.when(ints[f, slots + 1 + s] > 0)
        def _():
            strip = strips[0].at[:height]
            pltpu.make_async_copy(strip, held_strips.at[f, s], strip_sems.at[f, s]).wait()
            tile, strip = held.at[f, s], held_strips.at[f, s]
            lines = strip[: 2 * border].astype(f32)
            top, bottom = tile[: 2 * border].astype(f32), tile[side - 2 * border :].astype(f32)
            tile[: 2 * border] = jnp.concatenate([lines[:border], top[border:]]).astype(bf16)
            tile[side - 2 * border :] = jnp.concatenate([bottom[:border], lines[border:]]).astype(
                bf16
            )
            lane = lax.broadcasted_iota(jnp.int32, (side, 128), 1)
            left, right = columns_of(strip[2 * border :])
            for cells, inside, start in (
                (left, lane < border, 0),
                (right, lane >= 128 - border, side - 128),
            ):
                here = tile[:, start : start + 128].astype(f32)
                tile[:, start : start + 128] = jnp.where(inside, cells, here).astype(bf16)

    def work(f, step):
        rows = slice(step * blk, (step + 1) * blk)
        count = ints[f, slots] - step * blk

        @pl.when(count > 0)
        def _():
            amp = jnp.dot(ku[f, rows], sums[...], preferred_element_type=f32).astype(bf16)
            vis = dot_t(amp, kv[f], ((1,), (1,)))
            live = lax.broadcasted_iota(jnp.int32, vis.shape, 0) < count
            resid = jnp.where(live, vis - data[f, rows].astype(f32), 0.0)
            total[...] += 0.5 * inv_noise * folded(resid * resid)
            dvis = (inv_noise * resid).astype(bf16)
            damp = jnp.dot(dvis, kv[f], preferred_element_type=f32).astype(bf16)
            part = dot_t(ku[f, rows], damp, ((0,), (0,)))
            if step == 0:
                dsum[...] = part
            else:
                dsum[...] += part

    copies = [inputs(0)]
    total[...] = 0.5 * squares[...]
    for f in range(number):
        for s in range(slots):
            pltpu.make_async_copy(tiles[0], held.at[f, s], tile_sems.at[f, s]).wait()
            patch(f, s)
        copies[f][0].wait()
        if f + 1 < number:
            copies.append(inputs(f + 1))
        mixture = weights[f, 0] * held[f, 0].astype(f32)
        for s in range(1, slots):
            mixture += weights[f, s] * held[f, s].astype(f32)
        sums[...] = mixture.astype(bf16)
        copies[f][1].wait()
        copies[f][2].wait()
        for step in range(bins // blk):
            work(f, step)
        out_ref[f * side : (f + 1) * side] = dsum[...].astype(bf16)
    out_ref[number * side :] = jnp.zeros((32, side), bf16)
    out_ref[number * side :, :128] = in_three(total[...])


def facets(tiles, strips, ku, kv, data, ints, weights, squares):
    number, bins, side = ku.shape[1:]
    slots = weights.shape[1]
    return pl.pallas_call(
        functools.partial(facets_kernel, 512, len(tiles)),
        in_specs=[scalar] * 2 + [anywhere] * (len(tiles) + len(strips) + 3) + [whole],
        out_specs=whole,
        out_shape=jax.ShapeDtypeStruct((number * side + 32, side), bf16),
        scratch_shapes=[
            pltpu.VMEM((number, slots, side, side), bf16),
            pltpu.VMEM((number, slots, 4 * border, side), bf16),
            pltpu.VMEM((number, bins, side), bf16),
            pltpu.VMEM((number, bins, side), bf16),
            pltpu.VMEM((number, bins, bins), bf16),
            pltpu.VMEM((side, side), bf16),
            pltpu.VMEM((side, side), f32),
            pltpu.VMEM((8, 128), f32),
            pltpu.SemaphoreType.DMA((number, 3)),
            pltpu.SemaphoreType.DMA((number, slots)),
            pltpu.SemaphoreType.DMA((number, slots)),
        ],
        compiler_params=pltpu.CompilerParams(vmem_limit_bytes=44 * 1024 * 1024),
        name="facets",
    )(ints, weights, *tiles, *strips, ku, kv, data, squares)


def mix_kernel(scale, mine, theirs, *outs):
    side = outs[0].shape[1]
    number = mine.shape[0] // side
    for d, out in enumerate(outs):
        value = None
        for f in range(2 * number):
            ref, at = (mine, f) if f < number else (theirs, f - number)
            term = scale[d, f] * ref[at * side : (at + 1) * side].astype(f32)
            value = term if value is None else value + term
        out[...] = value.astype(bf16)


def mix_strips_kernel(scale, mine, theirs, *refs):
    outs, strips = refs[:-1], refs[-1]
    side = outs[0].shape[1]
    number = mine.shape[0] // side
    for f in range(2 * number):
        ref, at = (mine, f) if f < number else (theirs, f - number)
        strips_of(ref.at[at * side : (at + 1) * side], strips.at[f])
    total = from_three(mine[number * side :, :128]) + from_three(theirs[number * side :, :128])
    for d, out in enumerate(outs):
        value = None
        for f in range(2 * number):
            term = scale[d, f] * strips[f].astype(f32)
            value = term if value is None else value + term
        out[: 4 * border] = value.astype(bf16)
        out[4 * border :] = jnp.zeros((32, side), bf16)
        out[4 * border :, :128] = in_three(total)


def mixed(mine, theirs, scale, strips):
    side = mine.shape[1]
    rows = 4 * border + 32 if strips else side
    kept = [pltpu.VMEM((scale.shape[1], 4 * border, side), bf16)] if strips else []
    return pl.pallas_call(
        mix_strips_kernel if strips else mix_kernel,
        in_specs=[scalar, whole, whole],
        out_specs=[whole] * scale.shape[0],
        out_shape=[jax.ShapeDtypeStruct((rows, side), bf16)] * scale.shape[0],
        scratch_shapes=kept,
        compiler_params=pltpu.CompilerParams(vmem_limit_bytes=vmem),
        name="mixed",
    )(scale, mine, theirs)


def chip_shift(x, hop):
    size = lax.axis_size("gy")
    return lax.ppermute(x, "gy", [(i, (i + 2 * hop) % size) for i in range(size)])


def by_chips(x, pairs):
    return lax.ppermute(x, "gy", [(2 * a + c, 2 * b + c) for a, b in pairs for c in range(2)])


def paired(x, bits):
    return by_chips(x, [(i, i ^ bits) for i in range(lax.axis_size("gy") // 2)])


def swapped(x):
    return lax.ppermute(x, "gy", [(i, i ^ 1) for i in range(lax.axis_size("gy"))])


def body(
    xi_coarse,
    xi_middle,
    xi_fine,
    coef_middle,
    coef_fine,
    kern_u,
    kern_v,
    vis_data,
    facet_tiles,
    facet_weight,
    facet_count,
):
    fields = (xi_coarse, coef_middle, xi_middle, coef_fine, xi_fine)
    right, left = neighbours("gy")
    down, up = neighbours("gx")
    sides = halo_sides(xi_coarse, xi_middle, coef_middle)
    left_in = lax.ppermute(sides[1], "gy", right)
    right_in = lax.ppermute(sides[0], "gy", left)
    (first,) = sky_of(None, *fields)
    first, left_in, right_in, around, listed = lax.optimization_barrier(
        (
            first,
            left_in,
            right_in,
            (xi_coarse, xi_middle, coef_middle),
            (facet_tiles[0], facet_weight[0], facet_count[0]),
        )
    )
    lists, weights, counts = listed
    size = lax.axis_size("gy")
    chips = size // 2
    me = lax.axis_index("gy")
    ids = jnp.arange(size, dtype=jnp.int32)
    mixing = jnp.sum(
        weights[:, :, None] * (lists[:, :, None] == ids[None, None, :]).astype(f32), axis=1
    )
    order = 2 * ((me // 2 + jnp.arange(chips, dtype=jnp.int32)) % chips) + me % 2
    scale = jnp.concatenate([mixing, swapped(mixing)])[:, order].T
    hops = range(1, chips)
    chip, other_core = me // 2, jnp.where(lists % 2 == me % 2, 0, 1)
    if chips == 4:
        mine = {1: paired(first, 1), 2: paired(first, 2)}
    else:
        mine = {hop: chip_shift(first, hop) for hop in range(1, min(3, chips))}
    above, below = halo_rows(*around, left_in, right_in)
    sky, strips, squares, lefts, rights = sky_of((above, below, left_in, right_in, *sides), *fields)
    if chips == 4:
        strips = [paired(strips, hop) for hop in hops]
        away = chip ^ (lists // 2)
        place = jnp.where((away == 3) & ((chip == 0) | (chip == 3)), 4, away)
        kind = away
    else:
        strips = [chip_shift(strips, hop) for hop in mine]
        place = away = (chip - lists // 2) % chips
        kind = jnp.where(away <= len(mine), away, 0)
    kinds = len(strips)
    strips = jnp.concatenate(strips)
    sky, strips, mine, scale, weights = lax.optimization_barrier(
        (sky, strips, mine, scale, weights)
    )
    if chips == 4:
        mine[3] = by_chips(sky, ((1, 2), (2, 1)))
        mine[4] = by_chips(mine[2], ((2, 3), (1, 0)))
    else:
        mine |= {hop: chip_shift(sky, hop) for hop in hops[len(mine) :]}
    mine = [sky] + [mine[hop] for hop in sorted(mine)]
    tiles = mine + [swapped(tile) for tile in mine]
    strips = [strips, swapped(strips)]
    place += len(mine) * other_core
    kind = jnp.where(kind > 0, kind + kinds * other_core, 0)
    ints = jnp.concatenate([place, counts[:, None], kind], axis=1)
    dsums = facets(tiles, strips, kern_u, kern_v, vis_data, ints, weights, squares)
    theirs = swapped(dsums)
    strips = mixed(dsums, theirs, scale, True)
    strips, dsums, theirs = lax.optimization_barrier((strips, dsums, theirs))
    edges = [strips[0]] + [chip_shift(strips[hop], hop) for hop in hops]
    parts = mixed(dsums, theirs, scale, False)
    edges, _ = lax.optimization_barrier((edges, parts))
    parts = [parts[0]] + [chip_shift(parts[hop], hop) for hop in hops]
    around = (above, below, lefts, rights)
    to_left, to_right, upper, lower, total = adjoint(True, edges, around, fields)
    size = lax.axis_size("gx")
    steps = [1 << i for i in range(size.bit_length()) if 1 << i < size]

    def across(x, hop):
        return lax.ppermute(x, "gx", [(i, i ^ hop) for i in range(size)])

    from_below = lax.ppermute(upper, "gx", up)
    from_above = lax.ppermute(lower, "gx", down)
    other = across(total, steps[0])
    rows, cols = xi_coarse.shape
    to_left, to_right, total = pl.pallas_call(
        functools.partial(corners_kernel, rows, cols),
        in_specs=[whole] * 6,
        out_specs=[whole] * 3,
        out_shape=[shape(*to_left.shape), shape(*to_right.shape), shape(8, 128)],
        name="corners",
    )(to_left, to_right, from_above, from_below, total, other)
    for hop in steps[1:-1]:
        total += across(total, hop)
    other = across(total, steps[-1])
    from_left = lax.ppermute(to_right, "gy", right)
    from_right = lax.ppermute(to_left, "gy", left)
    parts, from_left, from_right, other = lax.optimization_barrier(
        (parts, from_left, from_right, other)
    )
    cells = size * lax.axis_size("gy") * 16 * rows * cols
    arrived = (from_left, from_right, from_above, from_below, total, other)
    grad_fine, grad_middle, grad_coarse, total = adjoint(
        False, parts, around, fields, arrived, cells
    )
    return grad_coarse, grad_middle, grad_fine, total.reshape(())


def solution(mesh):
    placed = (
        P("gx", "gy"),
        P("gx", "gy"),
        P("gx", "gy"),
        P(None, None, "gx", "gy"),
        P(None, None, "gx", "gy"),
        P("gx", "gy", None, None),
        P("gx", "gy", None, None),
        P("gx", "gy", None, None),
        P("gx", "gy", None),
        P("gx", "gy", None),
        P("gx", "gy"),
    )
    return jax.shard_map(
        body,
        mesh=mesh,
        in_specs=placed,
        out_specs=(P("gx", "gy"), P("gx", "gy"), P("gx", "gy"), P()),
        check_vma=False,
    )
```

```python
import functools

import jax
import jax.numpy as jnp
from jax import lax
from jax.experimental import pallas as pl
from jax.experimental.pallas import tpu as pltpu
from jax.sharding import PartitionSpec as P

inv_noise = 0.125
long_work = pl.CostEstimate(flops=40_000_000_000, transcendentals=0, bytes_accessed=64_000_000)
border = 8
vmem = 32 * 1024 * 1024
f32 = jnp.float32
bf16 = jnp.bfloat16


def halves(x):
    high = x.astype(bf16)
    return high, (x - high.astype(f32)).astype(bf16)


def interleaver(cols, transposed):
    shape = (2 * cols, 2 * cols)
    split = lax.broadcasted_iota(jnp.int32, shape, 1 if transposed else 0)
    whole = lax.broadcasted_iota(jnp.int32, shape, 0 if transposed else 1)
    place = jnp.where(split >= cols, 2 * (split - cols) + 1, 2 * split)
    return (place == whole).astype(f32).astype(bf16)


def folded(x):
    rows, cols = x.shape
    x = jnp.sum(x.reshape(rows // 8, 8, cols), axis=0)
    return sum(x[:, i : i + 128] for i in range(0, cols, 128))


def row_of(ref, i):
    return ref[i : i + 1, :]


def dot_t(x, y, dims):
    return lax.dot_general(x, y, (dims, ((), ())), preferred_element_type=f32)


def moved(x, perm):
    high, low = halves(x)
    return jnp.dot(high, perm, preferred_element_type=f32) + jnp.dot(
        low, perm, preferred_element_type=f32
    )


def ends_placed(first, last, cols):
    rows = jnp.concatenate([first, first, last, last, jnp.zeros((4, first.shape[1]), f32)])
    high = rows.astype(bf16).astype(f32)
    index = lax.broadcasted_iota(jnp.int32, rows.shape, 0)
    rows = jnp.where(index % 2 == 0, high, rows - high).astype(bf16)
    shape = (8, cols)
    index = lax.broadcasted_iota(jnp.int32, shape, 0)
    lane = lax.broadcasted_iota(jnp.int32, shape, 1)
    place = ((index < 2) & (lane == 0)) | ((index >= 2) & (index < 4) & (lane == cols - 1))
    return dot_t(rows, place.astype(f32).astype(bf16), ((0,), (0,)))


def weighed(win, coef_ref, perm, lhs, mix, rows, cols, chunks=()):
    def part(i, carry):
        r0 = pl.multiple_of(i * 16, 16)
        total = [jnp.zeros((16, cols), f32) for _ in range(4)]
        for near in range(9):
            w = win[near, pl.ds(r0, 16), :]
            for child in range(4):
                total[child] += coef_ref[child, near, pl.ds(r0, 16), :].astype(f32) * w
        for child in range(4):
            a, b = child // 2, child % 2
            high, low = halves(total[child])
            lhs[pl.ds(2 * a * rows + r0, 16), b * cols : (b + 1) * cols] = high
            lhs[pl.ds((2 * a + 1) * rows + r0, 16), b * cols : (b + 1) * cols] = low
        return carry

    in_chunks(part, rows, chunks)
    field = jnp.dot(lhs[...], perm[...], preferred_element_type=f32)
    for tile in range(2 * cols // 128):
        lanes = slice(tile * 128, (tile + 1) * 128)
        for a in range(2):
            mix[tile, pl.ds(a, rows, stride=2), :] = (
                field[2 * a * rows : (2 * a + 1) * rows, lanes]
                + field[(2 * a + 1) * rows : (2 * a + 2) * rows, lanes]
            )


def fetched(pairs, sems, first=0):
    copies = [
        pltpu.make_async_copy(src, dst, sems.at[first + i]) for i, (src, dst) in enumerate(pairs)
    ]
    for copy in copies:
        copy.start()
    return copies


def chunked(source, target, sems):
    number, rows = sems.shape[0], source.shape[2] // sems.shape[0]
    copies = []
    for i in range(number):
        at = slice(i * rows, (i + 1) * rows)
        copies.append(pltpu.make_async_copy(source.at[:, :, at], target.at[:, :, at], sems.at[i]))
        copies[i].start()
    return copies


def in_chunks(part, rows, chunks):
    steps = rows // 16
    if not chunks:
        lax.fori_loop(0, steps, part, 0)
    for i, copy in enumerate(chunks):
        copy.wait()
        lax.fori_loop(i * steps // len(chunks), (i + 1) * steps // len(chunks), part, 0)


def columns_beside(field, left, right):
    rows, cols = field.shape[1:]
    placed = ends_placed(left, right, cols)
    lane = lax.broadcasted_iota(jnp.int32, (rows, cols), 1)
    here = field[1]
    field[0] = jnp.where(lane == 0, placed, pltpu.roll(here, 1, 1))
    field[2] = jnp.where(lane == cols - 1, placed, pltpu.roll(here, cols - 1, 1))


def strips_of(tile, out):
    rows, cols = tile.shape
    first, last = tile[: 2 * border].astype(f32), tile[rows - 2 * border :].astype(f32)
    out[: 2 * border] = jnp.concatenate([first[:border], last[border:]]).astype(bf16)
    index = lax.broadcasted_iota(jnp.int32, (2 * border, cols), 0)
    lane = lax.broadcasted_iota(jnp.int32, (2 * border, cols), 1)
    pick = lane == jnp.where(index < border, index, index + cols - 2 * border)
    pick = pick.astype(f32).astype(bf16)
    out[2 * border : 4 * border] = dot_t(pick, tile[...], ((1,), (1,))).astype(bf16)


def columns_of(strip):
    index = lax.broadcasted_iota(jnp.int32, (2 * border, 128), 0)
    lane = lax.broadcasted_iota(jnp.int32, (2 * border, 128), 1)
    out = []
    for place in (
        (index < border) & (lane == index),
        (index >= border) & (lane == index + 128 - 2 * border),
    ):
        out.append(dot_t(strip, place.astype(f32).astype(bf16), ((0,), (0,))))
    return out


def stretch(out, side, over, under, b, lane, first):
    rows = side.shape[1]
    out[...] = jnp.zeros_like(out)
    out[:, 2 : rows + 2] = side[...]
    out[9:18, 1:2] = over[9 * b : 9 * b + 9, lane : lane + 1]
    out[21:22, 1:2] = over[20 + b : 21 + b, lane : lane + 1]
    out[0:9, rows + 2 : rows + 3] = under[9 * b : 9 * b + 9, lane : lane + 1]
    out[20:21, rows + 2 : rows + 3] = under[20 + b : 21 + b, lane : lane + 1]
    for k in range(2):
        at = slice(first + k, first + k + 1)
        for i in range(2):
            out[18 + k : 19 + k, i : i + 1] = over[18 + i : 19 + i, at]
            end = rows + 2 + i
            out[18 + k : 19 + k, end : end + 1] = under[18 + i : 19 + i, at]


def sky_kernel(alone, *refs):
    count = 5 if alone else 11
    sources, refs = refs[:count], refs[count:]
    outs, refs = (refs[:1], refs[1:]) if alone else (refs[:5], refs[5:])
    held, rest = refs[:11], refs[11:]
    win, perm, lhs, mix, near_coarse, shifted, fine_win, fine_perm, fine_lhs, fine_mix = rest[:10]
    lefts, rights, to_left, to_right, sems, chunk_sems = rest[10:]
    sky_ref = outs[0]
    if alone:
        for ref in held[1:7]:
            ref[...] = jnp.zeros_like(ref)
        held_here = (held[0], *held[7:])
    else:
        held_here = held
    copies = fetched(zip(sources[:-2], held_here[:-2]), sems)
    chunks = chunked(sources[-2], held_here[-2], chunk_sems)
    copies += fetched(zip(sources[-1:], held_here[-1:]), sems, len(copies))
    xi_coarse, over, under, left_in, right_in, left_side, right_side = held[:7]
    coef_middle, xi_middle, coef_fine, xi_fine = held[7:]
    rows, cols = win.shape[1:]
    perm[...] = interleaver(cols, False)
    fine_perm[...] = interleaver(2 * cols, False)
    near_coarse[...] = jnp.zeros_like(near_coarse)
    for copy in copies[:-2]:
        copy.wait()
    above, below = over[:, 2 : cols + 2], under[:, 2 : cols + 2]
    if alone:
        for ref in (lefts, rights):
            ref[...] = jnp.zeros_like(ref)
    else:
        stretch(lefts, left_in, over, under, 1, 1, 0)
        stretch(rights, right_in, over, under, 0, cols + 2, cols + 2)
        stretch(to_left, left_side, over, under, 0, 2, 2)
        stretch(to_right, right_side, over, under, 1, cols + 1, cols)
    near_coarse[1, 6:8] = above[18:20]
    near_coarse[1, 8 : 8 + rows] = xi_coarse[...]
    near_coarse[1, 8 + rows : 10 + rows] = below[18:20]
    pad = jnp.zeros((1, 6), f32)
    beside = [
        jnp.concatenate([pad, row_of(x, i)[:, : rows + 4], pad], axis=1)
        for x, i in ((lefts, 19), (rights, 18))
    ]
    columns_beside(near_coarse, *beside)
    for near in range(9):
        r, c = near // 3, near % 3
        win[near] = near_coarse[c, 7 + r : 7 + r + rows]
    weighed(win, coef_middle, perm, lhs, mix, rows, cols)

    def across(message, top):
        out = []
        for b in range(2):
            line = row_of(message, 20 + b)
            for near in range(9):
                r, c = near // 3, near % 3
                line += row_of(message, 9 * b + near) * near_coarse[c, top + r : top + r + 1]
            out.append(line)
        return jnp.concatenate(out, axis=1)

    def along(message, fields):
        out = []
        for a in range(2):
            line = row_of(message, 20 + a)[:, 1 : rows + 3]
            for near in range(9):
                r, c = near // 3, near % 3
                line += row_of(message, 9 * a + near)[:, 1 : rows + 3] * fields[c][:, r : r + rows + 2]
            out.append(line)
        inner = jnp.concatenate([line[:, 1 : rows + 1] for line in out], axis=1)
        return inner, out[1][:, :1], out[0][:, rows + 1 :]

    if alone:
        empty = jnp.zeros((1, 1), f32)
        top = bottom = left = right = jnp.zeros((1, 2 * cols), f32)
        top_left = bottom_left = top_right = bottom_right = empty
    else:
        top, bottom = across(above, 6), across(below, rows + 7)
        left, top_left, bottom_left = along(
            lefts, [row_of(lefts, 18), row_of(lefts, 19), row_of(to_left, 18)]
        )
        right, top_right, bottom_right = along(
            rights, [row_of(to_right, 19), row_of(rights, 18), row_of(rights, 19)]
        )
    lines = jnp.concatenate([top, bottom, left, right, jnp.zeros((4, 2 * cols), f32)])
    lines = moved(lines, perm[...])
    copies[-2].wait()
    xi = xi_middle[...]
    last = 8 + 2 * rows
    shifted[1] = jnp.zeros(shifted.shape[1:], f32)
    for tile in range(2 * cols // 128):
        lanes = slice(tile * 128, (tile + 1) * 128)
        shifted[1, 8:last, lanes] = mix[tile] + xi[:, lanes]
    shifted[1, 7:8, :] = lines[0:1]
    shifted[1, last : last + 1, :] = lines[1:2]
    pad = jnp.zeros((1, 7), f32)
    beside = [
        jnp.concatenate([pad, first, line, final, pad], axis=1)
        for first, line, final in (
            (top_left, lines[2:3], bottom_left),
            (top_right, lines[3:4], bottom_right),
        )
    ]
    columns_beside(shifted, *beside)
    for near in range(9):
        r, c = near // 3, near % 3
        fine_win[near] = shifted[c, 7 + r : 7 + r + 2 * rows, :]
    weighed(fine_win, coef_fine, fine_perm, fine_lhs, fine_mix, 2 * rows, 2 * cols, chunks)
    copies[-1].wait()
    for tile in range(4 * cols // 128):
        lanes = slice(tile * 128, (tile + 1) * 128)
        sky_ref[:, lanes] = (fine_mix[tile] + xi_fine[:, lanes]).astype(bf16)
    if alone:
        return
    strips_ref, sq_ref, lefts_ref, rights_ref = outs[1:]
    lefts_ref[...] = lefts[...]
    rights_ref[...] = rights[...]
    strips_of(sky_ref, strips_ref)
    sq_ref[...] = (
        folded(win[4] * win[4]) + folded(xi * xi) + folded(xi_fine[...] * xi_fine[...])
    )


def sides_kernel(left_in, right_in, first_side, last_side, to_above, to_below):
    rows = left_in.shape[1]
    stretch(to_above, first_side, left_in, right_in, 0, 0, 0)
    stretch(to_below, last_side, left_in, right_in, 1, rows - 1, rows - 2)


def neighbours(axis):
    size = lax.axis_size(axis)
    ahead = [(i, i + 1) for i in range(size - 1)]
    return ahead, [(j, i) for i, j in ahead]


def halo_sides(xi_coarse, xi_middle, coef_middle):
    rows, cols = xi_coarse.shape

    def inside(b, col, near):
        return jnp.concatenate(
            [
                coef_middle[b::2, :, :, col].reshape(18, rows).astype(f32),
                near.T,
                xi_middle[:, 2 * col + b].reshape(rows, 2).T,
            ]
        )

    return inside(0, 0, xi_coarse[:, :2]), inside(1, cols - 1, xi_coarse[:, -2:])


def halo_rows(xi_coarse, xi_middle, coef_middle, left_in, right_in):
    rows, cols = xi_coarse.shape

    def edge(a, row, near):
        return jnp.concatenate(
            [
                coef_middle[2 * a : 2 * a + 2, :, row].reshape(18, cols).astype(f32),
                near,
                xi_middle[2 * row + a].reshape(cols, 2).T,
            ]
        )

    to_above, to_below = pl.pallas_call(
        sides_kernel,
        in_specs=[whole] * 4,
        out_specs=[whole] * 2,
        out_shape=[jax.ShapeDtypeStruct((22, cols + 4), f32)] * 2,
        cost_estimate=long_work,
        name="sides",
    )(left_in, right_in, edge(0, 0, xi_coarse[:2]), edge(1, rows - 1, xi_coarse[-2:]))
    down, up = neighbours("gx")
    return lax.ppermute(to_below, "gx", down), lax.ppermute(to_above, "gx", up)


whole = pl.BlockSpec(memory_space=pltpu.VMEM)
scalar = pl.BlockSpec(memory_space=pltpu.SMEM)
anywhere = pl.BlockSpec(memory_space=pltpu.HBM)


def sky_of(halos, xi_coarse, coef_middle, xi_middle, coef_fine, xi_fine):
    rows, cols = coef_middle.shape[2:]
    alone = halos is None
    given = (coef_middle, xi_middle, coef_fine, xi_fine)
    operands = (xi_coarse, *given) if alone else (xi_coarse, *halos, *given)
    message = [(22, cols + 4)] * 2 + [(22, rows)] * 4
    return pl.pallas_call(
        functools.partial(sky_kernel, alone),
        in_specs=[anywhere] * len(operands),
        out_specs=[whole] * (1 if alone else 5),
        out_shape=[
            jax.ShapeDtypeStruct((4 * rows, 4 * cols), bf16),
            jax.ShapeDtypeStruct((4 * border, 4 * cols), bf16),
            jax.ShapeDtypeStruct((8, 128), f32),
            jax.ShapeDtypeStruct((22, rows + 4), f32),
            jax.ShapeDtypeStruct((22, rows + 4), f32),
        ][: 1 if alone else 5],
        scratch_shapes=[pltpu.VMEM(xi_coarse.shape, f32)]
        + [pltpu.VMEM(shape, f32) for shape in message]
        + [pltpu.VMEM(x.shape, x.dtype) for x in given]
        + [
            pltpu.VMEM((9, rows, cols), f32),
            pltpu.VMEM((2 * cols, 2 * cols), bf16),
            pltpu.VMEM((4 * rows, 2 * cols), bf16),
            pltpu.VMEM((2 * cols // 128, 2 * rows, 128), f32),
            pltpu.VMEM((3, rows + 16, cols), f32),
            pltpu.VMEM((3, 2 * rows + 16, 2 * cols), f32),
            pltpu.VMEM((9, 2 * rows, 2 * cols), f32),
            pltpu.VMEM((4 * cols, 4 * cols), bf16),
            pltpu.VMEM((8 * rows, 4 * cols), bf16),
            pltpu.VMEM((4 * cols // 128, 4 * rows, 128), f32),
            *[pltpu.VMEM((22, rows + 4), f32) for _ in range(4)],
            pltpu.SemaphoreType.DMA((11,)),
            pltpu.SemaphoreType.DMA((4,)),
        ],
        compiler_params=pltpu.CompilerParams(vmem_limit_bytes=60 * 1024 * 1024),
        name="sky",
    )(*operands)


def spread(mix, coef_ref, terms, rows, cols, chunks=()):
    def part(i, carry):
        r0 = pl.multiple_of(i * 16, 16)
        quads = []
        for a in range(2):
            for b in range(2):
                tiles = range(b * cols // 128, (b + 1) * cols // 128)
                lines = [mix[t, pl.ds(2 * r0 + a, 16, stride=2), :] for t in tiles]
                quads.append(jnp.concatenate(lines, axis=1))
        for near in range(9):
            total = jnp.zeros((16, cols), f32)
            for child in range(4):
                total += coef_ref[child, near, pl.ds(r0, 16), :].astype(f32) * quads[child]
            terms[near, pl.ds(16 + r0, 16), :] = total
        return carry

    in_chunks(part, rows, chunks)


def row_sums(terms, rowed):
    rows = terms.shape[1] - 32
    for near in range(9):
        terms[near, :16] = jnp.zeros((16, terms.shape[2]), f32)
        terms[near, rows + 16 :] = jnp.zeros((16, terms.shape[2]), f32)
    for c in range(3):
        total = terms[c, 9 : rows + 25]
        for r in (1, 2):
            total += terms[3 * r + c, 9 - r : rows + 25 - r]
        rowed[c, : rows + 16] = total
        rowed[c, rows + 16 :] = jnp.zeros((rowed.shape[1] - rows - 16, rowed.shape[2]), f32)


def joined(rowed, cols):
    lane = lax.broadcasted_iota(jnp.int32, rowed.shape[1:], 1)
    main = (
        rowed[1]
        + jnp.where(lane == 0, 0.0, pltpu.roll(rowed[2], 1, 1))
        + jnp.where(lane == cols - 1, 0.0, pltpu.roll(rowed[0], cols - 1, 1))
    )
    lane = lax.broadcasted_iota(jnp.int32, (8, cols), 1)
    outside = []
    for c, col in ((0, 0), (2, cols - 1)):
        pick = (lane == col).astype(f32).astype(bf16)
        high, low = halves(rowed[c])
        out = dot_t(pick, high, ((1,), (1,))) + dot_t(pick, low, ((1,), (1,)))
        outside.append(out[:1])
    return main, outside[0], outside[1]


def adjoint_kernel(edge, number, cells, *refs):
    count = 6 if edge else 15
    written = 5 if edge else 4
    count += number
    sources, outs, refs = refs[:count], refs[count : count + written], refs[count + written :]
    parts, held, rest = refs[:number], refs[number:count], refs[count:]
    fine_perm, fine_mix, fine_terms, fine_rowed, perm, mix, terms, rowed, full, sems, chunk_sems, out_sem = rest
    arriving = fetched(zip(sources[:number], parts), sems)
    chunks = chunked(sources[number], held[0], chunk_sems)
    copies = [None] + fetched(zip(sources[number + 1 :], held[1:]), sems, number)
    coef_fine, coef_middle, over, under, lefts, rights = held[:6]
    if edge:
        left_ref, right_ref, upper_ref, lower_ref, total_ref = outs
    else:
        grad_ref, middle_ref, coarse_ref, total_ref = outs
        xi_fine, xi_middle, xi_coarse, from_left, from_right, from_above, from_below = held[6:13]
        total, other = held[13:]
    rows, cols = terms.shape[1] - 32, terms.shape[2]
    fine_perm[...] = interleaver(2 * cols, True)
    perm[...] = interleaver(cols, True)
    for copy in arriving:
        copy.wait()
    g = parts[0][...].astype(f32)
    for part in parts[1:]:
        g += part[...].astype(f32)
    if edge:
        tail = g[4 * border :, :128]
        total_ref[...] = tail[:8] + tail[8:16] + tail[16:24]
        high, low = halves(g[2 * border : 4 * border])
        left, right = [x + y for x, y in zip(columns_of(high), columns_of(low))]
        full[...] = jnp.zeros_like(full)
        full[:, :128] = left
        full[:, 4 * cols - 128 :] = right
        full[:border] = g[:border]
        full[4 * rows - border :] = g[border : 2 * border]
        g = full[...]
    else:
        copies[6].wait()
        full[...] = g + xi_fine[...]
        leaving = pltpu.make_async_copy(full, grad_ref, out_sem)
        leaving.start()
    split = moved(g, fine_perm[...])
    for tile in range(4 * cols // 128):
        fine_mix[tile] = split[:, tile * 128 : (tile + 1) * 128]
    spread(fine_mix, coef_fine, fine_terms, 2 * rows, 2 * cols, chunks)
    row_sums(fine_terms, fine_rowed)
    main, left, right = joined(fine_rowed, 2 * cols)
    last = 8 + 2 * rows
    inner = main[8:last]
    for copy in copies[1:6] + copies[7:]:
        copy.wait()
    above, below = over[:, 2 : cols + 2], under[:, 2 : cols + 2]
    if not edge:
        line = slice(1, 2 * rows + 1)
        middle_ref[...] = (
            inner
            + xi_middle[...]
            + ends_placed(from_left[2:3, line], from_right[2:3, line], 2 * cols)
        )
        middle_ref[:1] += from_above[2:3, 1 : 2 * cols + 1]
        middle_ref[2 * rows - 1 :] += from_below[2:3, 1 : 2 * cols + 1]
    split = moved(inner, perm[...])
    for tile in range(2 * cols // 128):
        mix[tile] = split[:, tile * 128 : (tile + 1) * 128]
    spread(mix, coef_middle, terms, rows, cols)
    ring_above, ring_below = main[7:8], main[last : last + 1]
    lines = [ring_above, ring_below, left[:, 8:last], right[:, 8:last]]
    lines = moved(jnp.concatenate(lines + [jnp.zeros((4, 2 * cols), f32)]), perm[...])
    row_sums(terms, rowed)
    for line, message, top in ((0, above, 6), (1, below, 7 + rows)):
        for near in range(9):
            r, c = near // 3, near % 3
            term = row_of(message, near) * lines[line : line + 1, :cols]
            term += row_of(message, 9 + near) * lines[line : line + 1, cols:]
            rowed[c, top + r : top + r + 1, :] += term

    def along(line, ends, message):
        empty = jnp.zeros((1, 1), f32)
        first = [empty, lines[line : line + 1, :rows], ends[:, last : last + 1]]
        second = [ends[:, 7:8], lines[line : line + 1, cols : cols + rows], empty]
        first, second = jnp.concatenate(first, axis=1), jnp.concatenate(second, axis=1)
        out = []
        for c in range(3):
            total = jnp.zeros((1, rows + 4), f32)
            for r in range(3):
                near = 3 * r + c
                term = row_of(message, near)[:, 1 : rows + 3] * first
                term += row_of(message, 9 + near)[:, 1 : rows + 3] * second
                pads = [jnp.zeros((1, n), f32) for n in (r, 2 - r) if n]
                pieces = [term] + pads if r == 0 else pads[:1] + [term] + pads[1:]
                total += jnp.concatenate(pieces, axis=1)
            out.append(total)
        return out

    outer_left = along(2, left, lefts)
    outer_right = along(3, right, rights)
    main, near_left, near_right = joined(rowed, cols)
    if not edge:
        line = slice(2, rows + 2)
        first = outer_left[2][:, line] + from_left[1:2, line]
        last = outer_right[0][:, line] + from_right[1:2, line]
        second = ends_placed(from_left[0:1, line], from_right[0:1, line], cols)
        lane = lax.broadcasted_iota(jnp.int32, second.shape, 1)
        second = jnp.where(lane == 1, pltpu.roll(second, 1, 1), 0.0) + jnp.where(
            lane == cols - 2, pltpu.roll(second, cols - 1, 1), 0.0
        )
        coarse_ref[...] = (
            main[8 : 8 + rows] + xi_coarse[...] + ends_placed(first, last, cols) + second
        )
        coarse_ref[:2] += from_above[0:2, 2 : cols + 2]
        coarse_ref[rows - 2 :] += from_below[0:2, 2 : cols + 2]
        both = total[...] + other[...]
        both = jnp.sum(jnp.sum(both, axis=1, keepdims=True), axis=0, keepdims=True)
        total_ref[...] = both * (1.0 / cells)
        leaving.wait()
        return
    sides = []
    for ref, far, close, beyond, ends in (
        (left_ref, outer_left[0], outer_left[1], near_left, left),
        (right_ref, outer_right[2], outer_right[1], near_right, right),
    ):
        close += beyond[:, 6 : rows + 10]
        ends = ends[:, 7 : 2 * rows + 9]
        ref[...] = jnp.zeros_like(ref)
        ref[0:1, : rows + 4] = far
        ref[1:2, : rows + 4] = close
        ref[2:3, : 2 * rows + 2] = ends
        sides.append((far, close, ends))
    lane = lax.broadcasted_iota(jnp.int32, (1, cols), 1)
    (far_left, close_left, ends_left), (far_right, close_right, ends_right) = sides
    for ref, first, line, end in (
        (upper_ref, 6, ring_above, 0),
        (lower_ref, 8 + rows, ring_below, 2 * rows + 1),
    ):
        ref[...] = jnp.zeros_like(ref)
        for i in range(2):
            at = slice(first - 6 + i, first - 5 + i)
            inner = (
                main[first + i : first + i + 1]
                + jnp.where(lane == 0, outer_left[2][:, at], 0.0)
                + jnp.where(lane == cols - 1, outer_right[0][:, at], 0.0)
            )
            pieces = [far_left[:, at], close_left[:, at], inner, close_right[:, at], far_right[:, at]]
            ref[i : i + 1, : cols + 4] = jnp.concatenate(pieces, axis=1)
        pieces = [ends_left[:, end : end + 1], line, ends_right[:, end : end + 1]]
        ref[2:3, : 2 * cols + 2] = jnp.concatenate(pieces, axis=1)


def corners_kernel(rows, cols, left, right, from_above, from_below, total, other, left_out, right_out, total_out):
    for ref, out, far, close, end in (
        (left, left_out, 0, 1, 0),
        (right, right_out, cols + 3, cols + 2, 2 * cols + 1),
    ):
        out[...] = ref[...]
        for rows_in, first, line in ((from_above, 2, 1), (from_below, rows, 2 * rows)):
            for i in range(2):
                at = slice(first + i, first + i + 1)
                out[0:1, at] += rows_in[i : i + 1, far : far + 1]
                out[1:2, at] += rows_in[i : i + 1, close : close + 1]
            out[2:3, line : line + 1] += rows_in[2:3, end : end + 1]
    total_out[...] = total[...] + other[...]


def shape(*dims):
    return jax.ShapeDtypeStruct(dims, f32)


def adjoint(edge, parts, sides, fields, arrived=(), cells=0):
    rows, cols = fields[1].shape[2:]
    xi_coarse, coef_middle, xi_middle, coef_fine, xi_fine = fields
    wide = 2 * rows + 128
    operands = (coef_fine, coef_middle, *sides)
    if edge:
        outs = [shape(8, wide)] * 2 + [shape(8, 2 * cols + 128)] * 2 + [shape(8, 128)]
    else:
        operands += (xi_fine, xi_middle, xi_coarse, *arrived)
        outs = [shape(4 * rows, 4 * cols), shape(2 * rows, 2 * cols), shape(rows, cols)]
        outs += [shape(1, 1)]
    return pl.pallas_call(
        functools.partial(adjoint_kernel, edge, len(parts), cells),
        in_specs=[anywhere] * (len(parts) + len(operands)),
        out_specs=[whole] * 5 if edge else [anywhere, whole, whole, whole],
        out_shape=outs,
        scratch_shapes=[pltpu.VMEM(x.shape, x.dtype) for x in (*parts, *operands)]
        + [
            pltpu.VMEM((4 * cols, 4 * cols), bf16),
            pltpu.VMEM((4 * cols // 128, 4 * rows, 128), f32),
            pltpu.VMEM((9, 2 * rows + 32, 2 * cols), f32),
            pltpu.VMEM((3, 2 * rows + 128, 2 * cols), f32),
            pltpu.VMEM((2 * cols, 2 * cols), bf16),
            pltpu.VMEM((2 * cols // 128, 2 * rows, 128), f32),
            pltpu.VMEM((9, rows + 32, cols), f32),
            pltpu.VMEM((3, rows + 128, cols), f32),
            pltpu.VMEM((4 * rows, 4 * cols), f32),
            pltpu.SemaphoreType.DMA((len(parts) + len(operands),)),
            pltpu.SemaphoreType.DMA((4,)),
            pltpu.SemaphoreType.DMA,
        ],
        compiler_params=pltpu.CompilerParams(vmem_limit_bytes=60 * 1024 * 1024),
        cost_estimate=long_work if edge else None,
        name="adjoint",
    )(*parts, *operands)


def in_three(x):
    high = x.astype(bf16).astype(f32)
    middle = (x - high).astype(bf16).astype(f32)
    return jnp.concatenate([high, middle, x - high - middle, jnp.zeros_like(x)]).astype(bf16)


def from_three(x):
    x = x.astype(f32)
    return x[:8] + x[8:16] + x[16:24]


def facets_kernel(blk, given, ints, weights, *refs):
    number, slots = weights.shape
    tiles, strips, rest = refs[:given], refs[given : given + 2], refs[given + 2 :]
    height = 4 * border
    kinds = strips[0].shape[0] // height
    ku_hbm, kv_hbm, data_hbm, squares, out_ref = rest[:5]
    held, held_strips, ku, kv, data, sums, dsum, total, sems, tile_sems, strip_sems = rest[5:]
    bins, side = ku.shape[1:]

    def inputs(f):
        for s in range(slots):
            for i, tile in enumerate(tiles):

                @pl.when(ints[f, s] == i)
                def _():
                    pltpu.make_async_copy(tile, held.at[f, s], tile_sems.at[f, s]).start()

            for i in range(2 * kinds):

                @pl.when(ints[f, slots + 1 + s] == i + 1)
                def _():
                    first = i % kinds * height
                    strip = strips[i // kinds].at[first : first + height]
                    pltpu.make_async_copy(strip, held_strips.at[f, s], strip_sems.at[f, s]).start()

        pairs = ((ku_hbm, ku), (kv_hbm, kv), (data_hbm, data))
        copies = [
            pltpu.make_async_copy(src.at[0, f], dst.at[f], sems.at[f, i])
            for i, (src, dst) in enumerate(pairs)
        ]
        for copy in copies:
            copy.start()
        return copies

    def patch(f, s):
        @pl.when(ints[f, slots + 1 + s] > 0)
        def _():
            strip = strips[0].at[:height]
            pltpu.make_async_copy(strip, held_strips.at[f, s], strip_sems.at[f, s]).wait()
            tile, strip = held.at[f, s], held_strips.at[f, s]
            lines = strip[: 2 * border].astype(f32)
            top, bottom = tile[: 2 * border].astype(f32), tile[side - 2 * border :].astype(f32)
            tile[: 2 * border] = jnp.concatenate([lines[:border], top[border:]]).astype(bf16)
            tile[side - 2 * border :] = jnp.concatenate([bottom[:border], lines[border:]]).astype(
                bf16
            )
            lane = lax.broadcasted_iota(jnp.int32, (side, 128), 1)
            left, right = columns_of(strip[2 * border :])
            for cells, inside, start in (
                (left, lane < border, 0),
                (right, lane >= 128 - border, side - 128),
            ):
                here = tile[:, start : start + 128].astype(f32)
                tile[:, start : start + 128] = jnp.where(inside, cells, here).astype(bf16)

    def work(f, step):
        rows = slice(step * blk, (step + 1) * blk)
        count = ints[f, slots] - step * blk

        @pl.when(count > 0)
        def _():
            amp = jnp.dot(ku[f, rows], sums[...], preferred_element_type=f32).astype(bf16)
            vis = dot_t(amp, kv[f], ((1,), (1,)))
            live = lax.broadcasted_iota(jnp.int32, vis.shape, 0) < count
            resid = jnp.where(live, vis - data[f, rows].astype(f32), 0.0)
            total[...] += 0.5 * inv_noise * folded(resid * resid)
            dvis = (inv_noise * resid).astype(bf16)
            damp = jnp.dot(dvis, kv[f], preferred_element_type=f32).astype(bf16)
            part = dot_t(ku[f, rows], damp, ((0,), (0,)))
            if step == 0:
                dsum[...] = part
            else:
                dsum[...] += part

    copies = [inputs(0)]
    total[...] = 0.5 * squares[...]
    for f in range(number):
        for s in range(slots):
            pltpu.make_async_copy(tiles[0], held.at[f, s], tile_sems.at[f, s]).wait()
            patch(f, s)
        copies[f][0].wait()
        if f + 1 < number:
            copies.append(inputs(f + 1))
        mixture = weights[f, 0] * held[f, 0].astype(f32)
        for s in range(1, slots):
            mixture += weights[f, s] * held[f, s].astype(f32)
        sums[...] = mixture.astype(bf16)
        copies[f][1].wait()
        copies[f][2].wait()
        for step in range(bins // blk):
            work(f, step)
        out_ref[f * side : (f + 1) * side] = dsum[...].astype(bf16)
    out_ref[number * side :] = jnp.zeros((32, side), bf16)
    out_ref[number * side :, :128] = in_three(total[...])


def facets(tiles, strips, ku, kv, data, ints, weights, squares):
    number, bins, side = ku.shape[1:]
    slots = weights.shape[1]
    return pl.pallas_call(
        functools.partial(facets_kernel, 512, len(tiles)),
        in_specs=[scalar] * 2 + [anywhere] * (len(tiles) + len(strips) + 3) + [whole],
        out_specs=whole,
        out_shape=jax.ShapeDtypeStruct((number * side + 32, side), bf16),
        scratch_shapes=[
            pltpu.VMEM((number, slots, side, side), bf16),
            pltpu.VMEM((number, slots, 4 * border, side), bf16),
            pltpu.VMEM((number, bins, side), bf16),
            pltpu.VMEM((number, bins, side), bf16),
            pltpu.VMEM((number, bins, bins), bf16),
            pltpu.VMEM((side, side), bf16),
            pltpu.VMEM((side, side), f32),
            pltpu.VMEM((8, 128), f32),
            pltpu.SemaphoreType.DMA((number, 3)),
            pltpu.SemaphoreType.DMA((number, slots)),
            pltpu.SemaphoreType.DMA((number, slots)),
        ],
        compiler_params=pltpu.CompilerParams(vmem_limit_bytes=44 * 1024 * 1024),
        name="facets",
    )(ints, weights, *tiles, *strips, ku, kv, data, squares)


def mix_kernel(scale, mine, theirs, *outs):
    side = outs[0].shape[1]
    number = mine.shape[0] // side
    for d, out in enumerate(outs):
        value = None
        for f in range(2 * number):
            ref, at = (mine, f) if f < number else (theirs, f - number)
            term = scale[d, f] * ref[at * side : (at + 1) * side].astype(f32)
            value = term if value is None else value + term
        out[...] = value.astype(bf16)


def mix_strips_kernel(scale, mine, theirs, *refs):
    outs, strips = refs[:-1], refs[-1]
    side = outs[0].shape[1]
    number = mine.shape[0] // side
    for f in range(2 * number):
        ref, at = (mine, f) if f < number else (theirs, f - number)
        strips_of(ref.at[at * side : (at + 1) * side], strips.at[f])
    total = from_three(mine[number * side :, :128]) + from_three(theirs[number * side :, :128])
    for d, out in enumerate(outs):
        value = None
        for f in range(2 * number):
            term = scale[d, f] * strips[f].astype(f32)
            value = term if value is None else value + term
        out[: 4 * border] = value.astype(bf16)
        out[4 * border :] = jnp.zeros((32, side), bf16)
        out[4 * border :, :128] = in_three(total)


def mixed(mine, theirs, scale, strips):
    side = mine.shape[1]
    rows = 4 * border + 32 if strips else side
    kept = [pltpu.VMEM((scale.shape[1], 4 * border, side), bf16)] if strips else []
    return pl.pallas_call(
        mix_strips_kernel if strips else mix_kernel,
        in_specs=[scalar, whole, whole],
        out_specs=[whole] * scale.shape[0],
        out_shape=[jax.ShapeDtypeStruct((rows, side), bf16)] * scale.shape[0],
        scratch_shapes=kept,
        compiler_params=pltpu.CompilerParams(vmem_limit_bytes=vmem),
        name="mixed",
    )(scale, mine, theirs)


def chip_shift(x, hop):
    size = lax.axis_size("gy")
    return lax.ppermute(x, "gy", [(i, (i + 2 * hop) % size) for i in range(size)])


def by_chips(x, pairs):
    return lax.ppermute(x, "gy", [(2 * a + c, 2 * b + c) for a, b in pairs for c in range(2)])


def paired(x, bits):
    return by_chips(x, [(i, i ^ bits) for i in range(lax.axis_size("gy") // 2)])


def swapped(x):
    return lax.ppermute(x, "gy", [(i, i ^ 1) for i in range(lax.axis_size("gy"))])


def body(
    xi_coarse,
    xi_middle,
    xi_fine,
    coef_middle,
    coef_fine,
    kern_u,
    kern_v,
    vis_data,
    facet_tiles,
    facet_weight,
    facet_count,
):
    fields = (xi_coarse, coef_middle, xi_middle, coef_fine, xi_fine)
    right, left = neighbours("gy")
    down, up = neighbours("gx")
    sides = halo_sides(xi_coarse, xi_middle, coef_middle)
    left_in = lax.ppermute(sides[1], "gy", right)
    right_in = lax.ppermute(sides[0], "gy", left)
    (first,) = sky_of(None, *fields)
    first, left_in, right_in, around, listed = lax.optimization_barrier(
        (
            first,
            left_in,
            right_in,
            (xi_coarse, xi_middle, coef_middle),
            (facet_tiles[0], facet_weight[0], facet_count[0]),
        )
    )
    lists, weights, counts = listed
    size = lax.axis_size("gy")
    chips = size // 2
    me = lax.axis_index("gy")
    ids = jnp.arange(size, dtype=jnp.int32)
    mixing = jnp.sum(
        weights[:, :, None] * (lists[:, :, None] == ids[None, None, :]).astype(f32), axis=1
    )
    steps = jnp.arange(chips, dtype=jnp.int32)
    order = (me // 2) ^ steps if chips == 4 else (me // 2 + steps) % chips
    order = 2 * order + me % 2
    scale = jnp.concatenate([mixing, swapped(mixing)])[:, order].T
    hops = range(1, chips)
    chip, other_core = me // 2, jnp.where(lists % 2 == me % 2, 0, 1)
    if chips == 4:
        mine = {1: paired(first, 1), 2: paired(first, 2)}
    else:
        mine = {hop: chip_shift(first, hop) for hop in range(1, min(3, chips))}
    above, below = halo_rows(*around, left_in, right_in)
    sky, strips, squares, lefts, rights = sky_of((above, below, left_in, right_in, *sides), *fields)
    if chips == 4:
        strips = [paired(strips, hop) for hop in hops]
        away = chip ^ (lists // 2)
        place = jnp.where((away == 3) & ((chip == 0) | (chip == 3)), 4, away)
        kind = away
    else:
        strips = [chip_shift(strips, hop) for hop in mine]
        place = away = (chip - lists // 2) % chips
        kind = jnp.where(away <= len(mine), away, 0)
    kinds = len(strips)
    strips = jnp.concatenate(strips)
    sky, strips, mine, scale, weights = lax.optimization_barrier(
        (sky, strips, mine, scale, weights)
    )
    if chips == 4:
        mine[3] = by_chips(sky, ((1, 2), (2, 1)))
        mine[4] = by_chips(mine[2], ((2, 3), (1, 0)))
    else:
        mine |= {hop: chip_shift(sky, hop) for hop in hops[len(mine) :]}
    mine = [sky] + [mine[hop] for hop in sorted(mine)]
    tiles = mine + [swapped(tile) for tile in mine]
    strips = [strips, swapped(strips)]
    place += len(mine) * other_core
    kind = jnp.where(kind > 0, kind + kinds * other_core, 0)
    ints = jnp.concatenate([place, counts[:, None], kind], axis=1)
    dsums = facets(tiles, strips, kern_u, kern_v, vis_data, ints, weights, squares)
    theirs = swapped(dsums)
    strips = mixed(dsums, theirs, scale, True)
    strips, dsums, theirs = lax.optimization_barrier((strips, dsums, theirs))
    send = paired if chips == 4 else chip_shift
    edges = [strips[0]] + [send(strips[hop], hop) for hop in hops]
    parts = mixed(dsums, theirs, scale, False)
    edges, _ = lax.optimization_barrier((edges, parts))
    around = (above, below, lefts, rights)
    if chips == 4:
        middle = by_chips(parts[3], ((1, 2), (2, 1)))
        onward = by_chips(parts[3], ((0, 1), (3, 2)))
    outgoing = adjoint(True, edges, around, fields)
    if chips == 4:
        onward, middle, parts, outgoing = lax.optimization_barrier(
            (onward, middle, parts, outgoing)
        )
        both = (parts[2].astype(f32) + onward.astype(f32)).astype(bf16)
        parts = [parts[0], paired(parts[1], 1), paired(both, 2), middle]
    else:
        parts = [parts[0]] + [chip_shift(parts[hop], hop) for hop in hops]
    to_left, to_right, upper, lower, total = outgoing
    size = lax.axis_size("gx")
    steps = [1 << i for i in range(size.bit_length()) if 1 << i < size]

    def across(x, hop):
        return lax.ppermute(x, "gx", [(i, i ^ hop) for i in range(size)])

    from_below = lax.ppermute(upper, "gx", up)
    from_above = lax.ppermute(lower, "gx", down)
    other = across(total, steps[0])
    rows, cols = xi_coarse.shape
    to_left, to_right, total = pl.pallas_call(
        functools.partial(corners_kernel, rows, cols),
        in_specs=[whole] * 6,
        out_specs=[whole] * 3,
        out_shape=[shape(*to_left.shape), shape(*to_right.shape), shape(8, 128)],
        name="corners",
    )(to_left, to_right, from_above, from_below, total, other)
    for hop in steps[1:-1]:
        total += across(total, hop)
    other = across(total, steps[-1])
    from_left = lax.ppermute(to_right, "gy", right)
    from_right = lax.ppermute(to_left, "gy", left)
    parts, from_left, from_right, other = lax.optimization_barrier(
        (parts, from_left, from_right, other)
    )
    cells = size * lax.axis_size("gy") * 16 * rows * cols
    arrived = (from_left, from_right, from_above, from_below, total, other)
    grad_fine, grad_middle, grad_coarse, total = adjoint(
        False, parts, around, fields, arrived, cells
    )
    return grad_coarse, grad_middle, grad_fine, total.reshape(())


def solution(mesh):
    placed = (
        P("gx", "gy"),
        P("gx", "gy"),
        P("gx", "gy"),
        P(None, None, "gx", "gy"),
        P(None, None, "gx", "gy"),
        P("gx", "gy", None, None),
        P("gx", "gy", None, None),
        P("gx", "gy", None, None),
        P("gx", "gy", None),
        P("gx", "gy", None),
        P("gx", "gy"),
    )
    return jax.shard_map(
        body,
        mesh=mesh,
        in_specs=placed,
        out_specs=(P("gx", "gy"), P("gx", "gy"), P("gx", "gy"), P()),
        check_vma=False,
    )
```

```python
import functools

import jax
import jax.numpy as jnp
from jax import lax
from jax.experimental import pallas as pl
from jax.experimental.pallas import tpu as pltpu
from jax.sharding import PartitionSpec as P

inv_noise = 0.125
long_work = pl.CostEstimate(flops=40_000_000_000, transcendentals=0, bytes_accessed=64_000_000)
border = 8
vmem = 32 * 1024 * 1024
f32 = jnp.float32
bf16 = jnp.bfloat16


def halves(x):
    high = x.astype(bf16)
    return high, (x - high.astype(f32)).astype(bf16)


def interleaver(cols, transposed):
    shape = (2 * cols, 2 * cols)
    split = lax.broadcasted_iota(jnp.int32, shape, 1 if transposed else 0)
    whole = lax.broadcasted_iota(jnp.int32, shape, 0 if transposed else 1)
    place = jnp.where(split >= cols, 2 * (split - cols) + 1, 2 * split)
    return (place == whole).astype(f32).astype(bf16)


def folded(x):
    rows, cols = x.shape
    x = jnp.sum(x.reshape(rows // 8, 8, cols), axis=0)
    return sum(x[:, i : i + 128] for i in range(0, cols, 128))


def row_of(ref, i):
    return ref[i : i + 1, :]


def dot_t(x, y, dims):
    return lax.dot_general(x, y, (dims, ((), ())), preferred_element_type=f32)


def moved(x, perm):
    high, low = halves(x)
    return jnp.dot(high, perm, preferred_element_type=f32) + jnp.dot(
        low, perm, preferred_element_type=f32
    )


def ends_placed(first, last, cols):
    rows = jnp.concatenate([first, first, last, last, jnp.zeros((4, first.shape[1]), f32)])
    high = rows.astype(bf16).astype(f32)
    index = lax.broadcasted_iota(jnp.int32, rows.shape, 0)
    rows = jnp.where(index % 2 == 0, high, rows - high).astype(bf16)
    shape = (8, cols)
    index = lax.broadcasted_iota(jnp.int32, shape, 0)
    lane = lax.broadcasted_iota(jnp.int32, shape, 1)
    place = ((index < 2) & (lane == 0)) | ((index >= 2) & (index < 4) & (lane == cols - 1))
    return dot_t(rows, place.astype(f32).astype(bf16), ((0,), (0,)))


def weighed(win, coef_ref, perm, lhs, mix, rows, cols, chunks=()):
    def part(i, carry):
        r0 = pl.multiple_of(i * 16, 16)
        total = [jnp.zeros((16, cols), f32) for _ in range(4)]
        for near in range(9):
            w = win[near, pl.ds(r0, 16), :]
            for child in range(4):
                total[child] += coef_ref[child, near, pl.ds(r0, 16), :].astype(f32) * w
        for child in range(4):
            a, b = child // 2, child % 2
            high, low = halves(total[child])
            lhs[pl.ds(2 * a * rows + r0, 16), b * cols : (b + 1) * cols] = high
            lhs[pl.ds((2 * a + 1) * rows + r0, 16), b * cols : (b + 1) * cols] = low
        return carry

    in_chunks(part, rows, chunks)
    field = jnp.dot(lhs[...], perm[...], preferred_element_type=f32)
    for tile in range(2 * cols // 128):
        lanes = slice(tile * 128, (tile + 1) * 128)
        for a in range(2):
            mix[tile, pl.ds(a, rows, stride=2), :] = (
                field[2 * a * rows : (2 * a + 1) * rows, lanes]
                + field[(2 * a + 1) * rows : (2 * a + 2) * rows, lanes]
            )


def fetched(pairs, sems, first=0):
    copies = [
        pltpu.make_async_copy(src, dst, sems.at[first + i]) for i, (src, dst) in enumerate(pairs)
    ]
    for copy in copies:
        copy.start()
    return copies


def chunked(source, target, sems):
    number, rows = sems.shape[0], source.shape[2] // sems.shape[0]
    copies = []
    for i in range(number):
        at = slice(i * rows, (i + 1) * rows)
        copies.append(pltpu.make_async_copy(source.at[:, :, at], target.at[:, :, at], sems.at[i]))
        copies[i].start()
    return copies


def in_chunks(part, rows, chunks):
    steps = rows // 16
    if not chunks:
        lax.fori_loop(0, steps, part, 0)
    for i, copy in enumerate(chunks):
        copy.wait()
        lax.fori_loop(i * steps // len(chunks), (i + 1) * steps // len(chunks), part, 0)


def columns_beside(field, left, right):
    rows, cols = field.shape[1:]
    placed = ends_placed(left, right, cols)
    lane = lax.broadcasted_iota(jnp.int32, (rows, cols), 1)
    here = field[1]
    field[0] = jnp.where(lane == 0, placed, pltpu.roll(here, 1, 1))
    field[2] = jnp.where(lane == cols - 1, placed, pltpu.roll(here, cols - 1, 1))


def strips_of(tile, out):
    rows, cols = tile.shape
    first, last = tile[: 2 * border].astype(f32), tile[rows - 2 * border :].astype(f32)
    out[: 2 * border] = jnp.concatenate([first[:border], last[border:]]).astype(bf16)
    index = lax.broadcasted_iota(jnp.int32, (2 * border, cols), 0)
    lane = lax.broadcasted_iota(jnp.int32, (2 * border, cols), 1)
    pick = lane == jnp.where(index < border, index, index + cols - 2 * border)
    pick = pick.astype(f32).astype(bf16)
    out[2 * border : 4 * border] = dot_t(pick, tile[...], ((1,), (1,))).astype(bf16)


def columns_of(strip):
    index = lax.broadcasted_iota(jnp.int32, (2 * border, 128), 0)
    lane = lax.broadcasted_iota(jnp.int32, (2 * border, 128), 1)
    out = []
    for place in (
        (index < border) & (lane == index),
        (index >= border) & (lane == index + 128 - 2 * border),
    ):
        out.append(dot_t(strip, place.astype(f32).astype(bf16), ((0,), (0,))))
    return out


def stretch(out, side, over, under, b, lane, first):
    rows = side.shape[1]
    out[...] = jnp.zeros_like(out)
    out[:, 2 : rows + 2] = side[...]
    out[9:18, 1:2] = over[9 * b : 9 * b + 9, lane : lane + 1]
    out[21:22, 1:2] = over[20 + b : 21 + b, lane : lane + 1]
    out[0:9, rows + 2 : rows + 3] = under[9 * b : 9 * b + 9, lane : lane + 1]
    out[20:21, rows + 2 : rows + 3] = under[20 + b : 21 + b, lane : lane + 1]
    for k in range(2):
        at = slice(first + k, first + k + 1)
        for i in range(2):
            out[18 + k : 19 + k, i : i + 1] = over[18 + i : 19 + i, at]
            end = rows + 2 + i
            out[18 + k : 19 + k, end : end + 1] = under[18 + i : 19 + i, at]


def sky_kernel(alone, *refs):
    count = 5 if alone else 11
    sources, refs = refs[:count], refs[count:]
    outs, refs = (refs[:1], refs[1:]) if alone else (refs[:5], refs[5:])
    held, rest = refs[:11], refs[11:]
    win, perm, lhs, mix, near_coarse, shifted, fine_win, fine_perm, fine_lhs, fine_mix = rest[:10]
    lefts, rights, to_left, to_right, sems, chunk_sems = rest[10:]
    sky_ref = outs[0]
    if alone:
        for ref in held[1:7]:
            ref[...] = jnp.zeros_like(ref)
        held_here = (held[0], *held[7:])
    else:
        held_here = held
    copies = fetched(zip(sources[:-2], held_here[:-2]), sems)
    chunks = chunked(sources[-2], held_here[-2], chunk_sems)
    copies += fetched(zip(sources[-1:], held_here[-1:]), sems, len(copies))
    xi_coarse, over, under, left_in, right_in, left_side, right_side = held[:7]
    coef_middle, xi_middle, coef_fine, xi_fine = held[7:]
    rows, cols = win.shape[1:]
    perm[...] = interleaver(cols, False)
    fine_perm[...] = interleaver(2 * cols, False)
    near_coarse[...] = jnp.zeros_like(near_coarse)
    for copy in copies[:-2]:
        copy.wait()
    above, below = over[:, 2 : cols + 2], under[:, 2 : cols + 2]
    if alone:
        for ref in (lefts, rights):
            ref[...] = jnp.zeros_like(ref)
    else:
        stretch(lefts, left_in, over, under, 1, 1, 0)
        stretch(rights, right_in, over, under, 0, cols + 2, cols + 2)
        stretch(to_left, left_side, over, under, 0, 2, 2)
        stretch(to_right, right_side, over, under, 1, cols + 1, cols)
    near_coarse[1, 6:8] = above[18:20]
    near_coarse[1, 8 : 8 + rows] = xi_coarse[...]
    near_coarse[1, 8 + rows : 10 + rows] = below[18:20]
    pad = jnp.zeros((1, 6), f32)
    beside = [
        jnp.concatenate([pad, row_of(x, i)[:, : rows + 4], pad], axis=1)
        for x, i in ((lefts, 19), (rights, 18))
    ]
    columns_beside(near_coarse, *beside)
    for near in range(9):
        r, c = near // 3, near % 3
        win[near] = near_coarse[c, 7 + r : 7 + r + rows]
    weighed(win, coef_middle, perm, lhs, mix, rows, cols)

    def across(message, top):
        out = []
        for b in range(2):
            line = row_of(message, 20 + b)
            for near in range(9):
                r, c = near // 3, near % 3
                line += row_of(message, 9 * b + near) * near_coarse[c, top + r : top + r + 1]
            out.append(line)
        return jnp.concatenate(out, axis=1)

    def along(message, fields):
        out = []
        for a in range(2):
            line = row_of(message, 20 + a)[:, 1 : rows + 3]
            for near in range(9):
                r, c = near // 3, near % 3
                line += row_of(message, 9 * a + near)[:, 1 : rows + 3] * fields[c][:, r : r + rows + 2]
            out.append(line)
        inner = jnp.concatenate([line[:, 1 : rows + 1] for line in out], axis=1)
        return inner, out[1][:, :1], out[0][:, rows + 1 :]

    if alone:
        empty = jnp.zeros((1, 1), f32)
        top = bottom = left = right = jnp.zeros((1, 2 * cols), f32)
        top_left = bottom_left = top_right = bottom_right = empty
    else:
        top, bottom = across(above, 6), across(below, rows + 7)
        left, top_left, bottom_left = along(
            lefts, [row_of(lefts, 18), row_of(lefts, 19), row_of(to_left, 18)]
        )
        right, top_right, bottom_right = along(
            rights, [row_of(to_right, 19), row_of(rights, 18), row_of(rights, 19)]
        )
    lines = jnp.concatenate([top, bottom, left, right, jnp.zeros((4, 2 * cols), f32)])
    lines = moved(lines, perm[...])
    copies[-2].wait()
    xi = xi_middle[...]
    last = 8 + 2 * rows
    shifted[1] = jnp.zeros(shifted.shape[1:], f32)
    for tile in range(2 * cols // 128):
        lanes = slice(tile * 128, (tile + 1) * 128)
        shifted[1, 8:last, lanes] = mix[tile] + xi[:, lanes]
    shifted[1, 7:8, :] = lines[0:1]
    shifted[1, last : last + 1, :] = lines[1:2]
    pad = jnp.zeros((1, 7), f32)
    beside = [
        jnp.concatenate([pad, first, line, final, pad], axis=1)
        for first, line, final in (
            (top_left, lines[2:3], bottom_left),
            (top_right, lines[3:4], bottom_right),
        )
    ]
    columns_beside(shifted, *beside)
    for near in range(9):
        r, c = near // 3, near % 3
        fine_win[near] = shifted[c, 7 + r : 7 + r + 2 * rows, :]
    weighed(fine_win, coef_fine, fine_perm, fine_lhs, fine_mix, 2 * rows, 2 * cols, chunks)
    copies[-1].wait()
    for tile in range(4 * cols // 128):
        lanes = slice(tile * 128, (tile + 1) * 128)
        sky_ref[:, lanes] = (fine_mix[tile] + xi_fine[:, lanes]).astype(bf16)
    if alone:
        return
    strips_ref, sq_ref, lefts_ref, rights_ref = outs[1:]
    lefts_ref[...] = lefts[...]
    rights_ref[...] = rights[...]
    strips_of(sky_ref, strips_ref)
    sq_ref[...] = (
        folded(win[4] * win[4]) + folded(xi * xi) + folded(xi_fine[...] * xi_fine[...])
    )


def sides_kernel(left_in, right_in, first_side, last_side, to_above, to_below):
    rows = left_in.shape[1]
    stretch(to_above, first_side, left_in, right_in, 0, 0, 0)
    stretch(to_below, last_side, left_in, right_in, 1, rows - 1, rows - 2)


def neighbours(axis):
    size = lax.axis_size(axis)
    ahead = [(i, i + 1) for i in range(size - 1)]
    return ahead, [(j, i) for i, j in ahead]


def halo_sides(xi_coarse, xi_middle, coef_middle):
    rows, cols = xi_coarse.shape

    def inside(b, col, near):
        return jnp.concatenate(
            [
                coef_middle[b::2, :, :, col].reshape(18, rows).astype(f32),
                near.T,
                xi_middle[:, 2 * col + b].reshape(rows, 2).T,
            ]
        )

    return inside(0, 0, xi_coarse[:, :2]), inside(1, cols - 1, xi_coarse[:, -2:])


def halo_rows(xi_coarse, xi_middle, coef_middle, left_in, right_in):
    rows, cols = xi_coarse.shape

    def edge(a, row, near):
        return jnp.concatenate(
            [
                coef_middle[2 * a : 2 * a + 2, :, row].reshape(18, cols).astype(f32),
                near,
                xi_middle[2 * row + a].reshape(cols, 2).T,
            ]
        )

    to_above, to_below = pl.pallas_call(
        sides_kernel,
        in_specs=[whole] * 4,
        out_specs=[whole] * 2,
        out_shape=[jax.ShapeDtypeStruct((22, cols + 4), f32)] * 2,
        cost_estimate=long_work,
        name="sides",
    )(left_in, right_in, edge(0, 0, xi_coarse[:2]), edge(1, rows - 1, xi_coarse[-2:]))
    down, up = neighbours("gx")
    return lax.ppermute(to_below, "gx", down), lax.ppermute(to_above, "gx", up)


whole = pl.BlockSpec(memory_space=pltpu.VMEM)
scalar = pl.BlockSpec(memory_space=pltpu.SMEM)
anywhere = pl.BlockSpec(memory_space=pltpu.HBM)


def sky_of(halos, xi_coarse, coef_middle, xi_middle, coef_fine, xi_fine):
    rows, cols = coef_middle.shape[2:]
    alone = halos is None
    given = (coef_middle, xi_middle, coef_fine, xi_fine)
    operands = (xi_coarse, *given) if alone else (xi_coarse, *halos, *given)
    message = [(22, cols + 4)] * 2 + [(22, rows)] * 4
    return pl.pallas_call(
        functools.partial(sky_kernel, alone),
        in_specs=[anywhere] * len(operands),
        out_specs=[whole] * (1 if alone else 5),
        out_shape=[
            jax.ShapeDtypeStruct((4 * rows, 4 * cols), bf16),
            jax.ShapeDtypeStruct((4 * border, 4 * cols), bf16),
            jax.ShapeDtypeStruct((8, 128), f32),
            jax.ShapeDtypeStruct((22, rows + 4), f32),
            jax.ShapeDtypeStruct((22, rows + 4), f32),
        ][: 1 if alone else 5],
        scratch_shapes=[pltpu.VMEM(xi_coarse.shape, f32)]
        + [pltpu.VMEM(shape, f32) for shape in message]
        + [pltpu.VMEM(x.shape, x.dtype) for x in given]
        + [
            pltpu.VMEM((9, rows, cols), f32),
            pltpu.VMEM((2 * cols, 2 * cols), bf16),
            pltpu.VMEM((4 * rows, 2 * cols), bf16),
            pltpu.VMEM((2 * cols // 128, 2 * rows, 128), f32),
            pltpu.VMEM((3, rows + 16, cols), f32),
            pltpu.VMEM((3, 2 * rows + 16, 2 * cols), f32),
            pltpu.VMEM((9, 2 * rows, 2 * cols), f32),
            pltpu.VMEM((4 * cols, 4 * cols), bf16),
            pltpu.VMEM((8 * rows, 4 * cols), bf16),
            pltpu.VMEM((4 * cols // 128, 4 * rows, 128), f32),
            *[pltpu.VMEM((22, rows + 4), f32) for _ in range(4)],
            pltpu.SemaphoreType.DMA((11,)),
            pltpu.SemaphoreType.DMA((4,)),
        ],
        compiler_params=pltpu.CompilerParams(vmem_limit_bytes=48 * 1024 * 1024),
        name="sky",
    )(*operands)


def spread(mix, coef_ref, terms, rows, cols, chunks=()):
    def part(i, carry):
        r0 = pl.multiple_of(i * 16, 16)
        quads = []
        for a in range(2):
            for b in range(2):
                tiles = range(b * cols // 128, (b + 1) * cols // 128)
                lines = [mix[t, pl.ds(2 * r0 + a, 16, stride=2), :] for t in tiles]
                quads.append(jnp.concatenate(lines, axis=1))
        for near in range(9):
            total = jnp.zeros((16, cols), f32)
            for child in range(4):
                total += coef_ref[child, near, pl.ds(r0, 16), :].astype(f32) * quads[child]
            terms[near, pl.ds(16 + r0, 16), :] = total
        return carry

    in_chunks(part, rows, chunks)


def row_sums(terms, rowed):
    rows = terms.shape[1] - 32
    for near in range(9):
        terms[near, :16] = jnp.zeros((16, terms.shape[2]), f32)
        terms[near, rows + 16 :] = jnp.zeros((16, terms.shape[2]), f32)
    for c in range(3):
        total = terms[c, 9 : rows + 25]
        for r in (1, 2):
            total += terms[3 * r + c, 9 - r : rows + 25 - r]
        rowed[c, : rows + 16] = total
        rowed[c, rows + 16 :] = jnp.zeros((rowed.shape[1] - rows - 16, rowed.shape[2]), f32)


def joined(rowed, cols):
    lane = lax.broadcasted_iota(jnp.int32, rowed.shape[1:], 1)
    main = (
        rowed[1]
        + jnp.where(lane == 0, 0.0, pltpu.roll(rowed[2], 1, 1))
        + jnp.where(lane == cols - 1, 0.0, pltpu.roll(rowed[0], cols - 1, 1))
    )
    lane = lax.broadcasted_iota(jnp.int32, (8, cols), 1)
    outside = []
    for c, col in ((0, 0), (2, cols - 1)):
        pick = (lane == col).astype(f32).astype(bf16)
        high, low = halves(rowed[c])
        out = dot_t(pick, high, ((1,), (1,))) + dot_t(pick, low, ((1,), (1,)))
        outside.append(out[:1])
    return main, outside[0], outside[1]


def adjoint_kernel(edge, number, cells, *refs):
    count = 6 if edge else 15
    written = 5 if edge else 4
    count += number
    sources, outs, refs = refs[:count], refs[count : count + written], refs[count + written :]
    parts, held, rest = refs[:number], refs[number:count], refs[count:]
    fine_perm, fine_mix, fine_terms, fine_rowed, perm, mix, terms, rowed, full, sems, chunk_sems, out_sem = rest
    arriving = fetched(zip(sources[:number], parts), sems)
    chunks = chunked(sources[number], held[0], chunk_sems)
    copies = [None] + fetched(zip(sources[number + 1 :], held[1:]), sems, number)
    coef_fine, coef_middle, over, under, lefts, rights = held[:6]
    if edge:
        left_ref, right_ref, upper_ref, lower_ref, total_ref = outs
    else:
        grad_ref, middle_ref, coarse_ref, total_ref = outs
        xi_fine, xi_middle, xi_coarse, from_left, from_right, from_above, from_below = held[6:13]
        total, other = held[13:]
    rows, cols = terms.shape[1] - 32, terms.shape[2]
    fine_perm[...] = interleaver(2 * cols, True)
    perm[...] = interleaver(cols, True)
    for copy in arriving:
        copy.wait()
    g = parts[0][...].astype(f32)
    for part in parts[1:]:
        g += part[...].astype(f32)
    if edge:
        tail = g[4 * border :, :128]
        total_ref[...] = tail[:8] + tail[8:16] + tail[16:24]
        high, low = halves(g[2 * border : 4 * border])
        left, right = [x + y for x, y in zip(columns_of(high), columns_of(low))]
        full[...] = jnp.zeros_like(full)
        full[:, :128] = left
        full[:, 4 * cols - 128 :] = right
        full[:border] = g[:border]
        full[4 * rows - border :] = g[border : 2 * border]
        g = full[...]
    else:
        copies[6].wait()
        full[...] = g + xi_fine[...]
        leaving = pltpu.make_async_copy(full, grad_ref, out_sem)
        leaving.start()
    split = moved(g, fine_perm[...])
    for tile in range(4 * cols // 128):
        fine_mix[tile] = split[:, tile * 128 : (tile + 1) * 128]
    spread(fine_mix, coef_fine, fine_terms, 2 * rows, 2 * cols, chunks)
    row_sums(fine_terms, fine_rowed)
    main, left, right = joined(fine_rowed, 2 * cols)
    last = 8 + 2 * rows
    inner = main[8:last]
    for copy in copies[1:6] + copies[7:]:
        copy.wait()
    above, below = over[:, 2 : cols + 2], under[:, 2 : cols + 2]
    if not edge:
        line = slice(1, 2 * rows + 1)
        middle_ref[...] = (
            inner
            + xi_middle[...]
            + ends_placed(from_left[2:3, line], from_right[2:3, line], 2 * cols)
        )
        middle_ref[:1] += from_above[2:3, 1 : 2 * cols + 1]
        middle_ref[2 * rows - 1 :] += from_below[2:3, 1 : 2 * cols + 1]
    split = moved(inner, perm[...])
    for tile in range(2 * cols // 128):
        mix[tile] = split[:, tile * 128 : (tile + 1) * 128]
    spread(mix, coef_middle, terms, rows, cols)
    ring_above, ring_below = main[7:8], main[last : last + 1]
    lines = [ring_above, ring_below, left[:, 8:last], right[:, 8:last]]
    lines = moved(jnp.concatenate(lines + [jnp.zeros((4, 2 * cols), f32)]), perm[...])
    row_sums(terms, rowed)
    for line, message, top in ((0, above, 6), (1, below, 7 + rows)):
        for near in range(9):
            r, c = near // 3, near % 3
            term = row_of(message, near) * lines[line : line + 1, :cols]
            term += row_of(message, 9 + near) * lines[line : line + 1, cols:]
            rowed[c, top + r : top + r + 1, :] += term

    def along(line, ends, message):
        empty = jnp.zeros((1, 1), f32)
        first = [empty, lines[line : line + 1, :rows], ends[:, last : last + 1]]
        second = [ends[:, 7:8], lines[line : line + 1, cols : cols + rows], empty]
        first, second = jnp.concatenate(first, axis=1), jnp.concatenate(second, axis=1)
        out = []
        for c in range(3):
            total = jnp.zeros((1, rows + 4), f32)
            for r in range(3):
                near = 3 * r + c
                term = row_of(message, near)[:, 1 : rows + 3] * first
                term += row_of(message, 9 + near)[:, 1 : rows + 3] * second
                pads = [jnp.zeros((1, n), f32) for n in (r, 2 - r) if n]
                pieces = [term] + pads if r == 0 else pads[:1] + [term] + pads[1:]
                total += jnp.concatenate(pieces, axis=1)
            out.append(total)
        return out

    outer_left = along(2, left, lefts)
    outer_right = along(3, right, rights)
    main, near_left, near_right = joined(rowed, cols)
    if not edge:
        line = slice(2, rows + 2)
        first = outer_left[2][:, line] + from_left[1:2, line]
        last = outer_right[0][:, line] + from_right[1:2, line]
        second = ends_placed(from_left[0:1, line], from_right[0:1, line], cols)
        lane = lax.broadcasted_iota(jnp.int32, second.shape, 1)
        second = jnp.where(lane == 1, pltpu.roll(second, 1, 1), 0.0) + jnp.where(
            lane == cols - 2, pltpu.roll(second, cols - 1, 1), 0.0
        )
        coarse_ref[...] = (
            main[8 : 8 + rows] + xi_coarse[...] + ends_placed(first, last, cols) + second
        )
        coarse_ref[:2] += from_above[0:2, 2 : cols + 2]
        coarse_ref[rows - 2 :] += from_below[0:2, 2 : cols + 2]
        both = total[...] + other[...]
        both = jnp.sum(jnp.sum(both, axis=1, keepdims=True), axis=0, keepdims=True)
        total_ref[...] = both * (1.0 / cells)
        leaving.wait()
        return
    sides = []
    for ref, far, close, beyond, ends in (
        (left_ref, outer_left[0], outer_left[1], near_left, left),
        (right_ref, outer_right[2], outer_right[1], near_right, right),
    ):
        close += beyond[:, 6 : rows + 10]
        ends = ends[:, 7 : 2 * rows + 9]
        ref[...] = jnp.zeros_like(ref)
        ref[0:1, : rows + 4] = far
        ref[1:2, : rows + 4] = close
        ref[2:3, : 2 * rows + 2] = ends
        sides.append((far, close, ends))
    lane = lax.broadcasted_iota(jnp.int32, (1, cols), 1)
    (far_left, close_left, ends_left), (far_right, close_right, ends_right) = sides
    for ref, first, line, end in (
        (upper_ref, 6, ring_above, 0),
        (lower_ref, 8 + rows, ring_below, 2 * rows + 1),
    ):
        ref[...] = jnp.zeros_like(ref)
        for i in range(2):
            at = slice(first - 6 + i, first - 5 + i)
            inner = (
                main[first + i : first + i + 1]
                + jnp.where(lane == 0, outer_left[2][:, at], 0.0)
                + jnp.where(lane == cols - 1, outer_right[0][:, at], 0.0)
            )
            pieces = [far_left[:, at], close_left[:, at], inner, close_right[:, at], far_right[:, at]]
            ref[i : i + 1, : cols + 4] = jnp.concatenate(pieces, axis=1)
        pieces = [ends_left[:, end : end + 1], line, ends_right[:, end : end + 1]]
        ref[2:3, : 2 * cols + 2] = jnp.concatenate(pieces, axis=1)


def corners_kernel(rows, cols, left, right, from_above, from_below, total, other, left_out, right_out, total_out):
    for ref, out, far, close, end in (
        (left, left_out, 0, 1, 0),
        (right, right_out, cols + 3, cols + 2, 2 * cols + 1),
    ):
        out[...] = ref[...]
        for rows_in, first, line in ((from_above, 2, 1), (from_below, rows, 2 * rows)):
            for i in range(2):
                at = slice(first + i, first + i + 1)
                out[0:1, at] += rows_in[i : i + 1, far : far + 1]
                out[1:2, at] += rows_in[i : i + 1, close : close + 1]
            out[2:3, line : line + 1] += rows_in[2:3, end : end + 1]
    total_out[...] = total[...] + other[...]


def shape(*dims):
    return jax.ShapeDtypeStruct(dims, f32)


def adjoint(edge, parts, sides, fields, arrived=(), cells=0):
    rows, cols = fields[1].shape[2:]
    xi_coarse, coef_middle, xi_middle, coef_fine, xi_fine = fields
    wide = 2 * rows + 128
    operands = (coef_fine, coef_middle, *sides)
    if edge:
        outs = [shape(8, wide)] * 2 + [shape(8, 2 * cols + 128)] * 2 + [shape(8, 128)]
    else:
        operands += (xi_fine, xi_middle, xi_coarse, *arrived)
        outs = [shape(4 * rows, 4 * cols), shape(2 * rows, 2 * cols), shape(rows, cols)]
        outs += [shape(1, 1)]
    return pl.pallas_call(
        functools.partial(adjoint_kernel, edge, len(parts), cells),
        in_specs=[anywhere] * (len(parts) + len(operands)),
        out_specs=[whole] * 5 if edge else [anywhere, whole, whole, whole],
        out_shape=outs,
        scratch_shapes=[pltpu.VMEM(x.shape, x.dtype) for x in (*parts, *operands)]
        + [
            pltpu.VMEM((4 * cols, 4 * cols), bf16),
            pltpu.VMEM((4 * cols // 128, 4 * rows, 128), f32),
            pltpu.VMEM((9, 2 * rows + 32, 2 * cols), f32),
            pltpu.VMEM((3, 2 * rows + 128, 2 * cols), f32),
            pltpu.VMEM((2 * cols, 2 * cols), bf16),
            pltpu.VMEM((2 * cols // 128, 2 * rows, 128), f32),
            pltpu.VMEM((9, rows + 32, cols), f32),
            pltpu.VMEM((3, rows + 128, cols), f32),
            pltpu.VMEM((4 * rows, 4 * cols), f32),
            pltpu.SemaphoreType.DMA((len(parts) + len(operands),)),
            pltpu.SemaphoreType.DMA((4,)),
            pltpu.SemaphoreType.DMA,
        ],
        compiler_params=pltpu.CompilerParams(vmem_limit_bytes=60 * 1024 * 1024),
        cost_estimate=long_work if edge else None,
        name="adjoint",
    )(*parts, *operands)


def in_three(x):
    high = x.astype(bf16).astype(f32)
    middle = (x - high).astype(bf16).astype(f32)
    return jnp.concatenate([high, middle, x - high - middle, jnp.zeros_like(x)]).astype(bf16)


def from_three(x):
    x = x.astype(f32)
    return x[:8] + x[8:16] + x[16:24]


def facets_kernel(blk, given, ints, weights, *refs):
    number, slots = weights.shape
    tiles, strips, rest = refs[:given], refs[given : given + 2], refs[given + 2 :]
    height = 4 * border
    kinds = strips[0].shape[0] // height
    ku_hbm, kv_hbm, data_hbm, squares, out_ref = rest[:5]
    held, held_strips, ku, kv, data, sums, dsum, total, sems, tile_sems, strip_sems = rest[5:]
    bins, side = ku.shape[1:]

    def inputs(f):
        for s in range(slots):
            for i, tile in enumerate(tiles):

                @pl.when(ints[f, s] == i)
                def _():
                    pltpu.make_async_copy(tile, held.at[f, s], tile_sems.at[f, s]).start()

            for i in range(2 * kinds):

                @pl.when(ints[f, slots + 1 + s] == i + 1)
                def _():
                    first = i % kinds * height
                    strip = strips[i // kinds].at[first : first + height]
                    pltpu.make_async_copy(strip, held_strips.at[f, s], strip_sems.at[f, s]).start()

        pairs = ((ku_hbm, ku), (kv_hbm, kv), (data_hbm, data))
        copies = [
            pltpu.make_async_copy(src.at[0, f], dst.at[f], sems.at[f, i])
            for i, (src, dst) in enumerate(pairs)
        ]
        for copy in copies:
            copy.start()
        return copies

    def patch(f, s):
        @pl.when(ints[f, slots + 1 + s] > 0)
        def _():
            strip = strips[0].at[:height]
            pltpu.make_async_copy(strip, held_strips.at[f, s], strip_sems.at[f, s]).wait()
            tile, strip = held.at[f, s], held_strips.at[f, s]
            lines = strip[: 2 * border].astype(f32)
            top, bottom = tile[: 2 * border].astype(f32), tile[side - 2 * border :].astype(f32)
            tile[: 2 * border] = jnp.concatenate([lines[:border], top[border:]]).astype(bf16)
            tile[side - 2 * border :] = jnp.concatenate([bottom[:border], lines[border:]]).astype(
                bf16
            )
            lane = lax.broadcasted_iota(jnp.int32, (side, 128), 1)
            left, right = columns_of(strip[2 * border :])
            for cells, inside, start in (
                (left, lane < border, 0),
                (right, lane >= 128 - border, side - 128),
            ):
                here = tile[:, start : start + 128].astype(f32)
                tile[:, start : start + 128] = jnp.where(inside, cells, here).astype(bf16)

    def work(f, step):
        rows = slice(step * blk, (step + 1) * blk)
        count = ints[f, slots] - step * blk

        @pl.when(count > 0)
        def _():
            amp = jnp.dot(ku[f, rows], sums[...], preferred_element_type=f32).astype(bf16)
            vis = dot_t(amp, kv[f], ((1,), (1,)))
            live = lax.broadcasted_iota(jnp.int32, vis.shape, 0) < count
            resid = jnp.where(live, vis - data[f, rows].astype(f32), 0.0)
            total[...] += 0.5 * inv_noise * folded(resid * resid)
            dvis = (inv_noise * resid).astype(bf16)
            damp = jnp.dot(dvis, kv[f], preferred_element_type=f32).astype(bf16)
            part = dot_t(ku[f, rows], damp, ((0,), (0,)))
            if step == 0:
                dsum[...] = part
            else:
                dsum[...] += part

    copies = [inputs(0)]
    total[...] = 0.5 * squares[...]
    for f in range(number):
        for s in range(slots):
            pltpu.make_async_copy(tiles[0], held.at[f, s], tile_sems.at[f, s]).wait()
            patch(f, s)
        copies[f][0].wait()
        if f + 1 < number:
            copies.append(inputs(f + 1))
        mixture = weights[f, 0] * held[f, 0].astype(f32)
        for s in range(1, slots):
            mixture += weights[f, s] * held[f, s].astype(f32)
        sums[...] = mixture.astype(bf16)
        copies[f][1].wait()
        copies[f][2].wait()
        for step in range(bins // blk):
            work(f, step)
        out_ref[f * side : (f + 1) * side] = dsum[...].astype(bf16)
    out_ref[number * side :] = jnp.zeros((32, side), bf16)
    out_ref[number * side :, :128] = in_three(total[...])


def facets(tiles, strips, ku, kv, data, ints, weights, squares):
    number, bins, side = ku.shape[1:]
    slots = weights.shape[1]
    return pl.pallas_call(
        functools.partial(facets_kernel, 512, len(tiles)),
        in_specs=[scalar] * 2 + [anywhere] * (len(tiles) + len(strips) + 3) + [whole],
        out_specs=whole,
        out_shape=jax.ShapeDtypeStruct((number * side + 32, side), bf16),
        scratch_shapes=[
            pltpu.VMEM((number, slots, side, side), bf16),
            pltpu.VMEM((number, slots, 4 * border, side), bf16),
            pltpu.VMEM((number, bins, side), bf16),
            pltpu.VMEM((number, bins, side), bf16),
            pltpu.VMEM((number, bins, bins), bf16),
            pltpu.VMEM((side, side), bf16),
            pltpu.VMEM((side, side), f32),
            pltpu.VMEM((8, 128), f32),
            pltpu.SemaphoreType.DMA((number, 3)),
            pltpu.SemaphoreType.DMA((number, slots)),
            pltpu.SemaphoreType.DMA((number, slots)),
        ],
        compiler_params=pltpu.CompilerParams(vmem_limit_bytes=47 * 1024 * 1024),
        name="facets",
    )(ints, weights, *tiles, *strips, ku, kv, data, squares)


def mix_kernel(scale, mine, theirs, *outs):
    side = outs[0].shape[1]
    number = mine.shape[0] // side
    for d, out in enumerate(outs):
        value = None
        for f in range(2 * number):
            ref, at = (mine, f) if f < number else (theirs, f - number)
            term = scale[d, f] * ref[at * side : (at + 1) * side].astype(f32)
            value = term if value is None else value + term
        out[...] = value.astype(bf16)


def mix_strips_kernel(scale, mine, theirs, *refs):
    outs, strips = refs[:-1], refs[-1]
    side = outs[0].shape[1]
    number = mine.shape[0] // side
    for f in range(2 * number):
        ref, at = (mine, f) if f < number else (theirs, f - number)
        strips_of(ref.at[at * side : (at + 1) * side], strips.at[f])
    total = from_three(mine[number * side :, :128]) + from_three(theirs[number * side :, :128])
    for d, out in enumerate(outs):
        value = None
        for f in range(2 * number):
            term = scale[d, f] * strips[f].astype(f32)
            value = term if value is None else value + term
        out[: 4 * border] = value.astype(bf16)
        out[4 * border :] = jnp.zeros((32, side), bf16)
        out[4 * border :, :128] = in_three(total)


def mixed(mine, theirs, scale, strips):
    side = mine.shape[1]
    rows = 4 * border + 32 if strips else side
    kept = [pltpu.VMEM((scale.shape[1], 4 * border, side), bf16)] if strips else []
    return pl.pallas_call(
        mix_strips_kernel if strips else mix_kernel,
        in_specs=[scalar, whole, whole],
        out_specs=[whole] * scale.shape[0],
        out_shape=[jax.ShapeDtypeStruct((rows, side), bf16)] * scale.shape[0],
        scratch_shapes=kept,
        compiler_params=pltpu.CompilerParams(vmem_limit_bytes=vmem),
        name="mixed",
    )(scale, mine, theirs)


def chip_shift(x, hop):
    size = lax.axis_size("gy")
    return lax.ppermute(x, "gy", [(i, (i + 2 * hop) % size) for i in range(size)])


def by_chips(x, pairs):
    return lax.ppermute(x, "gy", [(2 * a + c, 2 * b + c) for a, b in pairs for c in range(2)])


def paired(x, bits):
    return by_chips(x, [(i, i ^ bits) for i in range(lax.axis_size("gy") // 2)])


def swapped(x):
    return lax.ppermute(x, "gy", [(i, i ^ 1) for i in range(lax.axis_size("gy"))])


def body(
    xi_coarse,
    xi_middle,
    xi_fine,
    coef_middle,
    coef_fine,
    kern_u,
    kern_v,
    vis_data,
    facet_tiles,
    facet_weight,
    facet_count,
):
    fields = (xi_coarse, coef_middle, xi_middle, coef_fine, xi_fine)
    right, left = neighbours("gy")
    down, up = neighbours("gx")
    sides = halo_sides(xi_coarse, xi_middle, coef_middle)
    left_in = lax.ppermute(sides[1], "gy", right)
    right_in = lax.ppermute(sides[0], "gy", left)
    (first,) = sky_of(None, *fields)
    first, left_in, right_in, around, listed = lax.optimization_barrier(
        (
            first,
            left_in,
            right_in,
            (xi_coarse, xi_middle, coef_middle),
            (facet_tiles[0], facet_weight[0], facet_count[0]),
        )
    )
    lists, weights, counts = listed
    size = lax.axis_size("gy")
    chips = size // 2
    me = lax.axis_index("gy")
    ids = jnp.arange(size, dtype=jnp.int32)
    mixing = jnp.sum(
        weights[:, :, None] * (lists[:, :, None] == ids[None, None, :]).astype(f32), axis=1
    )
    steps = jnp.arange(chips, dtype=jnp.int32)
    order = (me // 2) ^ steps if chips == 4 else (me // 2 + steps) % chips
    order = 2 * order + me % 2
    scale = jnp.concatenate([mixing, swapped(mixing)])[:, order].T
    hops = range(1, chips)
    chip, other_core = me // 2, jnp.where(lists % 2 == me % 2, 0, 1)
    if chips == 4:
        mine = {1: paired(first, 1), 2: paired(first, 2)}
    else:
        mine = {hop: chip_shift(first, hop) for hop in range(1, min(3, chips))}
    above, below = halo_rows(*around, left_in, right_in)
    sky, strips, squares, lefts, rights = sky_of((above, below, left_in, right_in, *sides), *fields)
    if chips == 4:
        strips = [paired(strips, hop) for hop in hops]
        away = chip ^ (lists // 2)
        place = jnp.where((away == 3) & ((chip == 0) | (chip == 3)), 4, away)
        kind = away
    else:
        strips = [chip_shift(strips, hop) for hop in mine]
        place = away = (chip - lists // 2) % chips
        kind = jnp.where(away <= len(mine), away, 0)
    kinds = len(strips)
    strips = jnp.concatenate(strips)
    sky, strips, mine, scale, weights = lax.optimization_barrier(
        (sky, strips, mine, scale, weights)
    )
    if chips == 4:
        mine[3] = by_chips(sky, ((1, 2), (2, 1)))
        mine[4] = by_chips(mine[2], ((2, 3), (1, 0)))
    else:
        mine |= {hop: chip_shift(sky, hop) for hop in hops[len(mine) :]}
    mine = [sky] + [mine[hop] for hop in sorted(mine)]
    tiles = mine + [swapped(tile) for tile in mine]
    strips = [strips, swapped(strips)]
    place += len(mine) * other_core
    kind = jnp.where(kind > 0, kind + kinds * other_core, 0)
    ints = jnp.concatenate([place, counts[:, None], kind], axis=1)
    dsums = facets(tiles, strips, kern_u, kern_v, vis_data, ints, weights, squares)
    theirs = swapped(dsums)
    strips = mixed(dsums, theirs, scale, True)
    strips, dsums, theirs = lax.optimization_barrier((strips, dsums, theirs))
    send = paired if chips == 4 else chip_shift
    edges = [strips[0]] + [send(strips[hop], hop) for hop in hops]
    parts = mixed(dsums, theirs, scale, False)
    edges, _ = lax.optimization_barrier((edges, parts))
    around = (above, below, lefts, rights)
    if chips == 4:
        middle = by_chips(parts[3], ((1, 2), (2, 1)))
        onward = by_chips(parts[3], ((0, 1), (3, 2)))
    outgoing = adjoint(True, edges, around, fields)
    if chips == 4:
        onward, middle, parts, outgoing = lax.optimization_barrier(
            (onward, middle, parts, outgoing)
        )
        both = (parts[2].astype(f32) + onward.astype(f32)).astype(bf16)
        parts = [parts[0], paired(parts[1], 1), paired(both, 2), middle]
    else:
        parts = [parts[0]] + [chip_shift(parts[hop], hop) for hop in hops]
    to_left, to_right, upper, lower, total = outgoing
    size = lax.axis_size("gx")
    steps = [1 << i for i in range(size.bit_length()) if 1 << i < size]

    def across(x, hop):
        return lax.ppermute(x, "gx", [(i, i ^ hop) for i in range(size)])

    from_below = lax.ppermute(upper, "gx", up)
    from_above = lax.ppermute(lower, "gx", down)
    other = across(total, steps[0])
    rows, cols = xi_coarse.shape
    to_left, to_right, total = pl.pallas_call(
        functools.partial(corners_kernel, rows, cols),
        in_specs=[whole] * 6,
        out_specs=[whole] * 3,
        out_shape=[shape(*to_left.shape), shape(*to_right.shape), shape(8, 128)],
        name="corners",
    )(to_left, to_right, from_above, from_below, total, other)
    for hop in steps[1:-1]:
        total += across(total, hop)
    other = across(total, steps[-1])
    from_left = lax.ppermute(to_right, "gy", right)
    from_right = lax.ppermute(to_left, "gy", left)
    parts, from_left, from_right, other = lax.optimization_barrier(
        (parts, from_left, from_right, other)
    )
    cells = size * lax.axis_size("gy") * 16 * rows * cols
    arrived = (from_left, from_right, from_above, from_below, total, other)
    grad_fine, grad_middle, grad_coarse, total = adjoint(
        False, parts, around, fields, arrived, cells
    )
    return grad_coarse, grad_middle, grad_fine, total.reshape(())


def solution(mesh):
    placed = (
        P("gx", "gy"),
        P("gx", "gy"),
        P("gx", "gy"),
        P(None, None, "gx", "gy"),
        P(None, None, "gx", "gy"),
        P("gx", "gy", None, None),
        P("gx", "gy", None, None),
        P("gx", "gy", None, None),
        P("gx", "gy", None),
        P("gx", "gy", None),
        P("gx", "gy"),
    )
    return jax.shard_map(
        body,
        mesh=mesh,
        in_specs=placed,
        out_specs=(P("gx", "gy"), P("gx", "gy"), P("gx", "gy"), P()),
        check_vma=False,
    )
```

```python
import functools

import jax
import jax.numpy as jnp
from jax import lax
from jax.experimental import pallas as pl
from jax.experimental.pallas import tpu as pltpu
from jax.sharding import PartitionSpec as P

inv_noise = 0.125
long_work = pl.CostEstimate(flops=40_000_000_000, transcendentals=0, bytes_accessed=64_000_000)
border = 8
vmem = 32 * 1024 * 1024
f32 = jnp.float32
bf16 = jnp.bfloat16


def halves(x):
    high = x.astype(bf16)
    return high, (x - high.astype(f32)).astype(bf16)


def interleaver(cols, transposed):
    shape = (2 * cols, 2 * cols)
    split = lax.broadcasted_iota(jnp.int32, shape, 1 if transposed else 0)
    whole = lax.broadcasted_iota(jnp.int32, shape, 0 if transposed else 1)
    place = jnp.where(split >= cols, 2 * (split - cols) + 1, 2 * split)
    return (place == whole).astype(f32).astype(bf16)


def folded(x):
    rows, cols = x.shape
    x = jnp.sum(x.reshape(rows // 8, 8, cols), axis=0)
    return sum(x[:, i : i + 128] for i in range(0, cols, 128))


def row_of(ref, i):
    return ref[i : i + 1, :]


def dot_t(x, y, dims):
    return lax.dot_general(x, y, (dims, ((), ())), preferred_element_type=f32)


def moved(x, perm):
    high, low = halves(x)
    return jnp.dot(high, perm, preferred_element_type=f32) + jnp.dot(
        low, perm, preferred_element_type=f32
    )


def ends_placed(first, last, cols):
    rows = jnp.concatenate([first, first, last, last, jnp.zeros((4, first.shape[1]), f32)])
    high = rows.astype(bf16).astype(f32)
    index = lax.broadcasted_iota(jnp.int32, rows.shape, 0)
    rows = jnp.where(index % 2 == 0, high, rows - high).astype(bf16)
    shape = (8, cols)
    index = lax.broadcasted_iota(jnp.int32, shape, 0)
    lane = lax.broadcasted_iota(jnp.int32, shape, 1)
    place = ((index < 2) & (lane == 0)) | ((index >= 2) & (index < 4) & (lane == cols - 1))
    return dot_t(rows, place.astype(f32).astype(bf16), ((0,), (0,)))


def weighed(win, coef_ref, perm, lhs, mix, rows, cols, chunks=()):
    def part(i, carry):
        r0 = pl.multiple_of(i * 16, 16)
        total = [jnp.zeros((16, cols), f32) for _ in range(4)]
        for near in range(9):
            w = win[near, pl.ds(r0, 16), :]
            for child in range(4):
                total[child] += coef_ref[child, near, pl.ds(r0, 16), :].astype(f32) * w
        for child in range(4):
            a, b = child // 2, child % 2
            high, low = halves(total[child])
            lhs[pl.ds(2 * a * rows + r0, 16), b * cols : (b + 1) * cols] = high
            lhs[pl.ds((2 * a + 1) * rows + r0, 16), b * cols : (b + 1) * cols] = low
        return carry

    in_chunks(part, rows, chunks)
    field = jnp.dot(lhs[...], perm[...], preferred_element_type=f32)
    for tile in range(2 * cols // 128):
        lanes = slice(tile * 128, (tile + 1) * 128)
        for a in range(2):
            mix[tile, pl.ds(a, rows, stride=2), :] = (
                field[2 * a * rows : (2 * a + 1) * rows, lanes]
                + field[(2 * a + 1) * rows : (2 * a + 2) * rows, lanes]
            )


def fetched(pairs, sems, first=0):
    copies = [
        pltpu.make_async_copy(src, dst, sems.at[first + i]) for i, (src, dst) in enumerate(pairs)
    ]
    for copy in copies:
        copy.start()
    return copies


def chunked(source, target, sems):
    number, rows = sems.shape[0], source.shape[2] // sems.shape[0]
    copies = []
    for i in range(number):
        at = slice(i * rows, (i + 1) * rows)
        copies.append(pltpu.make_async_copy(source.at[:, :, at], target.at[:, :, at], sems.at[i]))
        copies[i].start()
    return copies


def in_chunks(part, rows, chunks):
    steps = rows // 16
    if not chunks:
        lax.fori_loop(0, steps, part, 0)
    for i, copy in enumerate(chunks):
        copy.wait()
        lax.fori_loop(i * steps // len(chunks), (i + 1) * steps // len(chunks), part, 0)


def columns_beside(field, left, right):
    rows, cols = field.shape[1:]
    placed = ends_placed(left, right, cols)
    lane = lax.broadcasted_iota(jnp.int32, (rows, cols), 1)
    here = field[1]
    field[0] = jnp.where(lane == 0, placed, pltpu.roll(here, 1, 1))
    field[2] = jnp.where(lane == cols - 1, placed, pltpu.roll(here, cols - 1, 1))


def strips_of(tile, out):
    rows, cols = tile.shape
    first, last = tile[: 2 * border].astype(f32), tile[rows - 2 * border :].astype(f32)
    out[: 2 * border] = jnp.concatenate([first[:border], last[border:]]).astype(bf16)
    index = lax.broadcasted_iota(jnp.int32, (2 * border, cols), 0)
    lane = lax.broadcasted_iota(jnp.int32, (2 * border, cols), 1)
    pick = lane == jnp.where(index < border, index, index + cols - 2 * border)
    pick = pick.astype(f32).astype(bf16)
    out[2 * border : 4 * border] = dot_t(pick, tile[...], ((1,), (1,))).astype(bf16)


def columns_of(strip):
    index = lax.broadcasted_iota(jnp.int32, (2 * border, 128), 0)
    lane = lax.broadcasted_iota(jnp.int32, (2 * border, 128), 1)
    out = []
    for place in (
        (index < border) & (lane == index),
        (index >= border) & (lane == index + 128 - 2 * border),
    ):
        out.append(dot_t(strip, place.astype(f32).astype(bf16), ((0,), (0,))))
    return out


def stretch(out, side, over, under, b, lane, first):
    rows = side.shape[1]
    out[...] = jnp.zeros_like(out)
    out[:, 2 : rows + 2] = side[...]
    out[9:18, 1:2] = over[9 * b : 9 * b + 9, lane : lane + 1]
    out[21:22, 1:2] = over[20 + b : 21 + b, lane : lane + 1]
    out[0:9, rows + 2 : rows + 3] = under[9 * b : 9 * b + 9, lane : lane + 1]
    out[20:21, rows + 2 : rows + 3] = under[20 + b : 21 + b, lane : lane + 1]
    for k in range(2):
        at = slice(first + k, first + k + 1)
        for i in range(2):
            out[18 + k : 19 + k, i : i + 1] = over[18 + i : 19 + i, at]
            end = rows + 2 + i
            out[18 + k : 19 + k, end : end + 1] = under[18 + i : 19 + i, at]


def sky_kernel(alone, *refs):
    count = 5 if alone else 11
    sources, refs = refs[:count], refs[count:]
    outs, refs = (refs[:1], refs[1:]) if alone else (refs[:5], refs[5:])
    held, rest = refs[:11], refs[11:]
    win, perm, lhs, mix, near_coarse, shifted, fine_win, fine_perm, fine_lhs, fine_mix = rest[:10]
    lefts, rights, to_left, to_right, sems, chunk_sems = rest[10:]
    sky_ref = outs[0]
    if alone:
        for ref in held[1:7]:
            ref[...] = jnp.zeros_like(ref)
        held_here = (held[0], *held[7:])
    else:
        held_here = held
    copies = fetched(zip(sources[:-2], held_here[:-2]), sems)
    chunks = chunked(sources[-2], held_here[-2], chunk_sems)
    copies += fetched(zip(sources[-1:], held_here[-1:]), sems, len(copies))
    xi_coarse, over, under, left_in, right_in, left_side, right_side = held[:7]
    coef_middle, xi_middle, coef_fine, xi_fine = held[7:]
    rows, cols = win.shape[1:]
    perm[...] = interleaver(cols, False)
    fine_perm[...] = interleaver(2 * cols, False)
    near_coarse[...] = jnp.zeros_like(near_coarse)
    for copy in copies[:-2]:
        copy.wait()
    above, below = over[:, 2 : cols + 2], under[:, 2 : cols + 2]
    if alone:
        for ref in (lefts, rights):
            ref[...] = jnp.zeros_like(ref)
    else:
        stretch(lefts, left_in, over, under, 1, 1, 0)
        stretch(rights, right_in, over, under, 0, cols + 2, cols + 2)
        stretch(to_left, left_side, over, under, 0, 2, 2)
        stretch(to_right, right_side, over, under, 1, cols + 1, cols)
    near_coarse[1, 6:8] = above[18:20]
    near_coarse[1, 8 : 8 + rows] = xi_coarse[...]
    near_coarse[1, 8 + rows : 10 + rows] = below[18:20]
    pad = jnp.zeros((1, 6), f32)
    beside = [
        jnp.concatenate([pad, row_of(x, i)[:, : rows + 4], pad], axis=1)
        for x, i in ((lefts, 19), (rights, 18))
    ]
    columns_beside(near_coarse, *beside)
    for near in range(9):
        r, c = near // 3, near % 3
        win[near] = near_coarse[c, 7 + r : 7 + r + rows]
    weighed(win, coef_middle, perm, lhs, mix, rows, cols)

    def across(message, top):
        out = []
        for b in range(2):
            line = row_of(message, 20 + b)
            for near in range(9):
                r, c = near // 3, near % 3
                line += row_of(message, 9 * b + near) * near_coarse[c, top + r : top + r + 1]
            out.append(line)
        return jnp.concatenate(out, axis=1)

    def along(message, fields):
        out = []
        for a in range(2):
            line = row_of(message, 20 + a)[:, 1 : rows + 3]
            for near in range(9):
                r, c = near // 3, near % 3
                line += row_of(message, 9 * a + near)[:, 1 : rows + 3] * fields[c][:, r : r + rows + 2]
            out.append(line)
        inner = jnp.concatenate([line[:, 1 : rows + 1] for line in out], axis=1)
        return inner, out[1][:, :1], out[0][:, rows + 1 :]

    if alone:
        empty = jnp.zeros((1, 1), f32)
        top = bottom = left = right = jnp.zeros((1, 2 * cols), f32)
        top_left = bottom_left = top_right = bottom_right = empty
    else:
        top, bottom = across(above, 6), across(below, rows + 7)
        left, top_left, bottom_left = along(
            lefts, [row_of(lefts, 18), row_of(lefts, 19), row_of(to_left, 18)]
        )
        right, top_right, bottom_right = along(
            rights, [row_of(to_right, 19), row_of(rights, 18), row_of(rights, 19)]
        )
    lines = jnp.concatenate([top, bottom, left, right, jnp.zeros((4, 2 * cols), f32)])
    lines = moved(lines, perm[...])
    copies[-2].wait()
    xi = xi_middle[...]
    last = 8 + 2 * rows
    shifted[1] = jnp.zeros(shifted.shape[1:], f32)
    for tile in range(2 * cols // 128):
        lanes = slice(tile * 128, (tile + 1) * 128)
        shifted[1, 8:last, lanes] = mix[tile, : 2 * rows] + xi[:, lanes]
    shifted[1, 7:8, :] = lines[0:1]
    shifted[1, last : last + 1, :] = lines[1:2]
    pad = jnp.zeros((1, 7), f32)
    beside = [
        jnp.concatenate([pad, first, line, final, pad], axis=1)
        for first, line, final in (
            (top_left, lines[2:3], bottom_left),
            (top_right, lines[3:4], bottom_right),
        )
    ]
    columns_beside(shifted, *beside)
    for near in range(9):
        r, c = near // 3, near % 3
        fine_win[near] = shifted[c, 7 + r : 7 + r + 2 * rows, :]
    weighed(fine_win, coef_fine, fine_perm, fine_lhs, fine_mix, 2 * rows, 2 * cols, chunks)
    copies[-1].wait()
    for tile in range(4 * cols // 128):
        lanes = slice(tile * 128, (tile + 1) * 128)
        sky_ref[:, lanes] = (fine_mix[tile, : 4 * rows] + xi_fine[:, lanes]).astype(bf16)
    if alone:
        return
    strips_ref, sq_ref, lefts_ref, rights_ref = outs[1:]
    lefts_ref[...] = lefts[...]
    rights_ref[...] = rights[...]
    strips_of(sky_ref, strips_ref)
    sq_ref[...] = (
        folded(win[4] * win[4]) + folded(xi * xi) + folded(xi_fine[...] * xi_fine[...])
    )


def sides_kernel(left_in, right_in, first_side, last_side, to_above, to_below):
    rows = left_in.shape[1]
    stretch(to_above, first_side, left_in, right_in, 0, 0, 0)
    stretch(to_below, last_side, left_in, right_in, 1, rows - 1, rows - 2)


def neighbours(axis):
    size = lax.axis_size(axis)
    ahead = [(i, i + 1) for i in range(size - 1)]
    return ahead, [(j, i) for i, j in ahead]


def halo_sides(xi_coarse, xi_middle, coef_middle):
    rows, cols = xi_coarse.shape

    def inside(b, col, near):
        return jnp.concatenate(
            [
                coef_middle[b::2, :, :, col].reshape(18, rows).astype(f32),
                near.T,
                xi_middle[:, 2 * col + b].reshape(rows, 2).T,
            ]
        )

    return inside(0, 0, xi_coarse[:, :2]), inside(1, cols - 1, xi_coarse[:, -2:])


def halo_rows(xi_coarse, xi_middle, coef_middle, left_in, right_in):
    rows, cols = xi_coarse.shape

    def edge(a, row, near):
        return jnp.concatenate(
            [
                coef_middle[2 * a : 2 * a + 2, :, row].reshape(18, cols).astype(f32),
                near,
                xi_middle[2 * row + a].reshape(cols, 2).T,
            ]
        )

    to_above, to_below = pl.pallas_call(
        sides_kernel,
        in_specs=[whole] * 4,
        out_specs=[whole] * 2,
        out_shape=[jax.ShapeDtypeStruct((22, cols + 4), f32)] * 2,
        cost_estimate=long_work,
        name="sides",
    )(left_in, right_in, edge(0, 0, xi_coarse[:2]), edge(1, rows - 1, xi_coarse[-2:]))
    down, up = neighbours("gx")
    return lax.ppermute(to_below, "gx", down), lax.ppermute(to_above, "gx", up)


whole = pl.BlockSpec(memory_space=pltpu.VMEM)
scalar = pl.BlockSpec(memory_space=pltpu.SMEM)
anywhere = pl.BlockSpec(memory_space=pltpu.HBM)


def sky_of(halos, xi_coarse, coef_middle, xi_middle, coef_fine, xi_fine):
    rows, cols = coef_middle.shape[2:]
    alone = halos is None
    given = (coef_middle, xi_middle, coef_fine, xi_fine)
    operands = (xi_coarse, *given) if alone else (xi_coarse, *halos, *given)
    message = [(22, cols + 4)] * 2 + [(22, rows)] * 4
    return pl.pallas_call(
        functools.partial(sky_kernel, alone),
        in_specs=[anywhere] * len(operands),
        out_specs=[whole] * (1 if alone else 5),
        out_shape=[
            jax.ShapeDtypeStruct((4 * rows, 4 * cols), bf16),
            jax.ShapeDtypeStruct((4 * border, 4 * cols), bf16),
            jax.ShapeDtypeStruct((8, 128), f32),
            jax.ShapeDtypeStruct((22, rows + 4), f32),
            jax.ShapeDtypeStruct((22, rows + 4), f32),
        ][: 1 if alone else 5],
        scratch_shapes=[pltpu.VMEM(xi_coarse.shape, f32)]
        + [pltpu.VMEM(shape, f32) for shape in message]
        + [pltpu.VMEM(x.shape, x.dtype) for x in given]
        + [
            pltpu.VMEM((9, rows, cols), f32),
            pltpu.VMEM((2 * cols, 2 * cols), bf16),
            pltpu.VMEM((4 * rows, 2 * cols), bf16),
            pltpu.VMEM((2 * cols // 128, 2 * rows + 8, 128), f32),
            pltpu.VMEM((3, rows + 16, cols), f32),
            pltpu.VMEM((3, 2 * rows + 16, 2 * cols), f32),
            pltpu.VMEM((9, 2 * rows, 2 * cols), f32),
            pltpu.VMEM((4 * cols, 4 * cols), bf16),
            pltpu.VMEM((8 * rows, 4 * cols), bf16),
            pltpu.VMEM((4 * cols // 128, 4 * rows + 8, 128), f32),
            *[pltpu.VMEM((22, rows + 4), f32) for _ in range(4)],
            pltpu.SemaphoreType.DMA((11,)),
            pltpu.SemaphoreType.DMA((4,)),
        ],
        compiler_params=pltpu.CompilerParams(vmem_limit_bytes=48 * 1024 * 1024),
        name="sky",
    )(*operands)


def spread(mix, coef_ref, terms, rows, cols, chunks=()):
    def part(i, carry):
        r0 = pl.multiple_of(i * 16, 16)
        quads = []
        for a in range(2):
            for b in range(2):
                tiles = range(b * cols // 128, (b + 1) * cols // 128)
                lines = [mix[t, pl.ds(2 * r0 + a, 16, stride=2), :] for t in tiles]
                quads.append(jnp.concatenate(lines, axis=1))
        for near in range(9):
            total = jnp.zeros((16, cols), f32)
            for child in range(4):
                total += coef_ref[child, near, pl.ds(r0, 16), :].astype(f32) * quads[child]
            terms[near, pl.ds(16 + r0, 16), :] = total
        return carry

    in_chunks(part, rows, chunks)


def row_sums(terms, rowed):
    rows = terms.shape[1] - 32
    for near in range(9):
        terms[near, :16] = jnp.zeros((16, terms.shape[2]), f32)
        terms[near, rows + 16 :] = jnp.zeros((16, terms.shape[2]), f32)
    for c in range(3):
        total = terms[c, 9 : rows + 25]
        for r in (1, 2):
            total += terms[3 * r + c, 9 - r : rows + 25 - r]
        rowed[c, : rows + 16] = total
        rowed[c, rows + 16 :] = jnp.zeros((rowed.shape[1] - rows - 16, rowed.shape[2]), f32)


def joined(rowed, cols):
    lane = lax.broadcasted_iota(jnp.int32, rowed.shape[1:], 1)
    main = (
        rowed[1]
        + jnp.where(lane == 0, 0.0, pltpu.roll(rowed[2], 1, 1))
        + jnp.where(lane == cols - 1, 0.0, pltpu.roll(rowed[0], cols - 1, 1))
    )
    lane = lax.broadcasted_iota(jnp.int32, (8, cols), 1)
    outside = []
    for c, col in ((0, 0), (2, cols - 1)):
        pick = (lane == col).astype(f32).astype(bf16)
        high, low = halves(rowed[c])
        out = dot_t(pick, high, ((1,), (1,))) + dot_t(pick, low, ((1,), (1,)))
        outside.append(out[:1])
    return main, outside[0], outside[1]


def adjoint_kernel(edge, number, cells, *refs):
    count = 6 if edge else 15
    written = 5 if edge else 4
    count += number
    sources, outs, refs = refs[:count], refs[count : count + written], refs[count + written :]
    parts, held, rest = refs[:number], refs[number:count], refs[count:]
    fine_perm, fine_mix, fine_terms, fine_rowed, perm, mix, terms, rowed, full, sems, chunk_sems, out_sem = rest
    arriving = fetched(zip(sources[:number], parts), sems)
    chunks = chunked(sources[number], held[0], chunk_sems)
    copies = [None] + fetched(zip(sources[number + 1 :], held[1:]), sems, number)
    coef_fine, coef_middle, over, under, lefts, rights = held[:6]
    if edge:
        left_ref, right_ref, upper_ref, lower_ref, total_ref = outs
    else:
        grad_ref, middle_ref, coarse_ref, total_ref = outs
        xi_fine, xi_middle, xi_coarse, from_left, from_right, from_above, from_below = held[6:13]
        total, other = held[13:]
    rows, cols = terms.shape[1] - 32, terms.shape[2]
    fine_perm[...] = interleaver(2 * cols, True)
    perm[...] = interleaver(cols, True)
    for copy in arriving:
        copy.wait()
    g = parts[0][...].astype(f32)
    for part in parts[1:]:
        g += part[...].astype(f32)
    if edge:
        tail = g[4 * border :, :128]
        total_ref[...] = tail[:8] + tail[8:16] + tail[16:24]
        high, low = halves(g[2 * border : 4 * border])
        left, right = [x + y for x, y in zip(columns_of(high), columns_of(low))]
        full[...] = jnp.zeros_like(full)
        full[:, :128] = left
        full[:, 4 * cols - 128 :] = right
        full[:border] = g[:border]
        full[4 * rows - border :] = g[border : 2 * border]
        g = full[...]
    else:
        copies[6].wait()
        full[...] = g + xi_fine[...]
        leaving = pltpu.make_async_copy(full, grad_ref, out_sem)
        leaving.start()
    split = moved(g, fine_perm[...])
    for tile in range(4 * cols // 128):
        fine_mix[tile, : 4 * rows] = split[:, tile * 128 : (tile + 1) * 128]
    spread(fine_mix, coef_fine, fine_terms, 2 * rows, 2 * cols, chunks)
    row_sums(fine_terms, fine_rowed)
    main, left, right = joined(fine_rowed, 2 * cols)
    last = 8 + 2 * rows
    inner = main[8:last]
    for copy in copies[1:6] + copies[7:]:
        copy.wait()
    above, below = over[:, 2 : cols + 2], under[:, 2 : cols + 2]
    if not edge:
        line = slice(1, 2 * rows + 1)
        middle_ref[...] = (
            inner
            + xi_middle[...]
            + ends_placed(from_left[2:3, line], from_right[2:3, line], 2 * cols)
        )
        middle_ref[:1] += from_above[2:3, 1 : 2 * cols + 1]
        middle_ref[2 * rows - 1 :] += from_below[2:3, 1 : 2 * cols + 1]
    split = moved(inner, perm[...])
    for tile in range(2 * cols // 128):
        mix[tile, : 2 * rows] = split[:, tile * 128 : (tile + 1) * 128]
    spread(mix, coef_middle, terms, rows, cols)
    ring_above, ring_below = main[7:8], main[last : last + 1]
    lines = [ring_above, ring_below, left[:, 8:last], right[:, 8:last]]
    lines = moved(jnp.concatenate(lines + [jnp.zeros((4, 2 * cols), f32)]), perm[...])
    row_sums(terms, rowed)
    for line, message, top in ((0, above, 6), (1, below, 7 + rows)):
        for near in range(9):
            r, c = near // 3, near % 3
            term = row_of(message, near) * lines[line : line + 1, :cols]
            term += row_of(message, 9 + near) * lines[line : line + 1, cols:]
            rowed[c, top + r : top + r + 1, :] += term

    def along(line, ends, message):
        empty = jnp.zeros((1, 1), f32)
        first = [empty, lines[line : line + 1, :rows], ends[:, last : last + 1]]
        second = [ends[:, 7:8], lines[line : line + 1, cols : cols + rows], empty]
        first, second = jnp.concatenate(first, axis=1), jnp.concatenate(second, axis=1)
        out = []
        for c in range(3):
            total = jnp.zeros((1, rows + 4), f32)
            for r in range(3):
                near = 3 * r + c
                term = row_of(message, near)[:, 1 : rows + 3] * first
                term += row_of(message, 9 + near)[:, 1 : rows + 3] * second
                pads = [jnp.zeros((1, n), f32) for n in (r, 2 - r) if n]
                pieces = [term] + pads if r == 0 else pads[:1] + [term] + pads[1:]
                total += jnp.concatenate(pieces, axis=1)
            out.append(total)
        return out

    outer_left = along(2, left, lefts)
    outer_right = along(3, right, rights)
    main, near_left, near_right = joined(rowed, cols)
    if not edge:
        line = slice(2, rows + 2)
        first = outer_left[2][:, line] + from_left[1:2, line]
        last = outer_right[0][:, line] + from_right[1:2, line]
        second = ends_placed(from_left[0:1, line], from_right[0:1, line], cols)
        lane = lax.broadcasted_iota(jnp.int32, second.shape, 1)
        second = jnp.where(lane == 1, pltpu.roll(second, 1, 1), 0.0) + jnp.where(
            lane == cols - 2, pltpu.roll(second, cols - 1, 1), 0.0
        )
        coarse_ref[...] = (
            main[8 : 8 + rows] + xi_coarse[...] + ends_placed(first, last, cols) + second
        )
        coarse_ref[:2] += from_above[0:2, 2 : cols + 2]
        coarse_ref[rows - 2 :] += from_below[0:2, 2 : cols + 2]
        both = total[...] + other[...]
        both = jnp.sum(jnp.sum(both, axis=1, keepdims=True), axis=0, keepdims=True)
        total_ref[...] = both * (1.0 / cells)
        leaving.wait()
        return
    sides = []
    for ref, far, close, beyond, ends in (
        (left_ref, outer_left[0], outer_left[1], near_left, left),
        (right_ref, outer_right[2], outer_right[1], near_right, right),
    ):
        close += beyond[:, 6 : rows + 10]
        ends = ends[:, 7 : 2 * rows + 9]
        ref[...] = jnp.zeros_like(ref)
        ref[0:1, : rows + 4] = far
        ref[1:2, : rows + 4] = close
        ref[2:3, : 2 * rows + 2] = ends
        sides.append((far, close, ends))
    lane = lax.broadcasted_iota(jnp.int32, (1, cols), 1)
    (far_left, close_left, ends_left), (far_right, close_right, ends_right) = sides
    for ref, first, line, end in (
        (upper_ref, 6, ring_above, 0),
        (lower_ref, 8 + rows, ring_below, 2 * rows + 1),
    ):
        ref[...] = jnp.zeros_like(ref)
        for i in range(2):
            at = slice(first - 6 + i, first - 5 + i)
            inner = (
                main[first + i : first + i + 1]
                + jnp.where(lane == 0, outer_left[2][:, at], 0.0)
                + jnp.where(lane == cols - 1, outer_right[0][:, at], 0.0)
            )
            pieces = [far_left[:, at], close_left[:, at], inner, close_right[:, at], far_right[:, at]]
            ref[i : i + 1, : cols + 4] = jnp.concatenate(pieces, axis=1)
        pieces = [ends_left[:, end : end + 1], line, ends_right[:, end : end + 1]]
        ref[2:3, : 2 * cols + 2] = jnp.concatenate(pieces, axis=1)


def corners_kernel(rows, cols, left, right, from_above, from_below, total, other, left_out, right_out, total_out):
    for ref, out, far, close, end in (
        (left, left_out, 0, 1, 0),
        (right, right_out, cols + 3, cols + 2, 2 * cols + 1),
    ):
        out[...] = ref[...]
        for rows_in, first, line in ((from_above, 2, 1), (from_below, rows, 2 * rows)):
            for i in range(2):
                at = slice(first + i, first + i + 1)
                out[0:1, at] += rows_in[i : i + 1, far : far + 1]
                out[1:2, at] += rows_in[i : i + 1, close : close + 1]
            out[2:3, line : line + 1] += rows_in[2:3, end : end + 1]
    total_out[...] = total[...] + other[...]


def shape(*dims):
    return jax.ShapeDtypeStruct(dims, f32)


def adjoint(edge, parts, sides, fields, arrived=(), cells=0):
    rows, cols = fields[1].shape[2:]
    xi_coarse, coef_middle, xi_middle, coef_fine, xi_fine = fields
    wide = 2 * rows + 128
    operands = (coef_fine, coef_middle, *sides)
    if edge:
        outs = [shape(8, wide)] * 2 + [shape(8, 2 * cols + 128)] * 2 + [shape(8, 128)]
    else:
        operands += (xi_fine, xi_middle, xi_coarse, *arrived)
        outs = [shape(4 * rows, 4 * cols), shape(2 * rows, 2 * cols), shape(rows, cols)]
        outs += [shape(1, 1)]
    return pl.pallas_call(
        functools.partial(adjoint_kernel, edge, len(parts), cells),
        in_specs=[anywhere] * (len(parts) + len(operands)),
        out_specs=[whole] * 5 if edge else [anywhere, whole, whole, whole],
        out_shape=outs,
        scratch_shapes=[pltpu.VMEM(x.shape, x.dtype) for x in (*parts, *operands)]
        + [
            pltpu.VMEM((4 * cols, 4 * cols), bf16),
            pltpu.VMEM((4 * cols // 128, 4 * rows + 8, 128), f32),
            pltpu.VMEM((9, 2 * rows + 32, 2 * cols), f32),
            pltpu.VMEM((3, 2 * rows + 128, 2 * cols), f32),
            pltpu.VMEM((2 * cols, 2 * cols), bf16),
            pltpu.VMEM((2 * cols // 128, 2 * rows + 8, 128), f32),
            pltpu.VMEM((9, rows + 32, cols), f32),
            pltpu.VMEM((3, rows + 128, cols), f32),
            pltpu.VMEM((4 * rows, 4 * cols), f32),
            pltpu.SemaphoreType.DMA((len(parts) + len(operands),)),
            pltpu.SemaphoreType.DMA((4,)),
            pltpu.SemaphoreType.DMA,
        ],
        compiler_params=pltpu.CompilerParams(vmem_limit_bytes=60 * 1024 * 1024),
        cost_estimate=long_work if edge else None,
        name="adjoint",
    )(*parts, *operands)


def in_three(x):
    high = x.astype(bf16).astype(f32)
    middle = (x - high).astype(bf16).astype(f32)
    return jnp.concatenate([high, middle, x - high - middle, jnp.zeros_like(x)]).astype(bf16)


def from_three(x):
    x = x.astype(f32)
    return x[:8] + x[8:16] + x[16:24]


def facets_kernel(blk, given, ints, weights, *refs):
    number, slots = weights.shape
    tiles, strips, rest = refs[:given], refs[given : given + 2], refs[given + 2 :]
    height = 4 * border
    kinds = strips[0].shape[0] // height
    ku_hbm, kv_hbm, data_hbm, squares, out_ref = rest[:5]
    held, held_strips, ku, kv, data, sums, dsum, total, sems, tile_sems, strip_sems = rest[5:]
    bins, side = ku.shape[1:]

    def inputs(f):
        for s in range(slots):
            for i, tile in enumerate(tiles):

                @pl.when(ints[f, s] == i)
                def _():
                    pltpu.make_async_copy(tile, held.at[f, s], tile_sems.at[f, s]).start()

            for i in range(2 * kinds):

                @pl.when(ints[f, slots + 1 + s] == i + 1)
                def _():
                    first = i % kinds * height
                    strip = strips[i // kinds].at[first : first + height]
                    pltpu.make_async_copy(strip, held_strips.at[f, s], strip_sems.at[f, s]).start()

        pairs = ((ku_hbm, ku), (kv_hbm, kv), (data_hbm, data))
        copies = [
            pltpu.make_async_copy(src.at[0, f], dst.at[f], sems.at[f, i])
            for i, (src, dst) in enumerate(pairs)
        ]
        for copy in copies:
            copy.start()
        return copies

    def patch(f, s):
        @pl.when(ints[f, slots + 1 + s] > 0)
        def _():
            strip = strips[0].at[:height]
            pltpu.make_async_copy(strip, held_strips.at[f, s], strip_sems.at[f, s]).wait()
            tile, strip = held.at[f, s], held_strips.at[f, s]
            lines = strip[: 2 * border].astype(f32)
            top, bottom = tile[: 2 * border].astype(f32), tile[side - 2 * border :].astype(f32)
            tile[: 2 * border] = jnp.concatenate([lines[:border], top[border:]]).astype(bf16)
            tile[side - 2 * border :] = jnp.concatenate([bottom[:border], lines[border:]]).astype(
                bf16
            )
            lane = lax.broadcasted_iota(jnp.int32, (side, 128), 1)
            left, right = columns_of(strip[2 * border :])
            for cells, inside, start in (
                (left, lane < border, 0),
                (right, lane >= 128 - border, side - 128),
            ):
                here = tile[:, start : start + 128].astype(f32)
                tile[:, start : start + 128] = jnp.where(inside, cells, here).astype(bf16)

    def work(f, step):
        rows = slice(step * blk, (step + 1) * blk)
        count = ints[f, slots] - step * blk

        @pl.when(count > 0)
        def _():
            amp = jnp.dot(ku[f, rows], sums[...], preferred_element_type=f32).astype(bf16)
            vis = dot_t(amp, kv[f], ((1,), (1,)))
            live = lax.broadcasted_iota(jnp.int32, vis.shape, 0) < count
            resid = jnp.where(live, vis - data[f, rows].astype(f32), 0.0)
            total[...] += 0.5 * inv_noise * folded(resid * resid)
            dvis = (inv_noise * resid).astype(bf16)
            damp = jnp.dot(dvis, kv[f], preferred_element_type=f32).astype(bf16)
            part = dot_t(ku[f, rows], damp, ((0,), (0,)))
            if step == 0:
                dsum[...] = part
            else:
                dsum[...] += part

    copies = [inputs(0)]
    total[...] = 0.5 * squares[...]
    for f in range(number):
        for s in range(slots):
            pltpu.make_async_copy(tiles[0], held.at[f, s], tile_sems.at[f, s]).wait()
            patch(f, s)
        copies[f][0].wait()
        if f + 1 < number:
            copies.append(inputs(f + 1))
        mixture = weights[f, 0] * held[f, 0].astype(f32)
        for s in range(1, slots):
            mixture += weights[f, s] * held[f, s].astype(f32)
        sums[...] = mixture.astype(bf16)
        copies[f][1].wait()
        copies[f][2].wait()
        for step in range(bins // blk):
            work(f, step)
        out_ref[f * side : (f + 1) * side] = dsum[...].astype(bf16)
    out_ref[number * side :] = jnp.zeros((32, side), bf16)
    out_ref[number * side :, :128] = in_three(total[...])


def facets(tiles, strips, ku, kv, data, ints, weights, squares):
    number, bins, side = ku.shape[1:]
    slots = weights.shape[1]
    return pl.pallas_call(
        functools.partial(facets_kernel, 512, len(tiles)),
        in_specs=[scalar] * 2 + [anywhere] * (len(tiles) + len(strips) + 3) + [whole],
        out_specs=whole,
        out_shape=jax.ShapeDtypeStruct((number * side + 32, side), bf16),
        scratch_shapes=[
            pltpu.VMEM((number, slots, side, side), bf16),
            pltpu.VMEM((number, slots, 4 * border, side), bf16),
            pltpu.VMEM((number, bins, side), bf16),
            pltpu.VMEM((number, bins, side), bf16),
            pltpu.VMEM((number, bins, bins), bf16),
            pltpu.VMEM((side, side), bf16),
            pltpu.VMEM((side, side), f32),
            pltpu.VMEM((8, 128), f32),
            pltpu.SemaphoreType.DMA((number, 3)),
            pltpu.SemaphoreType.DMA((number, slots)),
            pltpu.SemaphoreType.DMA((number, slots)),
        ],
        compiler_params=pltpu.CompilerParams(vmem_limit_bytes=47 * 1024 * 1024),
        name="facets",
    )(ints, weights, *tiles, *strips, ku, kv, data, squares)


def mix_kernel(scale, mine, theirs, *outs):
    side = outs[0].shape[1]
    number = mine.shape[0] // side
    for d, out in enumerate(outs):
        value = None
        for f in range(2 * number):
            ref, at = (mine, f) if f < number else (theirs, f - number)
            term = scale[d, f] * ref[at * side : (at + 1) * side].astype(f32)
            value = term if value is None else value + term
        out[...] = value.astype(bf16)


def mix_strips_kernel(scale, mine, theirs, *refs):
    outs, strips = refs[:-1], refs[-1]
    side = outs[0].shape[1]
    number = mine.shape[0] // side
    for f in range(2 * number):
        ref, at = (mine, f) if f < number else (theirs, f - number)
        strips_of(ref.at[at * side : (at + 1) * side], strips.at[f])
    total = from_three(mine[number * side :, :128]) + from_three(theirs[number * side :, :128])
    for d, out in enumerate(outs):
        value = None
        for f in range(2 * number):
            term = scale[d, f] * strips[f].astype(f32)
            value = term if value is None else value + term
        out[: 4 * border] = value.astype(bf16)
        out[4 * border :] = jnp.zeros((32, side), bf16)
        out[4 * border :, :128] = in_three(total)


def mixed(mine, theirs, scale, strips):
    side = mine.shape[1]
    rows = 4 * border + 32 if strips else side
    kept = [pltpu.VMEM((scale.shape[1], 4 * border, side), bf16)] if strips else []
    return pl.pallas_call(
        mix_strips_kernel if strips else mix_kernel,
        in_specs=[scalar, whole, whole],
        out_specs=[whole] * scale.shape[0],
        out_shape=[jax.ShapeDtypeStruct((rows, side), bf16)] * scale.shape[0],
        scratch_shapes=kept,
        compiler_params=pltpu.CompilerParams(vmem_limit_bytes=vmem),
        name="mixed",
    )(scale, mine, theirs)


def chip_shift(x, hop):
    size = lax.axis_size("gy")
    return lax.ppermute(x, "gy", [(i, (i + 2 * hop) % size) for i in range(size)])


def by_chips(x, pairs):
    return lax.ppermute(x, "gy", [(2 * a + c, 2 * b + c) for a, b in pairs for c in range(2)])


def paired(x, bits):
    return by_chips(x, [(i, i ^ bits) for i in range(lax.axis_size("gy") // 2)])


def swapped(x):
    return lax.ppermute(x, "gy", [(i, i ^ 1) for i in range(lax.axis_size("gy"))])


def body(
    xi_coarse,
    xi_middle,
    xi_fine,
    coef_middle,
    coef_fine,
    kern_u,
    kern_v,
    vis_data,
    facet_tiles,
    facet_weight,
    facet_count,
):
    fields = (xi_coarse, coef_middle, xi_middle, coef_fine, xi_fine)
    right, left = neighbours("gy")
    down, up = neighbours("gx")
    sides = halo_sides(xi_coarse, xi_middle, coef_middle)
    left_in = lax.ppermute(sides[1], "gy", right)
    right_in = lax.ppermute(sides[0], "gy", left)
    (first,) = sky_of(None, *fields)
    first, left_in, right_in, around, listed = lax.optimization_barrier(
        (
            first,
            left_in,
            right_in,
            (xi_coarse, xi_middle, coef_middle),
            (facet_tiles[0], facet_weight[0], facet_count[0]),
        )
    )
    lists, weights, counts = listed
    size = lax.axis_size("gy")
    chips = size // 2
    me = lax.axis_index("gy")
    ids = jnp.arange(size, dtype=jnp.int32)
    mixing = jnp.sum(
        weights[:, :, None] * (lists[:, :, None] == ids[None, None, :]).astype(f32), axis=1
    )
    steps = jnp.arange(chips, dtype=jnp.int32)
    order = (me // 2) ^ steps if chips == 4 else (me // 2 + steps) % chips
    order = 2 * order + me % 2
    scale = jnp.concatenate([mixing, swapped(mixing)])[:, order].T
    hops = range(1, chips)
    chip, other_core = me // 2, jnp.where(lists % 2 == me % 2, 0, 1)
    if chips == 4:
        mine = {1: paired(first, 1), 2: paired(first, 2)}
    else:
        mine = {hop: chip_shift(first, hop) for hop in range(1, min(3, chips))}
    above, below = halo_rows(*around, left_in, right_in)
    sky, strips, squares, lefts, rights = sky_of((above, below, left_in, right_in, *sides), *fields)
    if chips == 4:
        strips = [paired(strips, hop) for hop in hops]
        away = chip ^ (lists // 2)
        place = jnp.where((away == 3) & ((chip == 0) | (chip == 3)), 4, away)
        kind = away
    else:
        strips = [chip_shift(strips, hop) for hop in mine]
        place = away = (chip - lists // 2) % chips
        kind = jnp.where(away <= len(mine), away, 0)
    kinds = len(strips)
    strips = jnp.concatenate(strips)
    sky, strips, mine, scale, weights = lax.optimization_barrier(
        (sky, strips, mine, scale, weights)
    )
    if chips == 4:
        mine[3] = by_chips(sky, ((1, 2), (2, 1)))
        mine[4] = by_chips(mine[2], ((2, 3), (1, 0)))
    else:
        mine |= {hop: chip_shift(sky, hop) for hop in hops[len(mine) :]}
    mine = [sky] + [mine[hop] for hop in sorted(mine)]
    tiles = mine + [swapped(tile) for tile in mine]
    strips = [strips, swapped(strips)]
    place += len(mine) * other_core
    kind = jnp.where(kind > 0, kind + kinds * other_core, 0)
    ints = jnp.concatenate([place, counts[:, None], kind], axis=1)
    dsums = facets(tiles, strips, kern_u, kern_v, vis_data, ints, weights, squares)
    theirs = swapped(dsums)
    strips = mixed(dsums, theirs, scale, True)
    strips, dsums, theirs = lax.optimization_barrier((strips, dsums, theirs))
    send = paired if chips == 4 else chip_shift
    edges = [strips[0]] + [send(strips[hop], hop) for hop in hops]
    parts = mixed(dsums, theirs, scale, False)
    edges, _ = lax.optimization_barrier((edges, parts))
    around = (above, below, lefts, rights)
    if chips == 4:
        middle = by_chips(parts[3], ((1, 2), (2, 1)))
        onward = by_chips(parts[3], ((0, 1), (3, 2)))
    outgoing = adjoint(True, edges, around, fields)
    if chips == 4:
        onward, middle, parts, outgoing = lax.optimization_barrier(
            (onward, middle, parts, outgoing)
        )
        both = (parts[2].astype(f32) + onward.astype(f32)).astype(bf16)
        parts = [parts[0], paired(parts[1], 1), paired(both, 2), middle]
    else:
        parts = [parts[0]] + [chip_shift(parts[hop], hop) for hop in hops]
    to_left, to_right, upper, lower, total = outgoing
    size = lax.axis_size("gx")
    steps = [1 << i for i in range(size.bit_length()) if 1 << i < size]

    def across(x, hop):
        return lax.ppermute(x, "gx", [(i, i ^ hop) for i in range(size)])

    from_below = lax.ppermute(upper, "gx", up)
    from_above = lax.ppermute(lower, "gx", down)
    other = across(total, steps[0])
    rows, cols = xi_coarse.shape
    to_left, to_right, total = pl.pallas_call(
        functools.partial(corners_kernel, rows, cols),
        in_specs=[whole] * 6,
        out_specs=[whole] * 3,
        out_shape=[shape(*to_left.shape), shape(*to_right.shape), shape(8, 128)],
        name="corners",
    )(to_left, to_right, from_above, from_below, total, other)
    for hop in steps[1:-1]:
        total += across(total, hop)
    other = across(total, steps[-1])
    from_left = lax.ppermute(to_right, "gy", right)
    from_right = lax.ppermute(to_left, "gy", left)
    parts, from_left, from_right, other = lax.optimization_barrier(
        (parts, from_left, from_right, other)
    )
    cells = size * lax.axis_size("gy") * 16 * rows * cols
    arrived = (from_left, from_right, from_above, from_below, total, other)
    grad_fine, grad_middle, grad_coarse, total = adjoint(
        False, parts, around, fields, arrived, cells
    )
    return grad_coarse, grad_middle, grad_fine, total.reshape(())


def solution(mesh):
    placed = (
        P("gx", "gy"),
        P("gx", "gy"),
        P("gx", "gy"),
        P(None, None, "gx", "gy"),
        P(None, None, "gx", "gy"),
        P("gx", "gy", None, None),
        P("gx", "gy", None, None),
        P("gx", "gy", None, None),
        P("gx", "gy", None),
        P("gx", "gy", None),
        P("gx", "gy"),
    )
    return jax.shard_map(
        body,
        mesh=mesh,
        in_specs=placed,
        out_specs=(P("gx", "gy"), P("gx", "gy"), P("gx", "gy"), P()),
        check_vma=False,
    )
```
